256 devices in a mesh: iface: 64 (over y, z, core), dom: 4 (over x).
Axes of the slice: x: 4, y: 4, z: 8, core: 2. Of those that a mesh axis runs over, the one named last changes fastest.
Arguments:
- interface: float32 [1048576], P(('iface', 'dom')), may hold values from -6 to 6
- previous_residual: float32 [1048576], P(('iface', 'dom')), may hold values from -6 to 6
- previous_estimate: float32 [1048576], P(('iface', 'dom')), may hold values from -6 to 6
- forcing: float32 [1048576], P(('iface', 'dom')), may hold values from -60 to 60
- stiffness: float32 [1048576], P(('iface', 'dom')), may hold values from 0.2 to 0.6
- history_residual: float32 [100, 1048576], P(None, ('iface', 'dom')), may hold values from -40 to 40
- history_estimate: float32 [100, 1048576], P(None, ('iface', 'dom')), may hold values from -6 to 6
Outputs:
- interface_next: float32 [1048576], P(('iface', 'dom'))
- residual_last: float32 [1048576], P(('iface', 'dom'))
The draws below stay inside these ranges and needn't reach their ends.
All inputs are finite; a program needn't handle non-finite values.
Results may differ from the reference program's by a relative error of at most 0.0003.
Values sent between devices are 32-bit elements; how exact they have to be, the bound alone decides.
No kernel may reach another device: no remote copies, remote signals or barrier semaphores. Data moves between devices by JAX's collectives and lax.ppermute only.
A program may use at most 64 MiB of HBM per device.

```python
import math
import jax
import jax.numpy as jnp
from jax import lax

HIST = 100
ITERS = 3
NI = 1048576


def shared_history(key):
    high = lax.Precision.HIGHEST
    base = jax.random.normal(jax.random.fold_in(key, 7), (HIST + 1, NI), jnp.float32)
    factors = jax.random.uniform(jax.random.fold_in(key, 11), (HIST, 1), jnp.float32, 0.4, 0.8)
    banded = base[1:] + factors * base[:-1]
    mixing = jnp.eye(HIST, dtype=jnp.float32) + 0.2 * jax.random.normal(jax.random.fold_in(key, 12), (HIST, HIST), jnp.float32) / math.sqrt(HIST)
    mixed = jnp.dot(mixing, banded, precision=high)
    return jnp.clip(mixed, -40.0, 40.0)


def draw_history_residual(key, part):
    return shared_history(key)


def draw_forcing(key, part):
    mixed = shared_history(key)
    weights = jax.random.normal(jax.random.fold_in(key, 9), (HIST,), jnp.float32) / math.sqrt(HIST)
    noise = jax.random.normal(jax.random.fold_in(key, 10), (NI,), jnp.float32)
    total = 0.8 * jnp.dot(weights, mixed, precision=lax.Precision.HIGHEST) + 0.5 * noise
    return jnp.clip(total, -60.0, 60.0)


def shard_levels(key, shape, pieces, least, high):
    level = 1.0
    for axis_at, shards_of in pieces:
        steps = jax.random.uniform(jax.random.fold_in(jax.random.fold_in(key, 6), axis_at), (shards_of,), jnp.float32, least / len(pieces), high / len(pieces))
        level = level * jnp.repeat(jnp.exp(steps), shape[axis_at] // shards_of).reshape((-1,) + (1,) * (len(shape) - 1 - axis_at))
    return level


def normal_values(rng, shape, deviation, most, shards=(), kind=jnp.bfloat16):
    loudness = shard_levels(rng, shape, shards, -0.22, 0.18) if shards else 1.0
    drawn = jax.random.normal(rng, shape, jnp.float32) * deviation * loudness
    return jnp.minimum(jnp.maximum(drawn, -most), most).astype(kind)


def setup_inputs(seed: int = 0) -> dict:
    streams_of = jax.random.split(jax.random.key(seed), 8)
    interface = normal_values(streams_of[0], (NI,), 1.0, 6.0, ((0, 256),), jnp.float32)
    previous_residual = normal_values(streams_of[1], (NI,), 1.0, 6.0, ((0, 256),), jnp.float32)
    previous_estimate = normal_values(streams_of[2], (NI,), 1.0, 6.0, ((0, 256),), jnp.float32)
    forcing = draw_forcing(jax.random.fold_in(streams_of[7], 71), 0)
    stiffness = jnp.clip(0.2 + 0.400000021 * jax.random.uniform(streams_of[4], (NI,), jnp.float32) ** shard_levels(streams_of[4], (NI,), ((0, 256),), -0.2, 0.2), 0.2, 0.6)
    history_residual = draw_history_residual(jax.random.fold_in(streams_of[7], 71), 0)
    history_estimate = normal_values(streams_of[6], (HIST, NI), 1.0, 6.0, ((1, 256),), jnp.float32)
    return dict(interface=interface, previous_residual=previous_residual, previous_estimate=previous_estimate, forcing=forcing, stiffness=stiffness, history_residual=history_residual, history_estimate=history_estimate)


coupling = 0.25

def solver_map(current, forcing, stiffness):
    padded = jnp.pad(current, 1)
    return forcing + stiffness * jnp.tanh(current) + coupling * (padded[:-2] + padded[2:])

def reference(interface, previous_residual, previous_estimate, forcing, stiffness, history_residual, history_estimate):
    high = lax.Precision.HIGHEST
    current = interface
    hist_v = history_residual
    hist_w = history_estimate
    old_residual = previous_residual
    old_estimate = previous_estimate
    residual = previous_residual
    for iteration in range(ITERS):
        estimate = solver_map(current, forcing, stiffness)
        residual = estimate - current
        hist_v = jnp.concatenate([hist_v, (residual - old_residual)[None, :]], axis=0)
        hist_w = jnp.concatenate([hist_w, (estimate - old_estimate)[None, :]], axis=0)
        gram_matrix = jnp.dot(hist_v, hist_v.T, precision=high)
        projection = jnp.dot(hist_v, residual, precision=high)
        factor = jnp.linalg.cholesky(gram_matrix)
        coeffs = -jax.scipy.linalg.cho_solve((factor, True), projection)
        current = estimate + jnp.dot(coeffs, hist_w, precision=high)
        old_residual = residual
        old_estimate = estimate
    return (current, residual)
```

```python
import functools

import jax
import jax.numpy as jnp
from jax import lax
from jax.experimental import pallas as pl
from jax.experimental.pallas import tpu as pltpu
from jax.sharding import Mesh
from jax.sharding import PartitionSpec as P

ITERS = 3
AXES = ("y", "z", "core", "x")
COUPLING = 0.25
LANES = 128
HIST = 100
NEW = HIST
RES = HIST + 1
FOLD = 56
GROUPS = 13

F32 = jnp.float32
VMEM = pl.BlockSpec(memory_space=pltpu.VMEM)


def iota(shape, axis):
    return lax.broadcasted_iota(jnp.int32, shape, axis)


def rows_of(group):
    return slice(8 * group, min(8 * group + 8, HIST))


def row_to_columns(row):
    lane, sub = iota((8, LANES), 1), iota((8, LANES), 0)
    full = jnp.broadcast_to(row, (8, LANES))
    return [
        jnp.sum(jnp.where(lane == sub + 8 * g, full, 0.0), axis=1, keepdims=True)
        for g in range(GROUPS)
    ]


def columns_to_row(columns):
    lane, sub = iota((8, LANES), 1), iota((8, LANES), 0)
    total = jnp.zeros((8, LANES), F32)
    for g, column in enumerate(columns):
        total = total + jnp.where(lane == sub + 8 * g, jnp.broadcast_to(column, (8, LANES)), 0.0)
    return jnp.sum(total, axis=0, keepdims=True)


def solver_map(current, forcing, stiffness, inside):
    width = current.shape[1]
    neighbours = pltpu.roll(current, 1, 1) + pltpu.roll(current, width - 1, 1)
    estimate = forcing + stiffness * jnp.tanh(current) + COUPLING * neighbours
    return jnp.where(inside, estimate, 0.0)


def halo_of(right_ref, left_ref, rows):
    lane = iota((rows.stop - rows.start, LANES), 1)
    return jnp.where(lane < LANES // 2, right_ref[rows, :], left_ref[rows, :])


def extended(row, halo):
    return jnp.concatenate([row, halo], axis=1)


def inside_mask(width, stiffness_halo):
    ones = jnp.ones((1, width), F32)
    return extended(ones, jnp.where(stiffness_halo != 0.0, 1.0, 0.0)) > 0.5


def gram_kernel(
    hist_ref, current_ref, old_res_ref, forcing_ref, stiffness_ref, right_ref, left_ref,
    packed_ref, state_ref, parts_ref,
):
    width = hist_ref.shape[1]
    halo = halo_of(right_ref, left_ref, slice(96, 104))
    current = extended(current_ref[...], halo[4:5])
    stiffness_halo = halo[6:7]
    inside = inside_mask(width, stiffness_halo)
    estimate = solver_map(
        current,
        extended(forcing_ref[...], halo[5:6]),
        extended(stiffness_ref[...], stiffness_halo),
        inside,
    )
    residual = estimate - current
    column = residual[:, :width] - old_res_ref[...]
    state_ref[0:1, :] = estimate
    state_ref[1:2, :] = residual
    state_ref[2:3, :width] = column

    def put(row, values):
        high = values.astype(jnp.bfloat16)
        parts_ref[row : row + values.shape[0], :] = high
        parts_ref[LANES + row : LANES + row + values.shape[0], :] = (
            values - high.astype(F32)
        ).astype(jnp.bfloat16)

    for start in range(0, 96, 16):
        put(start, hist_ref[start : start + 16, :])
    put(
        96,
        jnp.concatenate(
            [hist_ref[96:100, :], column, residual[:, :width], jnp.zeros((10, width), F32)], axis=0
        ),
    )
    put(112, jnp.zeros((16, width), F32))
    products = lax.dot_general(
        parts_ref[:LANES, :],
        parts_ref[...],
        (((1,), (1,)), ((), ())),
        preferred_element_type=F32,
    )
    cross = products[:, LANES:]
    gram = products[:, :LANES] + cross + cross.T
    lane, sub = iota((FOLD, LANES), 1), iota((FOLD, LANES), 0)
    corner = pltpu.roll(gram[FOLD:104, :], LANES - FOLD, 1)
    corner = jnp.concatenate([jnp.zeros((8, LANES), F32), corner], axis=0)
    packed_ref[...] = jnp.where(lane <= sub - 8, corner, gram[:FOLD, :])


def unfold(packed):
    lane, sub = iota((FOLD, LANES), 1), iota((FOLD, LANES), 0)
    square = jnp.concatenate([packed, jnp.zeros((LANES - FOLD, LANES), F32)], axis=0)
    turned = square.T
    top = jnp.where(lane >= sub, packed, turned[:FOLD, :])
    lower = packed[8:FOLD, :]
    upper = pltpu.roll(turned[: FOLD - 8, :], LANES - 8, 1)
    lane2, sub2 = iota((FOLD - 8, LANES), 1), iota((FOLD - 8, LANES), 0)
    corner = pltpu.roll(jnp.where(lane2 <= sub2, lower, upper), FOLD, 1)
    bottom = jnp.where(lane2 < FOLD, turned[FOLD:104, :], corner)
    return [top[8 * g : 8 * g + 8] for g in range(FOLD // 8)] + [
        bottom[8 * g : 8 * g + 8] for g in range(GROUPS - FOLD // 8)
    ]


def eliminate(groups):
    lane, sub = iota((8, LANES), 1), iota((8, LANES), 0)
    groups = list(groups)
    for k in range(RES):
        g, t = divmod(k, 8)
        pivot_row = groups[g][t : t + 1, :]
        inverse = 1.0 / pivot_row[:, k : k + 1]
        pivot_row = jnp.where(lane[:1] == k, 1.0, pivot_row)
        scaled = jnp.broadcast_to(pivot_row * inverse, (8, LANES))
        for h in range(g, GROUPS):
            old = groups[h]
            factor = jnp.broadcast_to(old[:, k : k + 1], (8, LANES))
            new = jnp.where(lane == k, 0.0, old) - factor * scaled
            groups[h] = jnp.where(sub > t, new, old) if h == g else new
    return groups


def update(current, coefficients, hist_ref, halo, width):
    wide = [jnp.broadcast_to(c, (8, LANES)) for c in coefficients]
    pieces = []
    for start in range(0, width + LANES, LANES):
        total = jnp.zeros((8, LANES), F32)
        for g in range(GROUPS - 1):
            if start < width:
                part = hist_ref[8 * g : 8 * g + 8, start : start + LANES]
            else:
                part = halo[8 * g : 8 * g + 8, :]
            total = total + wide[g] * part
        if start < width:
            last = hist_ref[96:100, start : start + LANES]
        else:
            last = halo[96:100, :]
        pieces.append(
            jnp.sum(total, axis=0, keepdims=True)
            + jnp.sum(wide[GROUPS - 1][:4] * last, axis=0, keepdims=True)
        )
    return current + jnp.concatenate(pieces, axis=1)


def history_products(hist_ref, column, width):
    totals = [jnp.zeros((8, LANES), F32) for _ in range(GROUPS - 1)]
    last = jnp.zeros((4, LANES), F32)
    for start in range(0, width, LANES):
        part = column[:, start : start + LANES]
        wide = jnp.broadcast_to(part, (8, LANES))
        for g in range(GROUPS - 1):
            totals[g] = totals[g] + hist_ref[8 * g : 8 * g + 8, start : start + LANES] * wide
        last = last + hist_ref[96:100, start : start + LANES] * wide[:4]
    totals.append(jnp.concatenate([last, jnp.zeros((4, LANES), F32)], axis=0))
    return [jnp.sum(t, axis=1, keepdims=True) for t in totals]


def dot_rows(a, b):
    return jnp.sum(a * b, axis=1, keepdims=True)


def coefficient_of(row, at):
    return jnp.sum(jnp.where(iota((1, LANES), 1) == at, row, 0.0), axis=1, keepdims=True)


def send_row(out_ref, hist_ref, columns, column, residual, width):
    row = columns_to_row(history_products(hist_ref, column, width))
    lane = iota((1, LANES), 1)
    for at, other in enumerate((*columns, column, residual)):
        row = jnp.where(lane == HIST + at, dot_rows(other, column), row)
    out_ref[...] = jnp.broadcast_to(row.reshape(1, 1, LANES), out_ref.shape)


def first_kernel(
    packed_ref, hist_ref, hist_w_ref, state_ref, current_ref, old_est_ref, forcing_ref, stiffness_ref,
    right_ref, left_ref, row_ref, next_ref, factor_ref,
):
    width = hist_ref.shape[1]
    whole = unfold(packed_ref[...])
    products = whole[RES // 8][RES % 8 : RES % 8 + 1, :]
    groups = eliminate(whole)
    coeffs = groups[RES // 8][RES % 8 : RES % 8 + 1, :]
    lane1 = iota((1, LANES), 1)
    coeffs = jnp.where(lane1 < RES, coeffs, 0.0)
    lane, sub = iota((8, LANES), 1), iota((8, LANES), 0)
    for g, group in enumerate(groups):
        row = sub + 8 * g
        pivots = jnp.sum(jnp.where(lane == row, group, 0.0), axis=1, keepdims=True)
        scale = lax.rsqrt(jnp.where(row[:, :1] < RES, pivots, 1.0))
        unit = jnp.where(lane < row, group, jnp.where(lane == row, 1.0, 0.0))
        factor_ref[8 * g : 8 * g + 8, :] = jnp.where(row < RES, unit * scale, 0.0)
    factor_ref[104:112, :] = jnp.broadcast_to(jnp.where(lane1 < RES, products, 0.0), (8, LANES))

    halo = halo_of(right_ref, left_ref, slice(0, 104))
    forcing = extended(forcing_ref[...], halo[101:102])
    stiffness = extended(stiffness_ref[...], halo[102:103])
    inside = inside_mask(width, halo[102:103])
    estimate = state_ref[0:1, :]
    residual = state_ref[1:2, :]
    moved = estimate - extended(old_est_ref[...], halo[103:104])
    column = state_ref[2:3, :width]
    current = update(estimate, row_to_columns(coeffs), hist_w_ref, halo, width)
    current = current + coefficient_of(coeffs, NEW) * moved
    estimate2 = solver_map(current, forcing, stiffness, inside)
    residual2 = estimate2 - current
    column2 = residual2[:, :width] - residual[:, :width]
    next_ref[0:1, :] = estimate2
    next_ref[1:2, :] = residual2
    next_ref[2:3, :width] = column
    next_ref[3:4, :width] = column2
    next_ref[4:5, :] = moved
    next_ref[5:6, :] = estimate2 - estimate
    send_row(row_ref, hist_ref, (column,), column2, residual2[:, :width], width)


def bordered(factor_ref, products, sent, count, extra):
    lane = iota((1, LANES), 1)
    cross = jnp.where(lane < count, sent, 0.0)
    square = coefficient_of(sent, count)
    with_residual = coefficient_of(sent, count + 1)
    products = jnp.where(lane == count, with_residual, jnp.where(lane < count, products + cross, 0.0))

    def solve(row):
        total = jnp.zeros((8, LANES), F32)
        norm = jnp.zeros((8, 1), F32)
        for g in range(GROUPS):
            block = factor_ref[8 * g : 8 * g + 8, :]
            y = jnp.sum(block * row, axis=1, keepdims=True)
            total = total + y * block
            norm = norm + y * y
        out, length = jnp.sum(total, axis=0, keepdims=True), jnp.sum(norm, axis=0, keepdims=True)
        for line in extra:
            y = dot_rows(line, row)
            out, length = out + y * line, length + y * y
        return out, length

    applied, length = solve(cross)
    scale = lax.rsqrt(square - length)
    line = jnp.where(lane == count, 1.0, -applied) * scale
    coeffs, _ = solve(products)
    coeffs = -(coeffs + dot_rows(line, products) * line)
    return coeffs, line, products


def second_kernel(
    got_ref, hist_ref, hist_w_ref, factor_ref, state_ref, forcing_ref, stiffness_ref, right_ref, left_ref,
    row_ref, next_ref, lines_ref,
):
    width = hist_ref.shape[1]
    sent = jnp.sum(got_ref[...], axis=0)
    coeffs, line, products = bordered(factor_ref, factor_ref[104:105, :], sent, RES, ())
    lines_ref[0:1, :] = line
    lines_ref[1:2, :] = products
    halo = halo_of(right_ref, left_ref, slice(0, 104))
    forcing = extended(forcing_ref[...], halo[101:102])
    stiffness = extended(stiffness_ref[...], halo[102:103])
    inside = inside_mask(width, halo[102:103])
    estimate = state_ref[0:1, :]
    residual = state_ref[1:2, :]
    moved, moved2 = state_ref[4:5, :], state_ref[5:6, :]
    column, column2 = state_ref[2:3, :width], state_ref[3:4, :width]
    current = update(estimate, row_to_columns(coeffs), hist_w_ref, halo, width)
    current = current + coefficient_of(coeffs, NEW) * moved + coefficient_of(coeffs, NEW + 1) * moved2
    estimate3 = solver_map(current, forcing, stiffness, inside)
    residual3 = estimate3 - current
    column3 = residual3[:, :width] - residual[:, :width]
    next_ref[0:1, :] = estimate3
    next_ref[1:2, :] = residual3
    next_ref[4:5, :] = moved
    next_ref[5:6, :] = moved2
    next_ref[6:7, :] = estimate3 - estimate
    send_row(row_ref, hist_ref, (column, column2), column3, residual3[:, :width], width)


def third_kernel(
    got_ref, hist_w_ref, factor_ref, lines_ref, state_ref, current_ref, residual_ref,
):
    width = hist_w_ref.shape[1]
    sent = jnp.sum(got_ref[...], axis=0)
    coeffs, _, _ = bordered(factor_ref, lines_ref[1:2, :], sent, RES + 1, (lines_ref[0:1, :],))
    estimate = state_ref[0:1, :]
    halo = jnp.zeros((104, LANES), F32)
    current = update(estimate, row_to_columns(coeffs), hist_w_ref, halo, width)
    for at in range(ITERS):
        current = current + coefficient_of(coeffs, NEW + at) * state_ref[4 + at : 5 + at, :]
    current_ref[...] = current[:, :width]
    residual_ref[...] = state_ref[1:2, :width]


def call(kernel, outs, scratch=()):
    return pl.pallas_call(
        kernel,
        out_shape=[jax.ShapeDtypeStruct(s, F32) for s in outs],
        out_specs=[VMEM] * len(outs),
        scratch_shapes=list(scratch),
        compiler_params=pltpu.CompilerParams(vmem_limit_bytes=40 * 2**20),
    )


def everywhere(row):
    return lax.all_to_all(row, AXES, 0, 0)


def sum_over(value, axes):
    count = lax.axis_size(axes)
    copies = jnp.broadcast_to(value[None], (count, *value.shape))
    return jnp.sum(lax.all_to_all(copies, axes, 0, 0), axis=0)


def shards(interface, previous_residual, previous_estimate, forcing, stiffness, hist_v, hist_w):
    width = interface.shape[0]
    count = lax.axis_size(AXES)
    vectors = jnp.stack([interface, forcing, stiffness, previous_estimate])
    edge = lambda at: jnp.concatenate([hist_w[:, at], vectors[:, at]], axis=0)
    left = lax.ppermute(edge(slice(width - LANES, width)), AXES, [(i, i + 1) for i in range(count - 1)])
    right = lax.ppermute(edge(slice(0, LANES)), AXES, [(i + 1, i) for i in range(count - 1)])
    row = lambda v: v.reshape(1, width)
    state_shape = (8, width + LANES)
    packed, state = call(
        gram_kernel, [(FOLD, LANES), state_shape], [pltpu.VMEM((2 * LANES, width), jnp.bfloat16)]
    )(hist_v, row(interface), row(previous_residual), row(forcing), row(stiffness), right, left)
    packed = packed + lax.ppermute(packed, "core", [(i, i ^ 1) for i in range(lax.axis_size("core"))])
    packed = sum_over(packed, ("y", "x"))
    packed = sum_over(packed, ("z",))
    sent, state, factor = call(first_kernel, [(count, 1, LANES), state_shape, (112, LANES)])(
        packed, hist_v, hist_w, state, row(interface), row(previous_estimate), row(forcing), row(stiffness),
        right, left,
    )
    got = everywhere(sent)
    sent, state, lines = call(second_kernel, [(count, 1, LANES), state_shape, (8, LANES)])(
        got, hist_v, hist_w, factor, state, row(forcing), row(stiffness), right, left
    )
    got = everywhere(sent)
    current, residual = call(third_kernel, [(1, width), (1, width)])(got, hist_w, factor, lines, state)
    return current.reshape(width), residual.reshape(width)


def solution(mesh):
    devices = mesh.devices.reshape(4, 8, 2, 4) if mesh.devices.size == 256 else mesh.devices.reshape(2, 2, 2, -1)
    finer = Mesh(devices, AXES)
    whole, columns = P(AXES), P(None, AXES)
    return jax.shard_map(
        shards,
        mesh=finer,
        in_specs=(whole,) * 5 + (columns,) * 2,
        out_specs=(whole, whole),
        check_vma=False,
    )
```

```python
import functools

import jax
import jax.numpy as jnp
from jax import lax
from jax.experimental import pallas as pl
from jax.experimental.pallas import tpu as pltpu
from jax.sharding import Mesh
from jax.sharding import PartitionSpec as P

ITERS = 3
AXES = ("y", "z", "core", "x")
COUPLING = 0.25
LANES = 128
HIST = 100
NEW = HIST
RES = HIST + 1
FOLD = 56
GROUPS = 13

F32 = jnp.float32
VMEM = pl.BlockSpec(memory_space=pltpu.VMEM)


def iota(shape, axis):
    return lax.broadcasted_iota(jnp.int32, shape, axis)


def rows_of(group):
    return slice(8 * group, min(8 * group + 8, HIST))


def row_to_columns(row):
    lane, sub = iota((8, LANES), 1), iota((8, LANES), 0)
    full = jnp.broadcast_to(row, (8, LANES))
    return [
        jnp.sum(jnp.where(lane == sub + 8 * g, full, 0.0), axis=1, keepdims=True)
        for g in range(GROUPS)
    ]


def columns_to_row(columns):
    lane, sub = iota((8, LANES), 1), iota((8, LANES), 0)
    total = jnp.zeros((8, LANES), F32)
    for g, column in enumerate(columns):
        total = total + jnp.where(lane == sub + 8 * g, jnp.broadcast_to(column, (8, LANES)), 0.0)
    return jnp.sum(total, axis=0, keepdims=True)


def solver_map(current, forcing, stiffness, inside):
    width = current.shape[1]
    neighbours = pltpu.roll(current, 1, 1) + pltpu.roll(current, width - 1, 1)
    estimate = forcing + stiffness * jnp.tanh(current) + COUPLING * neighbours
    return jnp.where(inside, estimate, 0.0)


def halo_of(right_ref, left_ref, rows):
    lane = iota((rows.stop - rows.start, LANES), 1)
    return jnp.where(lane < LANES // 2, right_ref[rows, :], left_ref[rows, :])


def extended(row, halo):
    return jnp.concatenate([row, halo], axis=1)


def inside_mask(width, stiffness_halo):
    ones = jnp.ones((1, width), F32)
    return extended(ones, jnp.where(stiffness_halo != 0.0, 1.0, 0.0)) > 0.5


def copy_all(pairs, sems):
    copies = [pltpu.make_async_copy(src, dst, sems.at[i]) for i, (src, dst) in enumerate(pairs)]
    for copy in copies:
        copy.start()
    return copies


def edge_kernel(hist_ref, current_ref, forcing_ref, stiffness_ref, old_est_ref, left_ref, right_ref, sems):
    width = hist_ref.shape[1]
    pairs = []
    for out_ref, at in ((left_ref, width - LANES), (right_ref, 0)):
        columns = slice(at, at + LANES)
        pairs.append((hist_ref.at[:, columns], out_ref.at[:HIST, :]))
        for i, ref in enumerate((current_ref, forcing_ref, stiffness_ref, old_est_ref)):
            pairs.append((ref.at[:, columns], out_ref.at[HIST + i : HIST + i + 1, :]))
    for copy in copy_all(pairs, sems):
        copy.wait()


def gram_kernel(
    v_ref, w_ref, current_ref, old_res_ref, old_est_ref, forcing_ref, stiffness_ref,
    hist_ref, hist_w_ref, vectors_ref, gram_ref, parts_ref, sems,
):
    width = v_ref.shape[1]
    vectors = (current_ref, old_res_ref, old_est_ref, forcing_ref, stiffness_ref)
    first, *others = copy_all(
        [(v_ref, hist_ref), (w_ref, hist_w_ref)]
        + [(ref, vectors_ref.at[i : i + 1, :]) for i, ref in enumerate(vectors)],
        sems,
    )

    def put(row, values):
        high = values.astype(jnp.bfloat16)
        parts_ref[row : row + values.shape[0], :] = high
        parts_ref[LANES + row : LANES + row + values.shape[0], :] = (
            values - high.astype(F32)
        ).astype(jnp.bfloat16)

    put(112, jnp.zeros((16, width), F32))
    first.wait()
    for start in range(0, 96, 16):
        put(start, hist_ref[start : start + 16, :])
    put(96, jnp.concatenate([hist_ref[96:100, :], jnp.zeros((12, width), F32)], axis=0))
    products = lax.dot_general(
        parts_ref[:LANES, :],
        parts_ref[...],
        (((1,), (1,)), ((), ())),
        preferred_element_type=F32,
    )
    cross = products[:, LANES:]
    gram_ref[...] = (products[:, :LANES] + cross + cross.T)[:104]
    for copy in others:
        copy.wait()


def column_kernel(
    gram_ref, hist_ref, vectors_ref, right_ref, left_ref, packed_ref, state_ref
):
    width = hist_ref.shape[1]
    halo = halo_of(right_ref, left_ref, slice(96, 104))
    current = extended(vectors_ref[0:1, :], halo[4:5])
    inside = inside_mask(width, halo[6:7])
    estimate = solver_map(
        current,
        extended(vectors_ref[3:4, :], halo[5:6]),
        extended(vectors_ref[4:5, :], halo[6:7]),
        inside,
    )
    residual = estimate - current
    column = residual[:, :width] - vectors_ref[1:2, :]
    state_ref[0:1, :] = estimate
    state_ref[1:2, :] = residual
    state_ref[2:3, :width] = column
    residual = residual[:, :width]
    by_column = history_products(hist_ref, column, width)
    by_residual = history_products(hist_ref, residual, width)
    square, mixed = dot_rows(column, column), dot_rows(column, residual)
    lane1 = iota((1, LANES), 1)
    column_row = jnp.where(lane1 == NEW, square, columns_to_row(by_column))
    residual_row = jnp.where(lane1 == NEW, mixed, columns_to_row(by_residual))
    lane, sub = iota((8, LANES), 1), iota((8, LANES), 0)
    top = [
        jnp.where(lane == NEW, by_column[g], jnp.where(lane == RES, by_residual[g], gram_ref[8 * g : 8 * g + 8, :]))
        for g in range(FOLD // 8)
    ]
    bottom = [gram_ref[8 * g : 8 * g + 8, :] for g in range(FOLD // 8, GROUPS)]
    at = NEW - 8 * (GROUPS - 1)
    bottom[-1] = jnp.where(sub == at, column_row, jnp.where(sub == at + 1, residual_row, bottom[-1]))
    packed_ref[:8, :] = top[0]
    for g in range(1, FOLD // 8):
        corner = pltpu.roll(bottom[g - 1], LANES - FOLD, 1)
        packed_ref[8 * g : 8 * g + 8, :] = jnp.where(lane <= sub + 8 * (g - 1), corner, top[g])


def spread_kernel(got_ref, out_ref):
    total = jnp.sum(got_ref[...], axis=0)
    out_ref[...] = jnp.broadcast_to(total[None], out_ref.shape)


def pair_kernel(mine_ref, other_ref, out_ref):
    total = mine_ref[...] + other_ref[...]
    out_ref[...] = jnp.broadcast_to(total[None], out_ref.shape)


def unfold(packed):
    lane, sub = iota((FOLD, LANES), 1), iota((FOLD, LANES), 0)
    square = jnp.concatenate([packed, jnp.zeros((LANES - FOLD, LANES), F32)], axis=0)
    turned = square.T
    top = jnp.where(lane >= sub, packed, turned[:FOLD, :])
    lower = packed[8:FOLD, :]
    upper = pltpu.roll(turned[: FOLD - 8, :], LANES - 8, 1)
    lane2, sub2 = iota((FOLD - 8, LANES), 1), iota((FOLD - 8, LANES), 0)
    corner = pltpu.roll(jnp.where(lane2 <= sub2, lower, upper), FOLD, 1)
    bottom = jnp.where(lane2 < FOLD, turned[FOLD:104, :], corner)
    return [top[8 * g : 8 * g + 8] for g in range(FOLD // 8)] + [
        bottom[8 * g : 8 * g + 8] for g in range(GROUPS - FOLD // 8)
    ]


def eliminate(groups):
    lane, sub = iota((8, LANES), 1), iota((8, LANES), 0)
    groups = list(groups)
    for k in range(RES):
        g, t = divmod(k, 8)
        pivot_row = groups[g][t : t + 1, :]
        inverse = 1.0 / pivot_row[:, k : k + 1]
        pivot_row = jnp.where(lane[:1] == k, 1.0, pivot_row)
        scaled = jnp.broadcast_to(pivot_row * inverse, (8, LANES))
        for h in range(g, GROUPS):
            old = groups[h]
            factor = jnp.broadcast_to(old[:, k : k + 1], (8, LANES))
            new = jnp.where(lane == k, 0.0, old) - factor * scaled
            groups[h] = jnp.where(sub > t, new, old) if h == g else new
    return groups


def update(current, coefficients, hist_ref, halo, width):
    wide = [jnp.broadcast_to(c, (8, LANES)) for c in coefficients]
    pieces = []
    for start in range(0, width + LANES, LANES):
        total = jnp.zeros((8, LANES), F32)
        for g in range(GROUPS - 1):
            if start < width:
                part = hist_ref[8 * g : 8 * g + 8, start : start + LANES]
            else:
                part = halo[8 * g : 8 * g + 8, :]
            total = total + wide[g] * part
        if start < width:
            last = hist_ref[96:100, start : start + LANES]
        else:
            last = halo[96:100, :]
        pieces.append(
            jnp.sum(total, axis=0, keepdims=True)
            + jnp.sum(wide[GROUPS - 1][:4] * last, axis=0, keepdims=True)
        )
    return current + jnp.concatenate(pieces, axis=1)


def history_products(hist_ref, column, width):
    totals = [jnp.zeros((8, LANES), F32) for _ in range(GROUPS - 1)]
    last = jnp.zeros((4, LANES), F32)
    for start in range(0, width, LANES):
        part = column[:, start : start + LANES]
        wide = jnp.broadcast_to(part, (8, LANES))
        for g in range(GROUPS - 1):
            totals[g] = totals[g] + hist_ref[8 * g : 8 * g + 8, start : start + LANES] * wide
        last = last + hist_ref[96:100, start : start + LANES] * wide[:4]
    totals.append(jnp.concatenate([last, jnp.zeros((4, LANES), F32)], axis=0))
    return [jnp.sum(t, axis=1, keepdims=True) for t in totals]


def dot_rows(a, b):
    return jnp.sum(a * b, axis=1, keepdims=True)


def coefficient_of(row, at):
    return jnp.sum(jnp.where(iota((1, LANES), 1) == at, row, 0.0), axis=1, keepdims=True)


def send_row(out_ref, hist_ref, columns, column, residual, width):
    row = columns_to_row(history_products(hist_ref, column, width))
    lane = iota((1, LANES), 1)
    for at, other in enumerate((*columns, column, residual)):
        row = jnp.where(lane == HIST + at, dot_rows(other, column), row)
    out_ref[...] = jnp.broadcast_to(row.reshape(1, 1, LANES), out_ref.shape)


def first_kernel(
    packed_ref, hist_ref, hist_w_ref, state_ref, vectors_ref, right_ref, left_ref,
    row_ref, next_ref, factor_ref,
):
    width = hist_ref.shape[1]
    whole = unfold(jnp.sum(packed_ref[...], axis=0))
    products = whole[RES // 8][RES % 8 : RES % 8 + 1, :]
    groups = eliminate(whole)
    coeffs = groups[RES // 8][RES % 8 : RES % 8 + 1, :]
    lane1 = iota((1, LANES), 1)
    coeffs = jnp.where(lane1 < RES, coeffs, 0.0)
    lane, sub = iota((8, LANES), 1), iota((8, LANES), 0)
    for g, group in enumerate(groups):
        row = sub + 8 * g
        pivots = jnp.sum(jnp.where(lane == row, group, 0.0), axis=1, keepdims=True)
        scale = lax.rsqrt(jnp.where(row[:, :1] < RES, pivots, 1.0))
        unit = jnp.where(lane < row, group, jnp.where(lane == row, 1.0, 0.0))
        factor_ref[8 * g : 8 * g + 8, :] = jnp.where(row < RES, unit * scale, 0.0)
    factor_ref[104:112, :] = jnp.broadcast_to(jnp.where(lane1 < RES, products, 0.0), (8, LANES))

    halo = halo_of(right_ref, left_ref, slice(0, 104))
    forcing = extended(vectors_ref[3:4, :], halo[101:102])
    stiffness = extended(vectors_ref[4:5, :], halo[102:103])
    inside = inside_mask(width, halo[102:103])
    estimate = state_ref[0:1, :]
    residual = state_ref[1:2, :]
    moved = estimate - extended(vectors_ref[2:3, :], halo[103:104])
    column = state_ref[2:3, :width]
    current = update(estimate, row_to_columns(coeffs), hist_w_ref, halo, width)
    current = current + coefficient_of(coeffs, NEW) * moved
    estimate2 = solver_map(current, forcing, stiffness, inside)
    residual2 = estimate2 - current
    column2 = residual2[:, :width] - residual[:, :width]
    next_ref[0:1, :] = estimate2
    next_ref[1:2, :] = residual2
    next_ref[2:3, :width] = column
    next_ref[3:4, :width] = column2
    next_ref[4:5, :] = moved
    next_ref[5:6, :] = estimate2 - estimate
    send_row(row_ref, hist_ref, (column,), column2, residual2[:, :width], width)


def bordered(factor_ref, products, sent, count, extra):
    lane = iota((1, LANES), 1)
    cross = jnp.where(lane < count, sent, 0.0)
    square = coefficient_of(sent, count)
    with_residual = coefficient_of(sent, count + 1)
    products = jnp.where(lane == count, with_residual, jnp.where(lane < count, products + cross, 0.0))

    def solve(row):
        total = jnp.zeros((8, LANES), F32)
        norm = jnp.zeros((8, 1), F32)
        for g in range(GROUPS):
            block = factor_ref[8 * g : 8 * g + 8, :]
            y = jnp.sum(block * row, axis=1, keepdims=True)
            total = total + y * block
            norm = norm + y * y
        out, length = jnp.sum(total, axis=0, keepdims=True), jnp.sum(norm, axis=0, keepdims=True)
        for line in extra:
            y = dot_rows(line, row)
            out, length = out + y * line, length + y * y
        return out, length

    applied, length = solve(cross)
    scale = lax.rsqrt(square - length)
    line = jnp.where(lane == count, 1.0, -applied) * scale
    coeffs, _ = solve(products)
    coeffs = -(coeffs + dot_rows(line, products) * line)
    return coeffs, line, products


def second_kernel(
    got_ref, hist_ref, hist_w_ref, factor_ref, state_ref, vectors_ref, right_ref, left_ref,
    row_ref, next_ref, lines_ref,
):
    width = hist_ref.shape[1]
    sent = jnp.sum(got_ref[...], axis=0)
    coeffs, line, products = bordered(factor_ref, factor_ref[104:105, :], sent, RES, ())
    lines_ref[0:1, :] = line
    lines_ref[1:2, :] = products
    halo = halo_of(right_ref, left_ref, slice(0, 104))
    forcing = extended(vectors_ref[3:4, :], halo[101:102])
    stiffness = extended(vectors_ref[4:5, :], halo[102:103])
    inside = inside_mask(width, halo[102:103])
    estimate = state_ref[0:1, :]
    residual = state_ref[1:2, :]
    moved, moved2 = state_ref[4:5, :], state_ref[5:6, :]
    column, column2 = state_ref[2:3, :width], state_ref[3:4, :width]
    current = update(estimate, row_to_columns(coeffs), hist_w_ref, halo, width)
    current = current + coefficient_of(coeffs, NEW) * moved + coefficient_of(coeffs, NEW + 1) * moved2
    estimate3 = solver_map(current, forcing, stiffness, inside)
    residual3 = estimate3 - current
    column3 = residual3[:, :width] - residual[:, :width]
    next_ref[0:1, :] = estimate3
    next_ref[1:2, :] = residual3
    next_ref[4:5, :] = moved
    next_ref[5:6, :] = moved2
    next_ref[6:7, :] = estimate3 - estimate
    send_row(row_ref, hist_ref, (column, column2), column3, residual3[:, :width], width)


def third_kernel(
    got_ref, hist_w_ref, factor_ref, lines_ref, state_ref, current_ref, residual_ref,
):
    width = hist_w_ref.shape[1]
    sent = jnp.sum(got_ref[...], axis=0)
    coeffs, _, _ = bordered(factor_ref, lines_ref[1:2, :], sent, RES + 1, (lines_ref[0:1, :],))
    estimate = state_ref[0:1, :]
    halo = jnp.zeros((104, LANES), F32)
    current = update(estimate, row_to_columns(coeffs), hist_w_ref, halo, width)
    for at in range(ITERS):
        current = current + coefficient_of(coeffs, NEW + at) * state_ref[4 + at : 5 + at, :]
    current_ref[...] = current[:, :width]
    residual_ref[...] = state_ref[1:2, :width]


def call(kernel, outs, scratch=(), inputs=0, copies=0, flops=0):
    extra = {"in_specs": [pl.BlockSpec(memory_space=pltpu.HBM)] * inputs} if inputs else {}
    return pl.pallas_call(
        kernel,
        out_shape=[jax.ShapeDtypeStruct(s, F32) for s in outs],
        out_specs=[VMEM] * len(outs),
        scratch_shapes=[*scratch, *([pltpu.SemaphoreType.DMA((copies,))] if copies else [])],
        cost_estimate=pl.CostEstimate(flops=flops, bytes_accessed=2**22, transcendentals=0) if flops else None,
        compiler_params=pltpu.CompilerParams(vmem_limit_bytes=12 * 2**20),
        **extra,
    )


def in_hbm(value):
    return pltpu.with_memory_space_constraint(value, pltpu.HBM)


def everywhere(blocks, axes):
    return lax.all_to_all(blocks, axes, 0, 0)


def shards(interface, previous_residual, previous_estimate, forcing, stiffness, hist_v, hist_w):
    width = interface.shape[0]
    count = lax.axis_size(AXES)
    plane, depth = lax.axis_size(("y", "x")), lax.axis_size("z")
    row = lambda v: in_hbm(v.reshape(1, width))
    hist_v, hist_w = in_hbm(hist_v), in_hbm(hist_w)
    current, residual, estimate = row(interface), row(previous_residual), row(previous_estimate)
    forcing, stiffness = row(forcing), row(stiffness)
    edge, folded, state_shape = (104, LANES), (FOLD, LANES), (8, width + LANES)

    last, first = call(edge_kernel, [edge, edge], inputs=5, copies=10)(
        hist_w, current, forcing, stiffness, estimate
    )
    left = lax.ppermute(last, AXES, [(i, i + 1) for i in range(count - 1)])
    right = lax.ppermute(first, AXES, [(i + 1, i) for i in range(count - 1)])
    hist, hist_w, vectors, gram = call(
        gram_kernel,
        [hist_v.shape, hist_w.shape, (8, width), edge],
        [pltpu.VMEM((2 * LANES, width), jnp.bfloat16)],
        inputs=7,
        copies=7,
        flops=2**30,
    )(hist_v, hist_w, current, residual, estimate, forcing, stiffness)
    packed, state = call(column_kernel, [folded, state_shape])(gram, hist, vectors, right, left)
    other = lax.ppermute(packed, "core", [(i, i ^ 1) for i in range(lax.axis_size("core"))])
    (copies,) = call(pair_kernel, [(plane, *folded)])(packed, other)
    (copies,) = call(spread_kernel, [(depth, *folded)])(everywhere(copies, ("y", "x")))
    sent, state, factor = call(first_kernel, [(count, 1, LANES), state_shape, (112, LANES)])(
        everywhere(copies, "z"), hist, hist_w, state, vectors, right, left
    )
    sent, state, lines = call(second_kernel, [(count, 1, LANES), state_shape, (8, LANES)])(
        everywhere(sent, AXES), hist, hist_w, factor, state, vectors, right, left
    )
    current, residual = call(third_kernel, [(1, width), (1, width)])(
        everywhere(sent, AXES), hist_w, factor, lines, state
    )
    return current.reshape(width), residual.reshape(width)


def solution(mesh):
    devices = mesh.devices.reshape(4, 8, 2, 4) if mesh.devices.size == 256 else mesh.devices.reshape(2, 2, 2, -1)
    finer = Mesh(devices, AXES)
    whole, columns = P(AXES), P(None, AXES)
    return jax.shard_map(
        shards,
        mesh=finer,
        in_specs=(whole,) * 5 + (columns,) * 2,
        out_specs=(whole, whole),
        check_vma=False,
    )
```

```python
import functools

import jax
import jax.numpy as jnp
from jax import lax
from jax.experimental import pallas as pl
from jax.experimental.pallas import tpu as pltpu
from jax.sharding import Mesh
from jax.sharding import PartitionSpec as P

ITERS = 3
AXES = ("y", "z", "core", "x")
COUPLING = 0.25
LANES = 128
HIST = 100
NEW = HIST
RES = HIST + 1
FOLD = 56
GROUPS = 13

F32 = jnp.float32
VMEM = pl.BlockSpec(memory_space=pltpu.VMEM)


def iota(shape, axis):
    return lax.broadcasted_iota(jnp.int32, shape, axis)


def rows_of(group):
    return slice(8 * group, min(8 * group + 8, HIST))


def row_to_columns(row):
    lane, sub = iota((8, LANES), 1), iota((8, LANES), 0)
    full = jnp.broadcast_to(row, (8, LANES))
    return [
        jnp.sum(jnp.where(lane == sub + 8 * g, full, 0.0), axis=1, keepdims=True)
        for g in range(GROUPS)
    ]


def columns_to_row(columns):
    lane, sub = iota((8, LANES), 1), iota((8, LANES), 0)
    total = jnp.zeros((8, LANES), F32)
    for g, column in enumerate(columns):
        total = total + jnp.where(lane == sub + 8 * g, jnp.broadcast_to(column, (8, LANES)), 0.0)
    return jnp.sum(total, axis=0, keepdims=True)


def solver_map(current, forcing, stiffness, inside):
    width = current.shape[1]
    neighbours = pltpu.roll(current, 1, 1) + pltpu.roll(current, width - 1, 1)
    estimate = forcing + stiffness * jnp.tanh(current) + COUPLING * neighbours
    return jnp.where(inside, estimate, 0.0)


def halo_of(right_ref, left_ref, rows):
    lane = iota((rows.stop - rows.start, LANES), 1)
    return jnp.where(lane < LANES // 2, right_ref[rows, :], left_ref[rows, :])


def extended(row, halo):
    return jnp.concatenate([row, halo], axis=1)


def inside_mask(width, stiffness_halo):
    ones = jnp.ones((1, width), F32)
    return extended(ones, jnp.where(stiffness_halo != 0.0, 1.0, 0.0)) > 0.5


def copy_all(pairs, sems):
    copies = [pltpu.make_async_copy(src, dst, sems.at[i]) for i, (src, dst) in enumerate(pairs)]
    for copy in copies:
        copy.start()
    return copies


def edge_kernel(
    v_ref, hist_ref, current_ref, forcing_ref, stiffness_ref, old_est_ref,
    left_ref, right_ref, held_ref, sems,
):
    width = hist_ref.shape[1]
    pairs = []
    for out_ref, at in ((left_ref, width - LANES), (right_ref, 0)):
        columns = slice(at, at + LANES)
        pairs.append((hist_ref.at[:, columns], out_ref.at[:HIST, :]))
        for i, ref in enumerate((current_ref, forcing_ref, stiffness_ref, old_est_ref)):
            pairs.append((ref.at[:, columns], out_ref.at[HIST + i : HIST + i + 1, :]))
    pairs.append((v_ref, held_ref))
    for copy in copy_all(pairs, sems):
        copy.wait()


def gram_kernel(
    hist_ref, w_ref, current_ref, old_res_ref, old_est_ref, forcing_ref, stiffness_ref,
    hist_w_ref, vectors_ref, gram_ref, parts_ref, sems,
):
    width = hist_ref.shape[1]
    vectors = (current_ref, old_res_ref, old_est_ref, forcing_ref, stiffness_ref)
    copies = copy_all(
        [(w_ref, hist_w_ref)]
        + [(ref, vectors_ref.at[i : i + 1, :]) for i, ref in enumerate(vectors)],
        sems,
    )

    def put(row, values):
        high = values.astype(jnp.bfloat16)
        parts_ref[row : row + values.shape[0], :] = high
        parts_ref[LANES + row : LANES + row + values.shape[0], :] = (
            values - high.astype(F32)
        ).astype(jnp.bfloat16)

    put(112, jnp.zeros((16, width), F32))
    for start in range(0, 96, 16):
        put(start, hist_ref[start : start + 16, :])
    put(96, jnp.concatenate([hist_ref[96:100, :], jnp.zeros((12, width), F32)], axis=0))
    products = lax.dot_general(
        parts_ref[:LANES, :],
        parts_ref[...],
        (((1,), (1,)), ((), ())),
        preferred_element_type=F32,
    )
    cross = products[:, LANES:]
    gram_ref[...] = (products[:, :LANES] + cross + cross.T)[:104]
    for copy in copies:
        copy.wait()


def column_kernel(
    gram_ref, hist_ref, vectors_ref, right_ref, left_ref, packed_ref, state_ref
):
    width = hist_ref.shape[1]
    halo = halo_of(right_ref, left_ref, slice(96, 104))
    current = extended(vectors_ref[0:1, :], halo[4:5])
    inside = inside_mask(width, halo[6:7])
    estimate = solver_map(
        current,
        extended(vectors_ref[3:4, :], halo[5:6]),
        extended(vectors_ref[4:5, :], halo[6:7]),
        inside,
    )
    residual = estimate - current
    column = residual[:, :width] - vectors_ref[1:2, :]
    state_ref[0:1, :] = estimate
    state_ref[1:2, :] = residual
    state_ref[2:3, :width] = column
    residual = residual[:, :width]
    by_column = history_products(hist_ref, column, width)
    by_residual = history_products(hist_ref, residual, width)
    square, mixed = dot_rows(column, column), dot_rows(column, residual)
    lane1 = iota((1, LANES), 1)
    column_row = jnp.where(lane1 == NEW, square, columns_to_row(by_column))
    residual_row = jnp.where(lane1 == NEW, mixed, columns_to_row(by_residual))
    lane, sub = iota((8, LANES), 1), iota((8, LANES), 0)
    top = [
        jnp.where(lane == NEW, by_column[g], jnp.where(lane == RES, by_residual[g], gram_ref[8 * g : 8 * g + 8, :]))
        for g in range(FOLD // 8)
    ]
    bottom = [gram_ref[8 * g : 8 * g + 8, :] for g in range(FOLD // 8, GROUPS)]
    at = NEW - 8 * (GROUPS - 1)
    bottom[-1] = jnp.where(sub == at, column_row, jnp.where(sub == at + 1, residual_row, bottom[-1]))
    packed_ref[:8, :] = top[0]
    for g in range(1, FOLD // 8):
        corner = pltpu.roll(bottom[g - 1], LANES - FOLD, 1)
        packed_ref[8 * g : 8 * g + 8, :] = jnp.where(lane <= sub + 8 * (g - 1), corner, top[g])


def spread_kernel(got_ref, out_ref):
    total = jnp.sum(got_ref[...], axis=0)
    out_ref[...] = jnp.broadcast_to(total[None], out_ref.shape)


def pair_kernel(mine_ref, other_ref, out_ref):
    total = mine_ref[...] + other_ref[...]
    out_ref[...] = jnp.broadcast_to(total[None], out_ref.shape)


def unfold(packed):
    lane, sub = iota((FOLD, LANES), 1), iota((FOLD, LANES), 0)
    square = jnp.concatenate([packed, jnp.zeros((LANES - FOLD, LANES), F32)], axis=0)
    turned = square.T
    top = jnp.where(lane >= sub, packed, turned[:FOLD, :])
    lower = packed[8:FOLD, :]
    upper = pltpu.roll(turned[: FOLD - 8, :], LANES - 8, 1)
    lane2, sub2 = iota((FOLD - 8, LANES), 1), iota((FOLD - 8, LANES), 0)
    corner = pltpu.roll(jnp.where(lane2 <= sub2, lower, upper), FOLD, 1)
    bottom = jnp.where(lane2 < FOLD, turned[FOLD:104, :], corner)
    return [top[8 * g : 8 * g + 8] for g in range(FOLD // 8)] + [
        bottom[8 * g : 8 * g + 8] for g in range(GROUPS - FOLD // 8)
    ]


def eliminate(groups):
    lane, sub = iota((8, LANES), 1), iota((8, LANES), 0)
    whole = lambda v: jnp.broadcast_to(v, (8, LANES))
    groups = list(groups)
    pivots = [jnp.ones((8, LANES), F32) for _ in range(GROUPS)]
    for g in range(GROUPS):
        first, count = 8 * g, min(8, RES - 8 * g)
        inside = (lane >= first) & (lane < first + count)
        columns = [[whole(group[:, first + j : first + j + 1]) for j in range(count)] for group in groups[g:]]
        left = [[whole(columns[0][j][i : i + 1, :]) for j in range(i + 1)] for i in range(count)]
        low = [[None] * count for _ in range(count)]
        inverse, rows = [], []
        for j in range(count):
            for i in range(j, count):
                for m in range(j):
                    left[i][j] = left[i][j] - low[i][m] * left[j][m]
            inverse.append(1.0 / left[j][j])
            for i in range(j + 1, count):
                low[i][j] = left[i][j] * inverse[j]
        for j in range(count):
            row = jnp.where(inside, jnp.where(lane == first + j, 1.0, 0.0), whole(groups[g][j : j + 1, :]))
            for m in range(j):
                row = row - low[j][m] * rows[m]
            rows.append(row)
            pivots[g] = jnp.where(sub == j, left[j][j], pivots[g])
        for h in range(g, GROUPS):
            if h == g and count == 8:
                continue
            new = jnp.where(inside, 0.0, groups[h])
            factors = []
            for j in range(count):
                factor = columns[h - g][j]
                for m in range(j):
                    factor = factor - factors[m] * left[j][m]
                factors.append(factor * inverse[j])
                new = new - factors[j] * rows[j]
            groups[h] = new
        for j in range(count):
            groups[g] = jnp.where(sub == j, rows[j], groups[g])
    return groups, pivots


def update(current, coefficients, hist_ref, halo, width):
    wide = [jnp.broadcast_to(c, (8, LANES)) for c in coefficients]
    pieces = []
    for start in range(0, width + LANES, LANES):
        total = jnp.zeros((8, LANES), F32)
        for g in range(GROUPS - 1):
            if start < width:
                part = hist_ref[8 * g : 8 * g + 8, start : start + LANES]
            else:
                part = halo[8 * g : 8 * g + 8, :]
            total = total + wide[g] * part
        if start < width:
            last = hist_ref[96:100, start : start + LANES]
        else:
            last = halo[96:100, :]
        pieces.append(
            jnp.sum(total, axis=0, keepdims=True)
            + jnp.sum(wide[GROUPS - 1][:4] * last, axis=0, keepdims=True)
        )
    return current + jnp.concatenate(pieces, axis=1)


def history_products(hist_ref, column, width):
    totals = [jnp.zeros((8, LANES), F32) for _ in range(GROUPS - 1)]
    last = jnp.zeros((4, LANES), F32)
    for start in range(0, width, LANES):
        part = column[:, start : start + LANES]
        wide = jnp.broadcast_to(part, (8, LANES))
        for g in range(GROUPS - 1):
            totals[g] = totals[g] + hist_ref[8 * g : 8 * g + 8, start : start + LANES] * wide
        last = last + hist_ref[96:100, start : start + LANES] * wide[:4]
    totals.append(jnp.concatenate([last, jnp.zeros((4, LANES), F32)], axis=0))
    return [jnp.sum(t, axis=1, keepdims=True) for t in totals]


def dot_rows(a, b):
    return jnp.sum(a * b, axis=1, keepdims=True)


def coefficient_of(row, at):
    return jnp.sum(jnp.where(iota((1, LANES), 1) == at, row, 0.0), axis=1, keepdims=True)


def send_row(out_ref, hist_ref, columns, column, residual, width):
    row = columns_to_row(history_products(hist_ref, column, width))
    lane = iota((1, LANES), 1)
    for at, other in enumerate((*columns, column, residual)):
        row = jnp.where(lane == HIST + at, dot_rows(other, column), row)
    out_ref[...] = jnp.broadcast_to(row.reshape(1, 1, LANES), out_ref.shape)


def first_kernel(
    packed_ref, hist_ref, hist_w_ref, state_ref, vectors_ref, right_ref, left_ref,
    row_ref, next_ref, factor_ref,
):
    width = hist_ref.shape[1]
    whole = unfold(jnp.sum(packed_ref[...], axis=0))
    products = whole[RES // 8][RES % 8 : RES % 8 + 1, :]
    groups, pivots = eliminate(whole)
    coeffs = groups[RES // 8][RES % 8 : RES % 8 + 1, :]
    lane1 = iota((1, LANES), 1)
    coeffs = jnp.where(lane1 < RES, coeffs, 0.0)
    lane, sub = iota((8, LANES), 1), iota((8, LANES), 0)
    for g, group in enumerate(groups):
        row = sub + 8 * g
        scale = lax.rsqrt(pivots[g])
        unit = jnp.where(lane < row, group, jnp.where(lane == row, 1.0, 0.0))
        factor_ref[8 * g : 8 * g + 8, :] = jnp.where(row < RES, unit * scale, 0.0)
    factor_ref[104:112, :] = jnp.broadcast_to(jnp.where(lane1 < RES, products, 0.0), (8, LANES))

    halo = halo_of(right_ref, left_ref, slice(0, 104))
    forcing = extended(vectors_ref[3:4, :], halo[101:102])
    stiffness = extended(vectors_ref[4:5, :], halo[102:103])
    inside = inside_mask(width, halo[102:103])
    estimate = state_ref[0:1, :]
    residual = state_ref[1:2, :]
    moved = estimate - extended(vectors_ref[2:3, :], halo[103:104])
    column = state_ref[2:3, :width]
    current = update(estimate, row_to_columns(coeffs), hist_w_ref, halo, width)
    current = current + coefficient_of(coeffs, NEW) * moved
    estimate2 = solver_map(current, forcing, stiffness, inside)
    residual2 = estimate2 - current
    column2 = residual2[:, :width] - residual[:, :width]
    next_ref[0:1, :] = estimate2
    next_ref[1:2, :] = residual2
    next_ref[2:3, :width] = column
    next_ref[3:4, :width] = column2
    next_ref[4:5, :] = moved
    next_ref[5:6, :] = estimate2 - estimate
    send_row(row_ref, hist_ref, (column,), column2, residual2[:, :width], width)


def bordered(factor_ref, products, sent, count, extra):
    lane = iota((1, LANES), 1)
    cross = jnp.where(lane < count, sent, 0.0)
    square = coefficient_of(sent, count)
    with_residual = coefficient_of(sent, count + 1)
    products = jnp.where(lane == count, with_residual, jnp.where(lane < count, products + cross, 0.0))

    def solve(row):
        total = jnp.zeros((8, LANES), F32)
        norm = jnp.zeros((8, 1), F32)
        for g in range(GROUPS):
            block = factor_ref[8 * g : 8 * g + 8, :]
            y = jnp.sum(block * row, axis=1, keepdims=True)
            total = total + y * block
            norm = norm + y * y
        out, length = jnp.sum(total, axis=0, keepdims=True), jnp.sum(norm, axis=0, keepdims=True)
        for line in extra:
            y = dot_rows(line, row)
            out, length = out + y * line, length + y * y
        return out, length

    applied, length = solve(cross)
    scale = lax.rsqrt(square - length)
    line = jnp.where(lane == count, 1.0, -applied) * scale
    coeffs, _ = solve(products)
    coeffs = -(coeffs + dot_rows(line, products) * line)
    return coeffs, line, products


def second_kernel(
    got_ref, hist_ref, hist_w_ref, factor_ref, state_ref, vectors_ref, right_ref, left_ref,
    row_ref, next_ref, lines_ref,
):
    width = hist_ref.shape[1]
    sent = jnp.sum(got_ref[...], axis=0)
    coeffs, line, products = bordered(factor_ref, factor_ref[104:105, :], sent, RES, ())
    lines_ref[0:1, :] = line
    lines_ref[1:2, :] = products
    halo = halo_of(right_ref, left_ref, slice(0, 104))
    forcing = extended(vectors_ref[3:4, :], halo[101:102])
    stiffness = extended(vectors_ref[4:5, :], halo[102:103])
    inside = inside_mask(width, halo[102:103])
    estimate = state_ref[0:1, :]
    residual = state_ref[1:2, :]
    moved, moved2 = state_ref[4:5, :], state_ref[5:6, :]
    column, column2 = state_ref[2:3, :width], state_ref[3:4, :width]
    current = update(estimate, row_to_columns(coeffs), hist_w_ref, halo, width)
    current = current + coefficient_of(coeffs, NEW) * moved + coefficient_of(coeffs, NEW + 1) * moved2
    estimate3 = solver_map(current, forcing, stiffness, inside)
    residual3 = estimate3 - current
    column3 = residual3[:, :width] - residual[:, :width]
    next_ref[0:1, :] = estimate3
    next_ref[1:2, :] = residual3
    next_ref[4:5, :] = moved
    next_ref[5:6, :] = moved2
    next_ref[6:7, :] = estimate3 - estimate
    send_row(row_ref, hist_ref, (column, column2), column3, residual3[:, :width], width)


def third_kernel(
    got_ref, hist_w_ref, factor_ref, lines_ref, state_ref, current_ref, residual_ref,
):
    width = hist_w_ref.shape[1]
    sent = jnp.sum(got_ref[...], axis=0)
    coeffs, _, _ = bordered(factor_ref, lines_ref[1:2, :], sent, RES + 1, (lines_ref[0:1, :],))
    estimate = state_ref[0:1, :]
    halo = jnp.zeros((104, LANES), F32)
    current = update(estimate, row_to_columns(coeffs), hist_w_ref, halo, width)
    for at in range(ITERS):
        current = current + coefficient_of(coeffs, NEW + at) * state_ref[4 + at : 5 + at, :]
    current_ref[...] = current[:, :width]
    residual_ref[...] = state_ref[1:2, :width]


def call(kernel, outs, scratch=(), held=0, inputs=0, copies=0, flops=0):
    extra = {}
    if inputs:
        extra["in_specs"] = [VMEM] * held + [pl.BlockSpec(memory_space=pltpu.HBM)] * inputs
    return pl.pallas_call(
        kernel,
        out_shape=[jax.ShapeDtypeStruct(s, F32) for s in outs],
        out_specs=[VMEM] * len(outs),
        scratch_shapes=[*scratch, *([pltpu.SemaphoreType.DMA((copies,))] if copies else [])],
        cost_estimate=pl.CostEstimate(flops=flops, bytes_accessed=2**22, transcendentals=0) if flops else None,
        compiler_params=pltpu.CompilerParams(vmem_limit_bytes=12 * 2**20),
        **extra,
    )


def in_hbm(value):
    return pltpu.with_memory_space_constraint(value, pltpu.HBM)


def everywhere(blocks, axes):
    return lax.all_to_all(blocks, axes, 0, 0)


def shards(interface, previous_residual, previous_estimate, forcing, stiffness, hist_v, hist_w):
    width = interface.shape[0]
    count = lax.axis_size(AXES)
    plane, depth = lax.axis_size(("y", "x")), lax.axis_size("z")
    row = lambda v: in_hbm(v.reshape(1, width))
    hist_v, hist_w = in_hbm(hist_v), in_hbm(hist_w)
    current, residual, estimate = row(interface), row(previous_residual), row(previous_estimate)
    forcing, stiffness = row(forcing), row(stiffness)
    edge, folded, state_shape = (104, LANES), (FOLD, LANES), (8, width + LANES)

    last, first, hist = call(edge_kernel, [edge, edge, hist_v.shape], inputs=6, copies=11)(
        hist_v, hist_w, current, forcing, stiffness, estimate
    )
    left = lax.ppermute(last, AXES, [(i, i + 1) for i in range(count - 1)])
    right = lax.ppermute(first, AXES, [(i + 1, i) for i in range(count - 1)])
    hist_w, vectors, gram = call(
        gram_kernel,
        [hist_w.shape, (8, width), edge],
        [pltpu.VMEM((2 * LANES, width), jnp.bfloat16)],
        held=1,
        inputs=6,
        copies=6,
        flops=2**30,
    )(hist, hist_w, current, residual, estimate, forcing, stiffness)
    packed, state = call(column_kernel, [folded, state_shape])(gram, hist, vectors, right, left)
    other = lax.ppermute(packed, "core", [(i, i ^ 1) for i in range(lax.axis_size("core"))])
    (copies,) = call(pair_kernel, [(plane, *folded)])(packed, other)
    (copies,) = call(spread_kernel, [(depth, *folded)])(everywhere(copies, ("y", "x")))
    sent, state, factor = call(first_kernel, [(count, 1, LANES), state_shape, (112, LANES)])(
        everywhere(copies, "z"), hist, hist_w, state, vectors, right, left
    )
    sent, state, lines = call(second_kernel, [(count, 1, LANES), state_shape, (8, LANES)])(
        everywhere(sent, AXES), hist, hist_w, factor, state, vectors, right, left
    )
    current, residual = call(third_kernel, [(1, width), (1, width)])(
        everywhere(sent, AXES), hist_w, factor, lines, state
    )
    return current.reshape(width), residual.reshape(width)


def solution(mesh):
    devices = mesh.devices.reshape(4, 8, 2, 4) if mesh.devices.size == 256 else mesh.devices.reshape(2, 2, 2, -1)
    finer = Mesh(devices, AXES)
    whole, columns = P(AXES), P(None, AXES)
    return jax.shard_map(
        shards,
        mesh=finer,
        in_specs=(whole,) * 5 + (columns,) * 2,
        out_specs=(whole, whole),
        check_vma=False,
    )
```

```python
import functools

import jax
import jax.numpy as jnp
from jax import lax
from jax.experimental import pallas as pl
from jax.experimental.pallas import tpu as pltpu
from jax.sharding import Mesh
from jax.sharding import PartitionSpec as P

ITERS = 3
AXES = ("y", "z", "core", "x")
COUPLING = 0.25
LANES = 128
HIST = 100
NEW = HIST
RES = HIST + 1
FOLD = 56
HALF = 32
GROUPS = 13

F32 = jnp.float32
VMEM = pl.BlockSpec(memory_space=pltpu.VMEM)


def iota(shape, axis):
    return lax.broadcasted_iota(jnp.int32, shape, axis)


def rows_of(group):
    return slice(8 * group, min(8 * group + 8, HIST))


def row_to_columns(row):
    lane, sub = iota((8, LANES), 1), iota((8, LANES), 0)
    full = jnp.broadcast_to(row, (8, LANES))
    return [
        jnp.sum(jnp.where(lane == sub + 8 * g, full, 0.0), axis=1, keepdims=True)
        for g in range(GROUPS)
    ]


def columns_to_row(columns):
    lane, sub = iota((8, LANES), 1), iota((8, LANES), 0)
    total = jnp.zeros((8, LANES), F32)
    for g, column in enumerate(columns):
        total = total + jnp.where(lane == sub + 8 * g, jnp.broadcast_to(column, (8, LANES)), 0.0)
    return jnp.sum(total, axis=0, keepdims=True)


def solver_map(current, forcing, stiffness, inside):
    width = current.shape[1]
    neighbours = pltpu.roll(current, 1, 1) + pltpu.roll(current, width - 1, 1)
    estimate = forcing + stiffness * jnp.tanh(current) + COUPLING * neighbours
    return jnp.where(inside, estimate, 0.0)


def halo_of(right_ref, left_ref, rows):
    lane = iota((rows.stop - rows.start, LANES), 1)
    return jnp.where(lane < LANES // 2, right_ref[rows, :], left_ref[rows, :])


def extended(row, halo):
    return jnp.concatenate([row, halo], axis=1)


def inside_mask(width, stiffness_halo):
    ones = jnp.ones((1, width), F32)
    return extended(ones, jnp.where(stiffness_halo != 0.0, 1.0, 0.0)) > 0.5


def copy_all(pairs, sems):
    copies = [pltpu.make_async_copy(src, dst, sems.at[i]) for i, (src, dst) in enumerate(pairs)]
    for copy in copies:
        copy.start()
    return copies


def edge_kernel(
    hist_ref, current_ref, forcing_ref, stiffness_ref, old_est_ref, left_ref, right_ref, sems
):
    width = hist_ref.shape[1]
    pairs = []
    for out_ref, at in ((left_ref, width - LANES), (right_ref, 0)):
        columns = slice(at, at + LANES)
        pairs.append((hist_ref.at[:, columns], out_ref.at[:HIST, :]))
        for i, ref in enumerate((current_ref, forcing_ref, stiffness_ref, old_est_ref)):
            pairs.append((ref.at[:, columns], out_ref.at[HIST + i : HIST + i + 1, :]))
    for copy in copy_all(pairs, sems):
        copy.wait()


def gram_kernel(
    hist_ref, current_ref, old_res_ref, old_est_ref, forcing_ref, stiffness_ref,
    vectors_ref, gram_ref, parts_ref, sems,
):
    width = hist_ref.shape[1]
    vectors = (current_ref, old_res_ref, old_est_ref, forcing_ref, stiffness_ref)
    copies = copy_all([(ref, vectors_ref.at[i : i + 1, :]) for i, ref in enumerate(vectors)], sems)

    def put(row, values):
        high = values.astype(jnp.bfloat16)
        parts_ref[row : row + values.shape[0], :] = high
        parts_ref[LANES + row : LANES + row + values.shape[0], :] = (
            values - high.astype(F32)
        ).astype(jnp.bfloat16)

    put(112, jnp.zeros((16, width), F32))
    for start in range(0, 96, 16):
        put(start, hist_ref[start : start + 16, :])
    put(96, jnp.concatenate([hist_ref[96:100, :], jnp.zeros((12, width), F32)], axis=0))
    products = lax.dot_general(
        parts_ref[:LANES, :],
        parts_ref[...],
        (((1,), (1,)), ((), ())),
        preferred_element_type=F32,
    )
    cross = products[:, LANES:]
    gram_ref[...] = (products[:, :LANES] + cross + cross.T)[:104]
    for copy in copies:
        copy.wait()


def column_kernel(
    gram_ref, hist_ref, vectors_ref, right_ref, left_ref, mine_ref, other_ref, state_ref, packed_ref
):
    width = hist_ref.shape[1]
    halo = halo_of(right_ref, left_ref, slice(96, 104))
    current = extended(vectors_ref[0:1, :], halo[4:5])
    inside = inside_mask(width, halo[6:7])
    estimate = solver_map(
        current,
        extended(vectors_ref[3:4, :], halo[5:6]),
        extended(vectors_ref[4:5, :], halo[6:7]),
        inside,
    )
    residual = estimate - current
    column = residual[:, :width] - vectors_ref[1:2, :]
    state_ref[0:1, :] = estimate
    state_ref[1:2, :] = residual
    state_ref[2:3, :width] = column
    residual = residual[:, :width]
    by_column = history_products(hist_ref, column, width)
    by_residual = history_products(hist_ref, residual, width)
    square, mixed = dot_rows(column, column), dot_rows(column, residual)
    lane1 = iota((1, LANES), 1)
    column_row = jnp.where(lane1 == NEW, square, columns_to_row(by_column))
    residual_row = jnp.where(lane1 == NEW, mixed, columns_to_row(by_residual))
    lane, sub = iota((8, LANES), 1), iota((8, LANES), 0)
    top = [
        jnp.where(lane == NEW, by_column[g], jnp.where(lane == RES, by_residual[g], gram_ref[8 * g : 8 * g + 8, :]))
        for g in range(FOLD // 8)
    ]
    bottom = [gram_ref[8 * g : 8 * g + 8, :] for g in range(FOLD // 8, GROUPS)]
    at = NEW - 8 * (GROUPS - 1)
    bottom[-1] = jnp.where(sub == at, column_row, jnp.where(sub == at + 1, residual_row, bottom[-1]))
    packed_ref[:8, :] = top[0]
    for g in range(1, FOLD // 8):
        corner = pltpu.roll(bottom[g - 1], LANES - FOLD, 1)
        packed_ref[8 * g : 8 * g + 8, :] = jnp.where(lane <= sub + 8 * (g - 1), corner, top[g])
    packed_ref[FOLD:, :] = jnp.zeros((2 * HALF - FOLD, LANES), F32)
    low, high = packed_ref[:HALF, :], packed_ref[HALF:, :]
    is_low = first_core()
    mine_ref[...] = jnp.where(is_low, low, high)
    other_ref[...] = jnp.where(is_low, high, low)


def first_core():
    return jnp.full((HALF, LANES), lax.axis_index("core"), jnp.int32) == 0


def total_kernel(got_ref, out_ref):
    out_ref[...] = jnp.sum(got_ref[...], axis=0)


def spread_kernel(got_ref, out_ref):
    total = jnp.sum(got_ref[...], axis=0)
    out_ref[...] = jnp.broadcast_to(total[None], out_ref.shape)


def pair_kernel(mine_ref, other_ref, out_ref):
    total = mine_ref[...] + other_ref[...]
    out_ref[...] = jnp.broadcast_to(total[None], out_ref.shape)


def unfold(packed):
    lane, sub = iota((FOLD, LANES), 1), iota((FOLD, LANES), 0)
    square = jnp.concatenate([packed, jnp.zeros((LANES - FOLD, LANES), F32)], axis=0)
    turned = square.T
    top = jnp.where(lane >= sub, packed, turned[:FOLD, :])
    lower = packed[8:FOLD, :]
    upper = pltpu.roll(turned[: FOLD - 8, :], LANES - 8, 1)
    lane2, sub2 = iota((FOLD - 8, LANES), 1), iota((FOLD - 8, LANES), 0)
    corner = pltpu.roll(jnp.where(lane2 <= sub2, lower, upper), FOLD, 1)
    bottom = jnp.where(lane2 < FOLD, turned[FOLD:104, :], corner)
    return [top[8 * g : 8 * g + 8] for g in range(FOLD // 8)] + [
        bottom[8 * g : 8 * g + 8] for g in range(GROUPS - FOLD // 8)
    ]


def eliminate(groups):
    lane, sub = iota((8, LANES), 1), iota((8, LANES), 0)
    whole = lambda v: jnp.broadcast_to(v, (8, LANES))
    groups = list(groups)
    pivots = [jnp.ones((8, LANES), F32) for _ in range(GROUPS)]
    for g in range(GROUPS):
        first, count = 8 * g, min(8, RES - 8 * g)
        inside = (lane >= first) & (lane < first + count)
        columns = [[whole(group[:, first + j : first + j + 1]) for j in range(count)] for group in groups[g:]]
        left = [[whole(columns[0][j][i : i + 1, :]) for j in range(i + 1)] for i in range(count)]
        low = [[None] * count for _ in range(count)]
        inverse, rows = [], []
        for j in range(count):
            for i in range(j, count):
                for m in range(j):
                    left[i][j] = left[i][j] - low[i][m] * left[j][m]
            inverse.append(1.0 / left[j][j])
            for i in range(j + 1, count):
                low[i][j] = left[i][j] * inverse[j]
        for j in range(count):
            row = jnp.where(inside, jnp.where(lane == first + j, 1.0, 0.0), whole(groups[g][j : j + 1, :]))
            for m in range(j):
                row = row - low[j][m] * rows[m]
            rows.append(row)
            pivots[g] = jnp.where(sub == j, left[j][j], pivots[g])
        for h in range(g, GROUPS):
            if h == g and count == 8:
                continue
            new = jnp.where(inside, 0.0, groups[h])
            factors = []
            for j in range(count):
                factor = columns[h - g][j]
                for m in range(j):
                    factor = factor - factors[m] * left[j][m]
                factors.append(factor * inverse[j])
                new = new - factors[j] * rows[j]
            groups[h] = new
        for j in range(count):
            groups[g] = jnp.where(sub == j, rows[j], groups[g])
    return groups, pivots


def update(current, coefficients, hist_ref, halo, width):
    wide = [jnp.broadcast_to(c, (8, LANES)) for c in coefficients]
    pieces = []
    for start in range(0, width + LANES, LANES):
        total = jnp.zeros((8, LANES), F32)
        for g in range(GROUPS - 1):
            if start < width:
                part = hist_ref[8 * g : 8 * g + 8, start : start + LANES]
            else:
                part = halo[8 * g : 8 * g + 8, :]
            total = total + wide[g] * part
        if start < width:
            last = hist_ref[96:100, start : start + LANES]
        else:
            last = halo[96:100, :]
        pieces.append(
            jnp.sum(total, axis=0, keepdims=True)
            + jnp.sum(wide[GROUPS - 1][:4] * last, axis=0, keepdims=True)
        )
    return current + jnp.concatenate(pieces, axis=1)


def history_products(hist_ref, column, width):
    totals = [jnp.zeros((8, LANES), F32) for _ in range(GROUPS - 1)]
    last = jnp.zeros((4, LANES), F32)
    for start in range(0, width, LANES):
        part = column[:, start : start + LANES]
        wide = jnp.broadcast_to(part, (8, LANES))
        for g in range(GROUPS - 1):
            totals[g] = totals[g] + hist_ref[8 * g : 8 * g + 8, start : start + LANES] * wide
        last = last + hist_ref[96:100, start : start + LANES] * wide[:4]
    totals.append(jnp.concatenate([last, jnp.zeros((4, LANES), F32)], axis=0))
    return [jnp.sum(t, axis=1, keepdims=True) for t in totals]


def dot_rows(a, b):
    return jnp.sum(a * b, axis=1, keepdims=True)


def coefficient_of(row, at):
    return jnp.sum(jnp.where(iota((1, LANES), 1) == at, row, 0.0), axis=1, keepdims=True)


def send_row(out_ref, hist_ref, columns, column, residual, width):
    row = columns_to_row(history_products(hist_ref, column, width))
    lane = iota((1, LANES), 1)
    for at, other in enumerate((*columns, column, residual)):
        row = jnp.where(lane == HIST + at, dot_rows(other, column), row)
    out_ref[...] = jnp.broadcast_to(row, out_ref.shape)


def first_kernel(
    mine_ref, other_ref, hist_ref, hist_w_ref, state_ref, vectors_ref, right_ref, left_ref,
    row_ref, next_ref, factor_ref,
):
    width = hist_ref.shape[1]
    mine, other = mine_ref[...], other_ref[...]
    is_low = first_core()
    low, high = jnp.where(is_low, mine, other), jnp.where(is_low, other, mine)
    whole = unfold(jnp.concatenate([low, high[: FOLD - HALF]], axis=0))
    products = whole[RES // 8][RES % 8 : RES % 8 + 1, :]
    groups, pivots = eliminate(whole)
    coeffs = groups[RES // 8][RES % 8 : RES % 8 + 1, :]
    lane1 = iota((1, LANES), 1)
    coeffs = jnp.where(lane1 < RES, coeffs, 0.0)
    lane, sub = iota((8, LANES), 1), iota((8, LANES), 0)
    for g, group in enumerate(groups):
        row = sub + 8 * g
        scale = lax.rsqrt(pivots[g])
        unit = jnp.where(lane < row, group, jnp.where(lane == row, 1.0, 0.0))
        factor_ref[8 * g : 8 * g + 8, :] = jnp.where(row < RES, unit * scale, 0.0)
    factor_ref[104:112, :] = jnp.broadcast_to(jnp.where(lane1 < RES, products, 0.0), (8, LANES))

    halo = halo_of(right_ref, left_ref, slice(0, 104))
    forcing = extended(vectors_ref[3:4, :], halo[101:102])
    stiffness = extended(vectors_ref[4:5, :], halo[102:103])
    inside = inside_mask(width, halo[102:103])
    estimate = state_ref[0:1, :]
    residual = state_ref[1:2, :]
    moved = estimate - extended(vectors_ref[2:3, :], halo[103:104])
    column = state_ref[2:3, :width]
    current = update(estimate, row_to_columns(coeffs), hist_w_ref, halo, width)
    current = current + coefficient_of(coeffs, NEW) * moved
    estimate2 = solver_map(current, forcing, stiffness, inside)
    residual2 = estimate2 - current
    column2 = residual2[:, :width] - residual[:, :width]
    next_ref[0:1, :] = estimate2
    next_ref[1:2, :] = residual2
    next_ref[2:3, :width] = column
    next_ref[3:4, :width] = column2
    next_ref[4:5, :] = moved
    next_ref[5:6, :] = estimate2 - estimate
    send_row(row_ref, hist_ref, (column,), column2, residual2[:, :width], width)


def bordered(factor_ref, products, sent, count, extra):
    lane = iota((1, LANES), 1)
    cross = jnp.where(lane < count, sent, 0.0)
    square = coefficient_of(sent, count)
    with_residual = coefficient_of(sent, count + 1)
    products = jnp.where(lane == count, with_residual, jnp.where(lane < count, products + cross, 0.0))

    def solve(row):
        total = jnp.zeros((8, LANES), F32)
        norm = jnp.zeros((8, 1), F32)
        for g in range(GROUPS):
            block = factor_ref[8 * g : 8 * g + 8, :]
            y = jnp.sum(block * row, axis=1, keepdims=True)
            total = total + y * block
            norm = norm + y * y
        out, length = jnp.sum(total, axis=0, keepdims=True), jnp.sum(norm, axis=0, keepdims=True)
        for line in extra:
            y = dot_rows(line, row)
            out, length = out + y * line, length + y * y
        return out, length

    applied, length = solve(cross)
    scale = lax.rsqrt(square - length)
    line = jnp.where(lane == count, 1.0, -applied) * scale
    coeffs, _ = solve(products)
    coeffs = -(coeffs + dot_rows(line, products) * line)
    return coeffs, line, products


def second_kernel(
    got_ref, hist_ref, hist_w_ref, factor_ref, state_ref, vectors_ref, right_ref, left_ref,
    row_ref, next_ref, lines_ref,
):
    width = hist_ref.shape[1]
    sent = jnp.sum(got_ref[...], axis=0, keepdims=True)
    coeffs, line, products = bordered(factor_ref, factor_ref[104:105, :], sent, RES, ())
    lines_ref[0:1, :] = line
    lines_ref[1:2, :] = products
    halo = halo_of(right_ref, left_ref, slice(0, 104))
    forcing = extended(vectors_ref[3:4, :], halo[101:102])
    stiffness = extended(vectors_ref[4:5, :], halo[102:103])
    inside = inside_mask(width, halo[102:103])
    estimate = state_ref[0:1, :]
    residual = state_ref[1:2, :]
    moved, moved2 = state_ref[4:5, :], state_ref[5:6, :]
    column, column2 = state_ref[2:3, :width], state_ref[3:4, :width]
    current = update(estimate, row_to_columns(coeffs), hist_w_ref, halo, width)
    current = current + coefficient_of(coeffs, NEW) * moved + coefficient_of(coeffs, NEW + 1) * moved2
    estimate3 = solver_map(current, forcing, stiffness, inside)
    residual3 = estimate3 - current
    column3 = residual3[:, :width] - residual[:, :width]
    next_ref[0:1, :] = estimate3
    next_ref[1:2, :] = residual3
    next_ref[4:5, :] = moved
    next_ref[5:6, :] = moved2
    next_ref[6:7, :] = estimate3 - estimate
    send_row(row_ref, hist_ref, (column, column2), column3, residual3[:, :width], width)


def third_kernel(
    got_ref, hist_w_ref, factor_ref, lines_ref, state_ref, current_ref, residual_ref,
):
    width = hist_w_ref.shape[1]
    sent = jnp.sum(got_ref[...], axis=0, keepdims=True)
    coeffs, _, _ = bordered(factor_ref, lines_ref[1:2, :], sent, RES + 1, (lines_ref[0:1, :],))
    estimate = state_ref[0:1, :]
    halo = jnp.zeros((104, LANES), F32)
    current = update(estimate, row_to_columns(coeffs), hist_w_ref, halo, width)
    for at in range(ITERS):
        current = current + coefficient_of(coeffs, NEW + at) * state_ref[4 + at : 5 + at, :]
    current_ref[...] = current[:, :width]
    residual_ref[...] = state_ref[1:2, :width]


def call(kernel, outs, scratch=(), held=0, inputs=0, copies=0, flops=0):
    extra = {}
    if inputs:
        extra["in_specs"] = [VMEM] * held + [pl.BlockSpec(memory_space=pltpu.HBM)] * inputs
    return pl.pallas_call(
        kernel,
        out_shape=[jax.ShapeDtypeStruct(s, F32) for s in outs],
        out_specs=[VMEM] * len(outs),
        scratch_shapes=[*scratch, *([pltpu.SemaphoreType.DMA((copies,))] if copies else [])],
        cost_estimate=pl.CostEstimate(flops=flops, bytes_accessed=2**22, transcendentals=0) if flops else None,
        compiler_params=pltpu.CompilerParams(vmem_limit_bytes=12 * 2**20),
        **extra,
    )


def in_hbm(value):
    return pltpu.with_memory_space_constraint(value, pltpu.HBM)


def everywhere(blocks, axes):
    return lax.all_to_all(blocks, axes, 0, 0)


def spread_rows(rows):
    count = rows.shape[0]
    return everywhere(rows.reshape(count, 1, LANES), AXES).reshape(count, LANES)


def shards(interface, previous_residual, previous_estimate, forcing, stiffness, hist_v, hist_w):
    width = interface.shape[0]
    count = lax.axis_size(AXES)
    plane, depth = lax.axis_size(("y", "x")), lax.axis_size("z")
    row = lambda v: in_hbm(v.reshape(1, width))
    hist = pltpu.with_memory_space_constraint(hist_v, pltpu.VMEM)
    held_w = pltpu.with_memory_space_constraint(hist_w, pltpu.VMEM)
    current, residual, estimate = row(interface), row(previous_residual), row(previous_estimate)
    forcing, stiffness = row(forcing), row(stiffness)
    edge, state_shape = (104, LANES), (8, width + LANES)

    last, first = call(edge_kernel, [edge, edge], inputs=5, copies=10)(
        in_hbm(hist_w), current, forcing, stiffness, estimate
    )
    left = lax.ppermute(last, AXES, [(i, i + 1) for i in range(count - 1)])
    right = lax.ppermute(first, AXES, [(i + 1, i) for i in range(count - 1)])
    vectors, gram = call(
        gram_kernel,
        [(8, width), edge],
        [pltpu.VMEM((2 * LANES, width), jnp.bfloat16)],
        held=1,
        inputs=5,
        copies=5,
        flops=2**30,
    )(hist, current, residual, estimate, forcing, stiffness)
    half = (HALF, LANES)
    mine, other, state = call(
        column_kernel, [half, half, state_shape], [pltpu.VMEM((2 * HALF, LANES), F32)]
    )(gram, hist, vectors, right, left)
    swap = lambda v: lax.ppermute(v, "core", [(i, i ^ 1) for i in range(lax.axis_size("core"))])
    (copies,) = call(pair_kernel, [(plane, *half)])(mine, swap(other))
    (copies,) = call(spread_kernel, [(depth, *half)])(everywhere(copies, ("y", "x")))
    (mine,) = call(total_kernel, [half])(everywhere(copies, "z"))
    sent, state, factor = call(first_kernel, [(count, LANES), state_shape, (112, LANES)])(
        mine, swap(mine), hist, held_w, state, vectors, right, left
    )
    sent, state, lines = call(second_kernel, [(count, LANES), state_shape, (8, LANES)])(
        spread_rows(sent), hist, held_w, factor, state, vectors, right, left
    )
    current, residual = call(third_kernel, [(1, width), (1, width)])(
        spread_rows(sent), held_w, factor, lines, state
    )
    return current.reshape(width), residual.reshape(width)


def solution(mesh):
    devices = mesh.devices.reshape(4, 8, 2, 4) if mesh.devices.size == 256 else mesh.devices.reshape(2, 2, 2, -1)
    finer = Mesh(devices, AXES)
    whole, columns = P(AXES), P(None, AXES)
    return jax.shard_map(
        shards,
        mesh=finer,
        in_specs=(whole,) * 5 + (columns,) * 2,
        out_specs=(whole, whole),
        check_vma=False,
    )
```

```python
import functools

import jax
import jax.numpy as jnp
from jax import lax
from jax.experimental import pallas as pl
from jax.experimental.pallas import tpu as pltpu
from jax.sharding import Mesh
from jax.sharding import PartitionSpec as P

ITERS = 3
AXES = ("y", "z", "core", "x")
COUPLING = 0.25
LANES = 128
HIST = 100
NEW = HIST
RES = HIST + 1
FOLD = 56
HALF = 32
GROUPS = 13

F32 = jnp.float32
VMEM = pl.BlockSpec(memory_space=pltpu.VMEM)


def iota(shape, axis):
    return lax.broadcasted_iota(jnp.int32, shape, axis)


def rows_of(group):
    return slice(8 * group, min(8 * group + 8, HIST))


def row_to_columns(row):
    lane, sub = iota((8, LANES), 1), iota((8, LANES), 0)
    full = jnp.broadcast_to(row, (8, LANES))
    return [
        jnp.sum(jnp.where(lane == sub + 8 * g, full, 0.0), axis=1, keepdims=True)
        for g in range(GROUPS)
    ]


def columns_to_row(columns):
    lane, sub = iota((8, LANES), 1), iota((8, LANES), 0)
    total = jnp.zeros((8, LANES), F32)
    for g, column in enumerate(columns):
        total = total + jnp.where(lane == sub + 8 * g, jnp.broadcast_to(column, (8, LANES)), 0.0)
    return jnp.sum(total, axis=0, keepdims=True)


def solver_map(current, forcing, stiffness, inside):
    width = current.shape[1]
    neighbours = pltpu.roll(current, 1, 1) + pltpu.roll(current, width - 1, 1)
    estimate = forcing + stiffness * jnp.tanh(current) + COUPLING * neighbours
    return jnp.where(inside, estimate, 0.0)


def even_place():
    return lax.rem(lax.axis_index("x"), 2) == 0


def halo_of(near_ref, beyond_ref, rows):
    shape = (rows.stop - rows.start, LANES)
    from_right = iota(shape, 1) < LANES // 2
    even = jnp.full(shape, jnp.where(even_place(), 1, 0), jnp.int32) == 1
    return jnp.where(from_right == even, near_ref[rows, :], beyond_ref[rows, :])


def extended(row, halo):
    return jnp.concatenate([row, halo], axis=1)


def inside_mask(width, stiffness_halo):
    ones = jnp.ones((1, width), F32)
    return extended(ones, jnp.where(stiffness_halo != 0.0, 1.0, 0.0)) > 0.5


def copy_all(pairs, sems):
    copies = [pltpu.make_async_copy(src, dst, sems.at[i]) for i, (src, dst) in enumerate(pairs)]
    for copy in copies:
        copy.start()
    return copies


def edge_kernel(
    hist_ref, current_ref, forcing_ref, stiffness_ref, old_est_ref, near_ref, beyond_ref, sems
):
    width = hist_ref.shape[1]
    pairs = []
    last = jnp.where(even_place(), width - LANES, 0)
    for out_ref, at in ((near_ref, last), (beyond_ref, width - LANES - last)):
        columns = pl.ds(pl.multiple_of(at, LANES), LANES)
        pairs.append((hist_ref.at[:, columns], out_ref.at[:HIST, :]))
        for i, ref in enumerate((current_ref, forcing_ref, stiffness_ref, old_est_ref)):
            pairs.append((ref.at[:, columns], out_ref.at[HIST + i : HIST + i + 1, :]))
    for copy in copy_all(pairs, sems):
        copy.wait()


def gram_kernel(
    hist_ref, current_ref, old_res_ref, old_est_ref, forcing_ref, stiffness_ref,
    vectors_ref, gram_ref, parts_ref, sems,
):
    width = hist_ref.shape[1]
    vectors = (current_ref, old_res_ref, old_est_ref, forcing_ref, stiffness_ref)
    copies = copy_all([(ref, vectors_ref.at[i : i + 1, :]) for i, ref in enumerate(vectors)], sems)

    def put(row, values):
        high = values.astype(jnp.bfloat16)
        parts_ref[row : row + values.shape[0], :] = high
        parts_ref[LANES + row : LANES + row + values.shape[0], :] = (
            values - high.astype(F32)
        ).astype(jnp.bfloat16)

    put(112, jnp.zeros((16, width), F32))
    for start in range(0, 96, 16):
        put(start, hist_ref[start : start + 16, :])
    put(96, jnp.concatenate([hist_ref[96:100, :], jnp.zeros((12, width), F32)], axis=0))
    products = lax.dot_general(
        parts_ref[:LANES, :],
        parts_ref[...],
        (((1,), (1,)), ((), ())),
        preferred_element_type=F32,
    )
    cross = products[:, LANES:]
    gram_ref[...] = (products[:, :LANES] + cross + cross.T)[:104]
    for copy in copies:
        copy.wait()


def column_kernel(
    gram_ref, hist_ref, vectors_ref, near_ref, beyond_ref, mine_ref, other_ref, state_ref, packed_ref
):
    width = hist_ref.shape[1]
    halo = halo_of(near_ref, beyond_ref, slice(96, 104))
    current = extended(vectors_ref[0:1, :], halo[4:5])
    inside = inside_mask(width, halo[6:7])
    estimate = solver_map(
        current,
        extended(vectors_ref[3:4, :], halo[5:6]),
        extended(vectors_ref[4:5, :], halo[6:7]),
        inside,
    )
    residual = estimate - current
    column = residual[:, :width] - vectors_ref[1:2, :]
    state_ref[0:1, :] = estimate
    state_ref[1:2, :] = residual
    state_ref[2:3, :width] = column
    residual = residual[:, :width]
    by_column = history_products(hist_ref, column, width)
    by_residual = history_products(hist_ref, residual, width)
    square, mixed = dot_rows(column, column), dot_rows(column, residual)
    lane1 = iota((1, LANES), 1)
    column_row = jnp.where(lane1 == NEW, square, columns_to_row(by_column))
    residual_row = jnp.where(lane1 == NEW, mixed, columns_to_row(by_residual))
    lane, sub = iota((8, LANES), 1), iota((8, LANES), 0)
    top = [
        jnp.where(lane == NEW, by_column[g], jnp.where(lane == RES, by_residual[g], gram_ref[8 * g : 8 * g + 8, :]))
        for g in range(FOLD // 8)
    ]
    bottom = [gram_ref[8 * g : 8 * g + 8, :] for g in range(FOLD // 8, GROUPS)]
    at = NEW - 8 * (GROUPS - 1)
    bottom[-1] = jnp.where(sub == at, column_row, jnp.where(sub == at + 1, residual_row, bottom[-1]))
    packed_ref[:8, :] = top[0]
    for g in range(1, FOLD // 8):
        corner = pltpu.roll(bottom[g - 1], LANES - FOLD, 1)
        packed_ref[8 * g : 8 * g + 8, :] = jnp.where(lane <= sub + 8 * (g - 1), corner, top[g])
    packed_ref[FOLD:, :] = jnp.zeros((2 * HALF - FOLD, LANES), F32)
    low, high = packed_ref[:HALF, :], packed_ref[HALF:, :]
    is_low = first_core()
    mine_ref[...] = jnp.where(is_low, low, high)
    other_ref[...] = jnp.where(is_low, high, low)


def first_core():
    return jnp.full((HALF, LANES), lax.axis_index("core"), jnp.int32) == 0


def total_kernel(got_ref, out_ref):
    out_ref[...] = jnp.sum(got_ref[...], axis=0)


def spread_kernel(got_ref, out_ref):
    total = jnp.sum(got_ref[...], axis=0)
    out_ref[...] = jnp.broadcast_to(total[None], out_ref.shape)


def pair_kernel(mine_ref, other_ref, out_ref):
    total = mine_ref[...] + other_ref[...]
    out_ref[...] = jnp.broadcast_to(total[None], out_ref.shape)


def unfold(packed):
    lane, sub = iota((FOLD, LANES), 1), iota((FOLD, LANES), 0)
    square = jnp.concatenate([packed, jnp.zeros((LANES - FOLD, LANES), F32)], axis=0)
    turned = square.T
    top = jnp.where(lane >= sub, packed, turned[:FOLD, :])
    lower = packed[8:FOLD, :]
    upper = pltpu.roll(turned[: FOLD - 8, :], LANES - 8, 1)
    lane2, sub2 = iota((FOLD - 8, LANES), 1), iota((FOLD - 8, LANES), 0)
    corner = pltpu.roll(jnp.where(lane2 <= sub2, lower, upper), FOLD, 1)
    bottom = jnp.where(lane2 < FOLD, turned[FOLD:104, :], corner)
    return [top[8 * g : 8 * g + 8] for g in range(FOLD // 8)] + [
        bottom[8 * g : 8 * g + 8] for g in range(GROUPS - FOLD // 8)
    ]


def eliminate(groups):
    lane, sub = iota((8, LANES), 1), iota((8, LANES), 0)
    whole = lambda v: jnp.broadcast_to(v, (8, LANES))
    groups = list(groups)
    pivots = [jnp.ones((8, LANES), F32) for _ in range(GROUPS)]
    for g in range(GROUPS):
        first, count = 8 * g, min(8, RES - 8 * g)
        inside = (lane >= first) & (lane < first + count)
        columns = [[whole(group[:, first + j : first + j + 1]) for j in range(count)] for group in groups[g:]]
        left = [[whole(columns[0][j][i : i + 1, :]) for j in range(i + 1)] for i in range(count)]
        low = [[None] * count for _ in range(count)]
        inverse, rows = [], []
        for j in range(count):
            for i in range(j, count):
                for m in range(j):
                    left[i][j] = left[i][j] - low[i][m] * left[j][m]
            inverse.append(1.0 / left[j][j])
            for i in range(j + 1, count):
                low[i][j] = left[i][j] * inverse[j]
        for j in range(count):
            row = jnp.where(inside, jnp.where(lane == first + j, 1.0, 0.0), whole(groups[g][j : j + 1, :]))
            for m in range(j):
                row = row - low[j][m] * rows[m]
            rows.append(row)
            pivots[g] = jnp.where(sub == j, left[j][j], pivots[g])
        for h in range(g, GROUPS):
            if h == g and count == 8:
                continue
            new = jnp.where(inside, 0.0, groups[h])
            factors = []
            for j in range(count):
                factor = columns[h - g][j]
                for m in range(j):
                    factor = factor - factors[m] * left[j][m]
                factors.append(factor * inverse[j])
                new = new - factors[j] * rows[j]
            groups[h] = new
        for j in range(count):
            groups[g] = jnp.where(sub == j, rows[j], groups[g])
    return groups, pivots


def update(current, coefficients, hist_ref, halo, width):
    wide = [jnp.broadcast_to(c, (8, LANES)) for c in coefficients]
    pieces = []
    for start in range(0, width + LANES, LANES):
        total = jnp.zeros((8, LANES), F32)
        for g in range(GROUPS - 1):
            if start < width:
                part = hist_ref[8 * g : 8 * g + 8, start : start + LANES]
            else:
                part = halo[8 * g : 8 * g + 8, :]
            total = total + wide[g] * part
        if start < width:
            last = hist_ref[96:100, start : start + LANES]
        else:
            last = halo[96:100, :]
        pieces.append(
            jnp.sum(total, axis=0, keepdims=True)
            + jnp.sum(wide[GROUPS - 1][:4] * last, axis=0, keepdims=True)
        )
    return current + jnp.concatenate(pieces, axis=1)


def history_products(hist_ref, column, width):
    totals = [jnp.zeros((8, LANES), F32) for _ in range(GROUPS - 1)]
    last = jnp.zeros((4, LANES), F32)
    for start in range(0, width, LANES):
        part = column[:, start : start + LANES]
        wide = jnp.broadcast_to(part, (8, LANES))
        for g in range(GROUPS - 1):
            totals[g] = totals[g] + hist_ref[8 * g : 8 * g + 8, start : start + LANES] * wide
        last = last + hist_ref[96:100, start : start + LANES] * wide[:4]
    totals.append(jnp.concatenate([last, jnp.zeros((4, LANES), F32)], axis=0))
    return [jnp.sum(t, axis=1, keepdims=True) for t in totals]


def dot_rows(a, b):
    return jnp.sum(a * b, axis=1, keepdims=True)


def coefficient_of(row, at):
    return jnp.sum(jnp.where(iota((1, LANES), 1) == at, row, 0.0), axis=1, keepdims=True)


def send_row(out_ref, hist_ref, columns, column, residual, width):
    row = columns_to_row(history_products(hist_ref, column, width))
    lane = iota((1, LANES), 1)
    for at, other in enumerate((*columns, column, residual)):
        row = jnp.where(lane == HIST + at, dot_rows(other, column), row)
    out_ref[...] = jnp.broadcast_to(row, out_ref.shape)


def first_kernel(
    mine_ref, other_ref, hist_ref, hist_w_ref, state_ref, vectors_ref, near_ref, beyond_ref,
    row_ref, next_ref, factor_ref,
):
    width = hist_ref.shape[1]
    mine, other = mine_ref[...], other_ref[...]
    is_low = first_core()
    low, high = jnp.where(is_low, mine, other), jnp.where(is_low, other, mine)
    whole = unfold(jnp.concatenate([low, high[: FOLD - HALF]], axis=0))
    products = whole[RES // 8][RES % 8 : RES % 8 + 1, :]
    groups, pivots = eliminate(whole)
    coeffs = groups[RES // 8][RES % 8 : RES % 8 + 1, :]
    lane1 = iota((1, LANES), 1)
    coeffs = jnp.where(lane1 < RES, coeffs, 0.0)
    lane, sub = iota((8, LANES), 1), iota((8, LANES), 0)
    for g, group in enumerate(groups):
        row = sub + 8 * g
        scale = lax.rsqrt(pivots[g])
        unit = jnp.where(lane < row, group, jnp.where(lane == row, 1.0, 0.0))
        factor_ref[8 * g : 8 * g + 8, :] = jnp.where(row < RES, unit * scale, 0.0)
    factor_ref[104:112, :] = jnp.broadcast_to(jnp.where(lane1 < RES, products, 0.0), (8, LANES))

    halo = halo_of(near_ref, beyond_ref, slice(0, 104))
    forcing = extended(vectors_ref[3:4, :], halo[101:102])
    stiffness = extended(vectors_ref[4:5, :], halo[102:103])
    inside = inside_mask(width, halo[102:103])
    estimate = state_ref[0:1, :]
    residual = state_ref[1:2, :]
    moved = estimate - extended(vectors_ref[2:3, :], halo[103:104])
    column = state_ref[2:3, :width]
    current = update(estimate, row_to_columns(coeffs), hist_w_ref, halo, width)
    current = current + coefficient_of(coeffs, NEW) * moved
    estimate2 = solver_map(current, forcing, stiffness, inside)
    residual2 = estimate2 - current
    column2 = residual2[:, :width] - residual[:, :width]
    next_ref[0:1, :] = estimate2
    next_ref[1:2, :] = residual2
    next_ref[2:3, :width] = column
    next_ref[3:4, :width] = column2
    next_ref[4:5, :] = moved
    next_ref[5:6, :] = estimate2 - estimate
    send_row(row_ref, hist_ref, (column,), column2, residual2[:, :width], width)


def bordered(factor_ref, products, sent, count, extra):
    lane = iota((1, LANES), 1)
    cross = jnp.where(lane < count, sent, 0.0)
    square = coefficient_of(sent, count)
    with_residual = coefficient_of(sent, count + 1)
    products = jnp.where(lane == count, with_residual, jnp.where(lane < count, products + cross, 0.0))

    def solve(row):
        total = jnp.zeros((8, LANES), F32)
        norm = jnp.zeros((8, 1), F32)
        for g in range(GROUPS):
            block = factor_ref[8 * g : 8 * g + 8, :]
            y = jnp.sum(block * row, axis=1, keepdims=True)
            total = total + y * block
            norm = norm + y * y
        out, length = jnp.sum(total, axis=0, keepdims=True), jnp.sum(norm, axis=0, keepdims=True)
        for line in extra:
            y = dot_rows(line, row)
            out, length = out + y * line, length + y * y
        return out, length

    applied, length = solve(cross)
    scale = lax.rsqrt(square - length)
    line = jnp.where(lane == count, 1.0, -applied) * scale
    coeffs, _ = solve(products)
    coeffs = -(coeffs + dot_rows(line, products) * line)
    return coeffs, line, products


def second_kernel(
    got_ref, hist_ref, hist_w_ref, factor_ref, state_ref, vectors_ref, near_ref, beyond_ref,
    row_ref, next_ref, lines_ref,
):
    width = hist_ref.shape[1]
    sent = jnp.sum(got_ref[...], axis=0, keepdims=True)
    coeffs, line, products = bordered(factor_ref, factor_ref[104:105, :], sent, RES, ())
    lines_ref[0:1, :] = line
    lines_ref[1:2, :] = products
    halo = halo_of(near_ref, beyond_ref, slice(0, 104))
    forcing = extended(vectors_ref[3:4, :], halo[101:102])
    stiffness = extended(vectors_ref[4:5, :], halo[102:103])
    inside = inside_mask(width, halo[102:103])
    estimate = state_ref[0:1, :]
    residual = state_ref[1:2, :]
    moved, moved2 = state_ref[4:5, :], state_ref[5:6, :]
    column, column2 = state_ref[2:3, :width], state_ref[3:4, :width]
    current = update(estimate, row_to_columns(coeffs), hist_w_ref, halo, width)
    current = current + coefficient_of(coeffs, NEW) * moved + coefficient_of(coeffs, NEW + 1) * moved2
    estimate3 = solver_map(current, forcing, stiffness, inside)
    residual3 = estimate3 - current
    column3 = residual3[:, :width] - residual[:, :width]
    next_ref[0:1, :] = estimate3
    next_ref[1:2, :] = residual3
    next_ref[4:5, :] = moved
    next_ref[5:6, :] = moved2
    next_ref[6:7, :] = estimate3 - estimate
    send_row(row_ref, hist_ref, (column, column2), column3, residual3[:, :width], width)


def third_kernel(
    got_ref, hist_w_ref, factor_ref, lines_ref, state_ref, current_ref, residual_ref,
):
    width = hist_w_ref.shape[1]
    sent = jnp.sum(got_ref[...], axis=0, keepdims=True)
    coeffs, _, _ = bordered(factor_ref, lines_ref[1:2, :], sent, RES + 1, (lines_ref[0:1, :],))
    estimate = state_ref[0:1, :]
    halo = jnp.zeros((104, LANES), F32)
    current = update(estimate, row_to_columns(coeffs), hist_w_ref, halo, width)
    for at in range(ITERS):
        current = current + coefficient_of(coeffs, NEW + at) * state_ref[4 + at : 5 + at, :]
    current_ref[...] = current[:, :width]
    residual_ref[...] = state_ref[1:2, :width]


def call(kernel, outs, scratch=(), held=0, inputs=0, copies=0, flops=0):
    extra = {}
    if inputs:
        extra["in_specs"] = [VMEM] * held + [pl.BlockSpec(memory_space=pltpu.HBM)] * inputs
    return pl.pallas_call(
        kernel,
        out_shape=[jax.ShapeDtypeStruct(s, F32) for s in outs],
        out_specs=[VMEM] * len(outs),
        scratch_shapes=[*scratch, *([pltpu.SemaphoreType.DMA((copies,))] if copies else [])],
        cost_estimate=pl.CostEstimate(flops=flops, bytes_accessed=2**22, transcendentals=0) if flops else None,
        compiler_params=pltpu.CompilerParams(vmem_limit_bytes=12 * 2**20),
        **extra,
    )


def in_hbm(value):
    return pltpu.with_memory_space_constraint(value, pltpu.HBM)


def everywhere(blocks, axes):
    return lax.all_to_all(blocks, axes, 0, 0)


def spread_rows(rows):
    count = rows.shape[0]
    return everywhere(rows.reshape(count, 1, LANES), AXES).reshape(count, LANES)


def shards(interface, previous_residual, previous_estimate, forcing, stiffness, hist_v, hist_w):
    width = interface.shape[0]
    count = lax.axis_size(AXES)
    plane, depth = lax.axis_size(("y", "x")), lax.axis_size("z")
    row = lambda v: in_hbm(v.reshape(1, width))
    hist = pltpu.with_memory_space_constraint(hist_v, pltpu.VMEM)
    held_w = pltpu.with_memory_space_constraint(hist_w, pltpu.VMEM)
    current, residual, estimate = row(interface), row(previous_residual), row(previous_estimate)
    forcing, stiffness = row(forcing), row(stiffness)
    edge, state_shape = (104, LANES), (8, width + LANES)

    near, beyond = call(edge_kernel, [edge, edge], inputs=5, copies=10)(
        in_hbm(hist_w), current, forcing, stiffness, estimate
    )
    near = lax.ppermute(near, AXES, [(i, i ^ 1) for i in range(count)])
    steps = [(i, i + 1) for i in range(1, count - 1, 2)]
    beyond = lax.ppermute(beyond, AXES, steps + [(j, i) for i, j in steps])
    vectors, gram = call(
        gram_kernel,
        [(8, width), edge],
        [pltpu.VMEM((2 * LANES, width), jnp.bfloat16)],
        held=1,
        inputs=5,
        copies=5,
        flops=2**30,
    )(hist, current, residual, estimate, forcing, stiffness)
    half = (HALF, LANES)
    mine, other, state = call(
        column_kernel, [half, half, state_shape], [pltpu.VMEM((2 * HALF, LANES), F32)]
    )(gram, hist, vectors, near, beyond)
    swap = lambda v: lax.ppermute(v, "core", [(i, i ^ 1) for i in range(lax.axis_size("core"))])
    (copies,) = call(pair_kernel, [(plane, *half)])(mine, swap(other))
    (copies,) = call(spread_kernel, [(depth, *half)])(everywhere(copies, ("y", "x")))
    (mine,) = call(total_kernel, [half])(everywhere(copies, "z"))
    sent, state, factor = call(first_kernel, [(count, LANES), state_shape, (112, LANES)])(
        mine, swap(mine), hist, held_w, state, vectors, near, beyond
    )
    sent, state, lines = call(second_kernel, [(count, LANES), state_shape, (8, LANES)])(
        spread_rows(sent), hist, held_w, factor, state, vectors, near, beyond
    )
    current, residual = call(third_kernel, [(1, width), (1, width)])(
        spread_rows(sent), held_w, factor, lines, state
    )
    return current.reshape(width), residual.reshape(width)


def solution(mesh):
    devices = mesh.devices.reshape(4, 8, 2, 4) if mesh.devices.size == 256 else mesh.devices.reshape(2, 2, 2, -1)
    finer = Mesh(devices, AXES)
    whole, columns = P(AXES), P(None, AXES)
    return jax.shard_map(
        shards,
        mesh=finer,
        in_specs=(whole,) * 5 + (columns,) * 2,
        out_specs=(whole, whole),
        check_vma=False,
    )
```

```python
import functools

import jax
import jax.numpy as jnp
from jax import lax
from jax.experimental import pallas as pl
from jax.experimental.pallas import tpu as pltpu
from jax.sharding import Mesh
from jax.sharding import PartitionSpec as P

ITERS = 3
AXES = ("y", "z", "core", "x")
COUPLING = 0.25
LANES = 128
HIST = 100
NEW = HIST
RES = HIST + 1
FOLD = 56
HALF = 32
FREE = 104
SCALARS = FREE + 8
GROUPS = 13

F32 = jnp.float32
VMEM = pl.BlockSpec(memory_space=pltpu.VMEM)


def iota(shape, axis):
    return lax.broadcasted_iota(jnp.int32, shape, axis)


def rows_of(group):
    return slice(8 * group, min(8 * group + 8, HIST))


def row_to_columns(row):
    lane, sub = iota((8, LANES), 1), iota((8, LANES), 0)
    full = jnp.broadcast_to(row, (8, LANES))
    return [
        jnp.sum(jnp.where(lane == sub + 8 * g, full, 0.0), axis=1, keepdims=True)
        for g in range(GROUPS)
    ]


def columns_to_row(columns):
    lane, sub = iota((8, LANES), 1), iota((8, LANES), 0)
    total = jnp.zeros((8, LANES), F32)
    for g, column in enumerate(columns):
        total = total + jnp.where(lane == sub + 8 * g, jnp.broadcast_to(column, (8, LANES)), 0.0)
    return jnp.sum(total, axis=0, keepdims=True)


def solver_map(current, forcing, stiffness, inside):
    width = current.shape[1]
    neighbours = pltpu.roll(current, 1, 1) + pltpu.roll(current, width - 1, 1)
    estimate = forcing + stiffness * jnp.tanh(current) + COUPLING * neighbours
    return jnp.where(inside, estimate, 0.0)


def even_place():
    return lax.rem(lax.axis_index("x"), 2) == 0


def halo_of(near_ref, beyond_ref):
    even = jnp.full((8, LANES), jnp.where(even_place(), 1, 0), jnp.int32) == 1
    near, beyond = near_ref[...], beyond_ref[...]
    right, left = jnp.where(even, near, beyond), jnp.where(even, beyond, near)
    return jnp.concatenate([right, jnp.zeros((LANES - 16, LANES), F32), left], axis=0).T[:104]


def extended(row, halo):
    return jnp.concatenate([row, halo], axis=1)


def inside_mask(width, stiffness_halo):
    ones = jnp.ones((1, width), F32)
    return extended(ones, jnp.where(stiffness_halo != 0.0, 1.0, 0.0)) > 0.5


def copy_all(pairs, sems):
    copies = [pltpu.make_async_copy(src, dst, sems.at[i]) for i, (src, dst) in enumerate(pairs)]
    for copy in copies:
        copy.start()
    return copies


def edge_kernel(
    hist_ref, current_ref, forcing_ref, stiffness_ref, old_est_ref,
    near_ref, beyond_ref, first_ref, last_ref, sems,
):
    width = hist_ref.shape[1]
    pairs = []
    for block_ref, at in ((first_ref, 0), (last_ref, width - LANES)):
        columns = slice(at, at + LANES)
        pairs.append((hist_ref.at[:, columns], block_ref.at[:HIST, :]))
        for i, ref in enumerate((current_ref, forcing_ref, stiffness_ref, old_est_ref)):
            pairs.append((ref.at[:, columns], block_ref.at[HIST + i : HIST + i + 1, :]))
    copies = copy_all(pairs, sems)
    for block_ref in (first_ref, last_ref):
        block_ref[104:, :] = jnp.zeros((LANES - 104, LANES), F32)
    for copy in copies:
        copy.wait()
    even = jnp.full((8, LANES), jnp.where(even_place(), 1, 0), jnp.int32) == 1
    first, last = first_ref[...].T[:8], last_ref[...].T[LANES - 8 :]
    near_ref[...] = jnp.where(even, last, first)
    beyond_ref[...] = jnp.where(even, first, last)


def first_core():
    return jnp.full((HALF, LANES), lax.axis_index("core"), jnp.int32) == 0


def place(g, kind):
    at = 8 * (g % (HALF // 8))
    return slice(at, at + 8), FREE + 4 * kind + g // (HALF // 8)


def gram_kernel(
    hist_ref, current_ref, old_res_ref, old_est_ref, forcing_ref, stiffness_ref,
    vectors_ref, mine_ref, other_ref, products_ref, parts_ref, packed_ref, sems,
):
    width = hist_ref.shape[1]
    vectors = (current_ref, old_res_ref, old_est_ref, forcing_ref, stiffness_ref)
    copies = copy_all([(ref, vectors_ref.at[i : i + 1, :]) for i, ref in enumerate(vectors)], sems)

    def put(row, values):
        high = values.astype(jnp.bfloat16)
        parts_ref[row : row + values.shape[0], :] = high
        parts_ref[LANES + row : LANES + row + values.shape[0], :] = (
            values - high.astype(F32)
        ).astype(jnp.bfloat16)

    put(112, jnp.zeros((16, width), F32))
    for start in range(0, 96, 16):
        put(start, hist_ref[start : start + 16, :])
    put(96, jnp.concatenate([hist_ref[96:100, :], jnp.zeros((12, width), F32)], axis=0))
    products = lax.dot_general(
        parts_ref[:LANES, :],
        parts_ref[...],
        (((1,), (1,)), ((), ())),
        preferred_element_type=F32,
    )
    cross = products[:, LANES:]
    gram = (products[:, :LANES] + cross + cross.T)[:104]
    lane, sub = iota((8, LANES), 1), iota((8, LANES), 0)
    packed_ref[:8, :] = gram[:8]
    for g in range(1, FOLD // 8):
        corner = pltpu.roll(gram[FOLD + 8 * g - 8 : FOLD + 8 * g], LANES - FOLD, 1)
        packed_ref[8 * g : 8 * g + 8, :] = jnp.where(
            lane <= sub + 8 * (g - 1), corner, gram[8 * g : 8 * g + 8]
        )
    packed_ref[FOLD:, :] = jnp.zeros((2 * HALF - FOLD, LANES), F32)
    low, high = packed_ref[:HALF, :], packed_ref[HALF:, :]
    is_low = first_core()
    mine_ref[...] = jnp.where(is_low, low, high)
    other_ref[...] = jnp.where(is_low, high, low)

    for copy in copies:
        copy.wait()
    nothing = jnp.zeros((1, LANES), F32)
    wide = [extended(vectors_ref[i : i + 1, :], nothing) for i in (0, 3, 4)]
    residual = (solver_map(*wide, iota((1, width + LANES), 1) < width) - wide[0])[:, :width]
    column = residual - vectors_ref[1:2, :]
    blocks = [jnp.zeros((8, LANES), F32) for _ in range(HALF // 8)]
    for kind, row in enumerate((column, residual)):
        for g, part in enumerate(history_products(hist_ref, row, width)):
            at = g % (HALF // 8)
            blocks[at] = jnp.where(lane == place(g, kind)[1], part, blocks[at])
    for at, block in enumerate(blocks):
        products_ref[8 * at : 8 * at + 8, :] = block


def column_kernel(
    products_ref, hist_ref, vectors_ref, near_ref, beyond_ref, out_ref, state_ref, halo_ref
):
    width = hist_ref.shape[1]
    halo = halo_of(near_ref, beyond_ref)
    halo_ref[...] = halo
    current = extended(vectors_ref[0:1, :], halo[100:101])
    estimate = solver_map(
        current,
        extended(vectors_ref[3:4, :], halo[101:102]),
        extended(vectors_ref[4:5, :], halo[102:103]),
        inside_mask(width, halo[102:103]),
    )
    residual = estimate - current
    column = residual[:, :width] - vectors_ref[1:2, :]
    state_ref[0:1, :] = estimate
    state_ref[1:2, :] = residual
    state_ref[2:3, :width] = column
    residual = residual[:, :width]
    before = COUPLING * coefficient_of(halo[100:101], LANES - 1)
    after = COUPLING * coefficient_of(halo[100:101], 0)
    lane, sub = iota((8, LANES), 1), iota((8, LANES), 0)
    blocks = [products_ref[8 * at : 8 * at + 8, :] for at in range(HALF // 8)]
    for g in range(GROUPS):
        rows = rows_of(g)
        edge = before * hist_ref[rows, :LANES][:, :1] + after * hist_ref[rows, width - LANES :][:, LANES - 1 :]
        if edge.shape[0] < 8:
            edge = jnp.concatenate([edge, jnp.zeros((8 - edge.shape[0], 1), F32)], axis=0)
        at = g % (HALF // 8)
        mask = (lane == place(g, 0)[1]) | (lane == place(g, 1)[1])
        blocks[at] = blocks[at] + jnp.where(mask, edge, 0.0)
    square, mixed = dot_rows(column, column), dot_rows(column, residual)
    blocks[0] = jnp.where(lane == SCALARS, jnp.where(sub == 0, square, jnp.where(sub == 1, mixed, 0.0)), blocks[0])
    for at, block in enumerate(blocks):
        out_ref[8 * at : 8 * at + 8, :] = block


def pair_kernel(mine_ref, other_ref, products_ref, out_ref):
    filled = jnp.where(iota((HALF, LANES), 1) >= FREE, products_ref[...], mine_ref[...] + other_ref[...])
    out_ref[...] = jnp.broadcast_to(filled[None], out_ref.shape)


def total_kernel(got_ref, out_ref):
    out_ref[...] = jnp.sum(got_ref[...], axis=0)


def spread_kernel(got_ref, out_ref):
    total = jnp.sum(got_ref[...], axis=0)
    out_ref[...] = jnp.broadcast_to(total[None], out_ref.shape)


def unfold(packed):
    lane, sub = iota((FOLD, LANES), 1), iota((FOLD, LANES), 0)
    square = jnp.concatenate([packed, jnp.zeros((LANES - FOLD, LANES), F32)], axis=0)
    turned = square.T
    top = jnp.where(lane >= sub, packed, turned[:FOLD, :])
    lower = packed[8:FOLD, :]
    upper = pltpu.roll(turned[: FOLD - 8, :], LANES - 8, 1)
    lane2, sub2 = iota((FOLD - 8, LANES), 1), iota((FOLD - 8, LANES), 0)
    corner = pltpu.roll(jnp.where(lane2 <= sub2, lower, upper), FOLD, 1)
    bottom = jnp.where(lane2 < FOLD, turned[FOLD:104, :], corner)
    return [top[8 * g : 8 * g + 8] for g in range(FOLD // 8)] + [
        bottom[8 * g : 8 * g + 8] for g in range(GROUPS - FOLD // 8)
    ]


def with_products(groups, sums):
    lane, sub = iota((8, LANES), 1), iota((8, LANES), 0)
    lane1 = iota((1, LANES), 1)
    groups = list(groups)
    columns = [[], []]
    for g in range(GROUPS):
        for kind in range(2):
            rows, at = place(g, kind)
            columns[kind].append(sums[rows, at : at + 1])
            groups[g] = jnp.where(lane == NEW + kind, columns[kind][g], groups[g])
    square, mixed = sums[0:1, SCALARS : SCALARS + 1], sums[1:2, SCALARS : SCALARS + 1]
    by_column = jnp.where(lane1 == NEW, square, jnp.where(lane1 == RES, mixed, columns_to_row(columns[0])))
    by_residual = jnp.where(lane1 == NEW, mixed, columns_to_row(columns[1]))
    at = NEW - 8 * (GROUPS - 1)
    groups[-1] = jnp.where(sub == at, by_column, jnp.where(sub == at + 1, by_residual, groups[-1]))
    return groups


def eliminate(groups):
    lane, sub = iota((8, LANES), 1), iota((8, LANES), 0)
    whole = lambda v: jnp.broadcast_to(v, (8, LANES))
    groups = list(groups)
    pivots = [jnp.ones((8, LANES), F32) for _ in range(GROUPS)]
    for g in range(GROUPS):
        first, count = 8 * g, min(8, RES - 8 * g)
        inside = (lane >= first) & (lane < first + count)
        columns = [[whole(group[:, first + j : first + j + 1]) for j in range(count)] for group in groups[g:]]
        left = [[whole(columns[0][j][i : i + 1, :]) for j in range(i + 1)] for i in range(count)]
        low = [[None] * count for _ in range(count)]
        inverse, rows = [], []
        for j in range(count):
            for i in range(j, count):
                for m in range(j):
                    left[i][j] = left[i][j] - low[i][m] * left[j][m]
            inverse.append(1.0 / left[j][j])
            for i in range(j + 1, count):
                low[i][j] = left[i][j] * inverse[j]
        for j in range(count):
            row = jnp.where(inside, jnp.where(lane == first + j, 1.0, 0.0), whole(groups[g][j : j + 1, :]))
            for m in range(j):
                row = row - low[j][m] * rows[m]
            rows.append(row)
            pivots[g] = jnp.where(sub == j, left[j][j], pivots[g])
        for h in range(g, GROUPS):
            if h == g and count == 8:
                continue
            new = jnp.where(inside, 0.0, groups[h])
            factors = []
            for j in range(count):
                factor = columns[h - g][j]
                for m in range(j):
                    factor = factor - factors[m] * left[j][m]
                factors.append(factor * inverse[j])
                new = new - factors[j] * rows[j]
            groups[h] = new
        for j in range(count):
            groups[g] = jnp.where(sub == j, rows[j], groups[g])
    return groups, pivots


def update(current, coefficients, hist_ref, halo, width):
    wide = [jnp.broadcast_to(c, (8, LANES)) for c in coefficients]
    pieces = []
    for start in range(0, width + LANES, LANES):
        total = jnp.zeros((8, LANES), F32)
        for g in range(GROUPS - 1):
            if start < width:
                part = hist_ref[8 * g : 8 * g + 8, start : start + LANES]
            else:
                part = halo[8 * g : 8 * g + 8, :]
            total = total + wide[g] * part
        if start < width:
            last = hist_ref[96:100, start : start + LANES]
        else:
            last = halo[96:100, :]
        pieces.append(
            jnp.sum(total, axis=0, keepdims=True)
            + jnp.sum(wide[GROUPS - 1][:4] * last, axis=0, keepdims=True)
        )
    return current + jnp.concatenate(pieces, axis=1)


def history_products(hist_ref, column, width):
    totals = [jnp.zeros((8, LANES), F32) for _ in range(GROUPS - 1)]
    last = jnp.zeros((4, LANES), F32)
    for start in range(0, width, LANES):
        part = column[:, start : start + LANES]
        wide = jnp.broadcast_to(part, (8, LANES))
        for g in range(GROUPS - 1):
            totals[g] = totals[g] + hist_ref[8 * g : 8 * g + 8, start : start + LANES] * wide
        last = last + hist_ref[96:100, start : start + LANES] * wide[:4]
    totals.append(jnp.concatenate([last, jnp.zeros((4, LANES), F32)], axis=0))
    return [jnp.sum(t, axis=1, keepdims=True) for t in totals]


def dot_rows(a, b):
    return jnp.sum(a * b, axis=1, keepdims=True)


def coefficient_of(row, at):
    return jnp.sum(jnp.where(iota((1, LANES), 1) == at, row, 0.0), axis=1, keepdims=True)


def send_row(out_ref, hist_ref, columns, column, residual, width):
    row = columns_to_row(history_products(hist_ref, column, width))
    lane = iota((1, LANES), 1)
    for at, other in enumerate((*columns, column, residual)):
        row = jnp.where(lane == HIST + at, dot_rows(other, column), row)
    out_ref[...] = jnp.broadcast_to(row, out_ref.shape)


def first_kernel(
    mine_ref, other_ref, hist_ref, hist_w_ref, state_ref, vectors_ref, halo_ref,
    row_ref, next_ref, factor_ref,
):
    width = hist_ref.shape[1]
    mine, other = mine_ref[...], other_ref[...]
    is_low = first_core()
    low, high = jnp.where(is_low, mine, other), jnp.where(is_low, other, mine)
    packed = jnp.concatenate([low, high[: FOLD - HALF]], axis=0)
    whole = unfold(jnp.where(iota((FOLD, LANES), 1) < FREE, packed, 0.0))
    whole = with_products(whole, mine + other)
    products = whole[RES // 8][RES % 8 : RES % 8 + 1, :]
    groups, pivots = eliminate(whole)
    coeffs = groups[RES // 8][RES % 8 : RES % 8 + 1, :]
    lane1 = iota((1, LANES), 1)
    coeffs = jnp.where(lane1 < RES, coeffs, 0.0)
    lane, sub = iota((8, LANES), 1), iota((8, LANES), 0)
    for g, group in enumerate(groups):
        row = sub + 8 * g
        scale = lax.rsqrt(pivots[g])
        unit = jnp.where(lane < row, group, jnp.where(lane == row, 1.0, 0.0))
        factor_ref[8 * g : 8 * g + 8, :] = jnp.where(row < RES, unit * scale, 0.0)
    factor_ref[104:112, :] = jnp.broadcast_to(jnp.where(lane1 < RES, products, 0.0), (8, LANES))

    halo = halo_ref[...]
    forcing = extended(vectors_ref[3:4, :], halo[101:102])
    stiffness = extended(vectors_ref[4:5, :], halo[102:103])
    inside = inside_mask(width, halo[102:103])
    estimate = state_ref[0:1, :]
    residual = state_ref[1:2, :]
    moved = estimate - extended(vectors_ref[2:3, :], halo[103:104])
    column = state_ref[2:3, :width]
    current = update(estimate, row_to_columns(coeffs), hist_w_ref, halo, width)
    current = current + coefficient_of(coeffs, NEW) * moved
    estimate2 = solver_map(current, forcing, stiffness, inside)
    residual2 = estimate2 - current
    column2 = residual2[:, :width] - residual[:, :width]
    next_ref[0:1, :] = estimate2
    next_ref[1:2, :] = residual2
    next_ref[2:3, :width] = column
    next_ref[3:4, :width] = column2
    next_ref[4:5, :] = moved
    next_ref[5:6, :] = estimate2 - estimate
    send_row(row_ref, hist_ref, (column,), column2, residual2[:, :width], width)


def bordered(factor_ref, products, sent, count, extra):
    lane = iota((1, LANES), 1)
    cross = jnp.where(lane < count, sent, 0.0)
    square = coefficient_of(sent, count)
    with_residual = coefficient_of(sent, count + 1)
    products = jnp.where(lane == count, with_residual, jnp.where(lane < count, products + cross, 0.0))

    def solve(row):
        total = jnp.zeros((8, LANES), F32)
        norm = jnp.zeros((8, 1), F32)
        for g in range(GROUPS):
            block = factor_ref[8 * g : 8 * g + 8, :]
            y = jnp.sum(block * row, axis=1, keepdims=True)
            total = total + y * block
            norm = norm + y * y
        out, length = jnp.sum(total, axis=0, keepdims=True), jnp.sum(norm, axis=0, keepdims=True)
        for line in extra:
            y = dot_rows(line, row)
            out, length = out + y * line, length + y * y
        return out, length

    applied, length = solve(cross)
    scale = lax.rsqrt(square - length)
    line = jnp.where(lane == count, 1.0, -applied) * scale
    coeffs, _ = solve(products)
    coeffs = -(coeffs + dot_rows(line, products) * line)
    return coeffs, line, products


def second_kernel(
    got_ref, hist_ref, hist_w_ref, factor_ref, state_ref, vectors_ref, halo_ref,
    row_ref, next_ref, lines_ref,
):
    width = hist_ref.shape[1]
    sent = jnp.sum(got_ref[...], axis=0, keepdims=True)
    coeffs, line, products = bordered(factor_ref, factor_ref[104:105, :], sent, RES, ())
    lines_ref[0:1, :] = line
    lines_ref[1:2, :] = products
    halo = halo_ref[...]
    forcing = extended(vectors_ref[3:4, :], halo[101:102])
    stiffness = extended(vectors_ref[4:5, :], halo[102:103])
    inside = inside_mask(width, halo[102:103])
    estimate = state_ref[0:1, :]
    residual = state_ref[1:2, :]
    moved, moved2 = state_ref[4:5, :], state_ref[5:6, :]
    column, column2 = state_ref[2:3, :width], state_ref[3:4, :width]
    current = update(estimate, row_to_columns(coeffs), hist_w_ref, halo, width)
    current = current + coefficient_of(coeffs, NEW) * moved + coefficient_of(coeffs, NEW + 1) * moved2
    estimate3 = solver_map(current, forcing, stiffness, inside)
    residual3 = estimate3 - current
    column3 = residual3[:, :width] - residual[:, :width]
    next_ref[0:1, :] = estimate3
    next_ref[1:2, :] = residual3
    next_ref[4:5, :] = moved
    next_ref[5:6, :] = moved2
    next_ref[6:7, :] = estimate3 - estimate
    send_row(row_ref, hist_ref, (column, column2), column3, residual3[:, :width], width)


def third_kernel(
    got_ref, hist_w_ref, factor_ref, lines_ref, state_ref, current_ref, residual_ref,
):
    width = hist_w_ref.shape[1]
    sent = jnp.sum(got_ref[...], axis=0, keepdims=True)
    coeffs, _, _ = bordered(factor_ref, lines_ref[1:2, :], sent, RES + 1, (lines_ref[0:1, :],))
    estimate = state_ref[0:1, :]
    halo = jnp.zeros((104, LANES), F32)
    current = update(estimate, row_to_columns(coeffs), hist_w_ref, halo, width)
    for at in range(ITERS):
        current = current + coefficient_of(coeffs, NEW + at) * state_ref[4 + at : 5 + at, :]
    current_ref[...] = current[:, :width]
    residual_ref[...] = state_ref[1:2, :width]


def call(kernel, outs, scratch=(), held=0, inputs=0, copies=0, flops=0):
    extra = {}
    if inputs:
        extra["in_specs"] = [VMEM] * held + [pl.BlockSpec(memory_space=pltpu.HBM)] * inputs
    return pl.pallas_call(
        kernel,
        out_shape=[jax.ShapeDtypeStruct(s, F32) for s in outs],
        out_specs=[VMEM] * len(outs),
        scratch_shapes=[*scratch, *([pltpu.SemaphoreType.DMA((copies,))] if copies else [])],
        cost_estimate=pl.CostEstimate(flops=flops, bytes_accessed=2**22, transcendentals=0) if flops else None,
        compiler_params=pltpu.CompilerParams(vmem_limit_bytes=12 * 2**20),
        **extra,
    )


def in_hbm(value):
    return pltpu.with_memory_space_constraint(value, pltpu.HBM)


def everywhere(blocks, axes):
    return lax.all_to_all(blocks, axes, 0, 0)


def spread_rows(rows):
    count = rows.shape[0]
    return everywhere(rows.reshape(count, 1, LANES), AXES).reshape(count, LANES)


def shards(interface, previous_residual, previous_estimate, forcing, stiffness, hist_v, hist_w):
    width = interface.shape[0]
    count = lax.axis_size(AXES)
    plane, depth = lax.axis_size(("y", "x")), lax.axis_size("z")
    row = lambda v: in_hbm(v.reshape(1, width))
    hist = pltpu.with_memory_space_constraint(hist_v, pltpu.VMEM)
    held_w = pltpu.with_memory_space_constraint(hist_w, pltpu.VMEM)
    current, residual, estimate = row(interface), row(previous_residual), row(previous_estimate)
    forcing, stiffness = row(forcing), row(stiffness)
    edge, state_shape = (104, LANES), (8, width + LANES)

    turned, block = (8, LANES), pltpu.VMEM((LANES, LANES), F32)
    near, beyond = call(edge_kernel, [turned, turned], [block, block], inputs=5, copies=10)(
        in_hbm(hist_w), current, forcing, stiffness, estimate
    )
    near = lax.ppermute(near, AXES, [(i, i ^ 1) for i in range(count)])
    steps = [(i, i + 1) for i in range(1, count - 1, 2)]
    beyond = lax.ppermute(beyond, AXES, steps + [(j, i) for i, j in steps])
    half = (HALF, LANES)
    vectors, mine, other, products = call(
        gram_kernel,
        [(8, width), half, half, half],
        [pltpu.VMEM((2 * LANES, width), jnp.bfloat16), pltpu.VMEM((2 * HALF, LANES), F32)],
        held=1,
        inputs=5,
        copies=5,
        flops=2**30,
    )(hist, current, residual, estimate, forcing, stiffness)
    swap = lambda v: lax.ppermute(v, "core", [(i, i ^ 1) for i in range(lax.axis_size("core"))])
    products, state, halo = call(column_kernel, [half, state_shape, edge], flops=2**29)(
        products, hist, vectors, near, beyond
    )
    (copies,) = call(pair_kernel, [(plane, *half)])(mine, swap(other), products)
    (copies,) = call(spread_kernel, [(depth, *half)])(everywhere(copies, ("y", "x")))
    (mine,) = call(total_kernel, [half])(everywhere(copies, "z"))
    sent, state, factor = call(first_kernel, [(count, LANES), state_shape, (112, LANES)])(
        mine, swap(mine), hist, held_w, state, vectors, halo
    )
    sent, state, lines = call(second_kernel, [(count, LANES), state_shape, (8, LANES)])(
        spread_rows(sent), hist, held_w, factor, state, vectors, halo
    )
    current, residual = call(third_kernel, [(1, width), (1, width)])(
        spread_rows(sent), held_w, factor, lines, state
    )
    return current.reshape(width), residual.reshape(width)


def solution(mesh):
    devices = mesh.devices.reshape(4, 8, 2, 4) if mesh.devices.size == 256 else mesh.devices.reshape(2, 2, 2, -1)
    finer = Mesh(devices, AXES)
    whole, columns = P(AXES), P(None, AXES)
    return jax.shard_map(
        shards,
        mesh=finer,
        in_specs=(whole,) * 5 + (columns,) * 2,
        out_specs=(whole, whole),
        check_vma=False,
    )
```

```python
import functools

import jax
import jax.numpy as jnp
from jax import lax
from jax.experimental import pallas as pl
from jax.experimental.pallas import tpu as pltpu
from jax.sharding import Mesh
from jax.sharding import PartitionSpec as P

ITERS = 3
AXES = ("y", "z", "core", "x")
COUPLING = 0.25
LANES = 128
HIST = 100
NEW = HIST
RES = HIST + 1
FOLD = 56
HALF = 32
FREE = 104
SCALARS = FREE + 8
GROUPS = 13

F32 = jnp.float32
VMEM = pl.BlockSpec(memory_space=pltpu.VMEM)


def iota(shape, axis):
    return lax.broadcasted_iota(jnp.int32, shape, axis)


def rows_of(group):
    return slice(8 * group, min(8 * group + 8, HIST))


def row_to_columns(row):
    lane, sub = iota((8, LANES), 1), iota((8, LANES), 0)
    full = jnp.broadcast_to(row, (8, LANES))
    return [
        jnp.sum(jnp.where(lane == sub + 8 * g, full, 0.0), axis=1, keepdims=True)
        for g in range(GROUPS)
    ]


def columns_to_row(columns):
    lane, sub = iota((8, LANES), 1), iota((8, LANES), 0)
    total = jnp.zeros((8, LANES), F32)
    for g, column in enumerate(columns):
        total = total + jnp.where(lane == sub + 8 * g, jnp.broadcast_to(column, (8, LANES)), 0.0)
    return jnp.sum(total, axis=0, keepdims=True)


def solver_map(current, forcing, stiffness, inside):
    width = current.shape[1]
    neighbours = pltpu.roll(current, 1, 1) + pltpu.roll(current, width - 1, 1)
    estimate = forcing + stiffness * jnp.tanh(current) + COUPLING * neighbours
    return jnp.where(inside, estimate, 0.0)


def even_place():
    return lax.rem(lax.axis_index("x"), 2) == 0


def halo_of(near_ref, beyond_ref):
    even = jnp.full((8, LANES), jnp.where(even_place(), 1, 0), jnp.int32) == 1
    near, beyond = near_ref[...], beyond_ref[...]
    right, left = jnp.where(even, near, beyond), jnp.where(even, beyond, near)
    return jnp.concatenate([right, jnp.zeros((LANES - 16, LANES), F32), left], axis=0).T[:104]


def extended(row, halo):
    return jnp.concatenate([row, halo], axis=1)


def inside_mask(width, stiffness_halo):
    ones = jnp.ones((1, width), F32)
    return extended(ones, jnp.where(stiffness_halo != 0.0, 1.0, 0.0)) > 0.5


def copy_all(pairs, sems):
    copies = [pltpu.make_async_copy(src, dst, sems.at[i]) for i, (src, dst) in enumerate(pairs)]
    for copy in copies:
        copy.start()
    return copies


def edge_kernel(
    hist_ref, current_ref, forcing_ref, stiffness_ref, old_est_ref,
    near_ref, beyond_ref, first_ref, last_ref, sems,
):
    width = hist_ref.shape[1]
    pairs = []
    for block_ref, at in ((first_ref, 0), (last_ref, width - LANES)):
        columns = slice(at, at + LANES)
        pairs.append((hist_ref.at[:, columns], block_ref.at[:HIST, :]))
        for i, ref in enumerate((current_ref, forcing_ref, stiffness_ref, old_est_ref)):
            pairs.append((ref.at[:, columns], block_ref.at[HIST + i : HIST + i + 1, :]))
    copies = copy_all(pairs, sems)
    for block_ref in (first_ref, last_ref):
        block_ref[104:, :] = jnp.zeros((LANES - 104, LANES), F32)
    for copy in copies:
        copy.wait()
    even = jnp.full((8, LANES), jnp.where(even_place(), 1, 0), jnp.int32) == 1
    first, last = first_ref[...].T[:8], last_ref[...].T[LANES - 8 :]
    near_ref[...] = jnp.where(even, last, first)
    beyond_ref[...] = jnp.where(even, first, last)


def first_core():
    return jnp.full((HALF, LANES), lax.axis_index("core"), jnp.int32) == 0


def place(g, kind):
    at = 8 * (g % (HALF // 8))
    return slice(at, at + 8), FREE + 4 * kind + g // (HALF // 8)


def gram_kernel(
    hist_ref, current_ref, old_res_ref, old_est_ref, forcing_ref, stiffness_ref,
    vectors_ref, mine_ref, other_ref, products_ref, parts_ref, packed_ref, sems,
):
    width = hist_ref.shape[1]
    vectors = (current_ref, old_res_ref, old_est_ref, forcing_ref, stiffness_ref)
    copies = copy_all([(ref, vectors_ref.at[i : i + 1, :]) for i, ref in enumerate(vectors)], sems)

    def put(row, values):
        high = values.astype(jnp.bfloat16)
        parts_ref[row : row + values.shape[0], :] = high
        parts_ref[LANES + row : LANES + row + values.shape[0], :] = (
            values - high.astype(F32)
        ).astype(jnp.bfloat16)

    put(112, jnp.zeros((16, width), F32))
    for start in range(0, 96, 16):
        put(start, hist_ref[start : start + 16, :])
    put(96, jnp.concatenate([hist_ref[96:100, :], jnp.zeros((12, width), F32)], axis=0))
    products = lax.dot_general(
        parts_ref[...],
        parts_ref[...],
        (((1,), (1,)), ((), ())),
        preferred_element_type=F32,
    )
    cross = products[:104, LANES:] + products[LANES : LANES + 104, :LANES]
    gram = products[:104, :LANES] + (cross + products[LANES : LANES + 104, LANES:])
    lane, sub = iota((8, LANES), 1), iota((8, LANES), 0)
    packed_ref[:8, :] = gram[:8]
    for g in range(1, FOLD // 8):
        corner = pltpu.roll(gram[FOLD + 8 * g - 8 : FOLD + 8 * g], LANES - FOLD, 1)
        packed_ref[8 * g : 8 * g + 8, :] = jnp.where(
            lane <= sub + 8 * (g - 1), corner, gram[8 * g : 8 * g + 8]
        )
    packed_ref[FOLD:, :] = jnp.zeros((2 * HALF - FOLD, LANES), F32)
    low, high = packed_ref[:HALF, :], packed_ref[HALF:, :]
    is_low = first_core()
    mine_ref[...] = jnp.where(is_low, low, high)
    other_ref[...] = jnp.where(is_low, high, low)

    for copy in copies:
        copy.wait()
    nothing = jnp.zeros((1, LANES), F32)
    wide = [extended(vectors_ref[i : i + 1, :], nothing) for i in (0, 3, 4)]
    residual = (solver_map(*wide, iota((1, width + LANES), 1) < width) - wide[0])[:, :width]
    column = residual - vectors_ref[1:2, :]
    blocks = [jnp.zeros((8, LANES), F32) for _ in range(HALF // 8)]
    for kind, row in enumerate((column, residual)):
        for g, part in enumerate(history_products(hist_ref, row, width)):
            at = g % (HALF // 8)
            blocks[at] = jnp.where(lane == place(g, kind)[1], part, blocks[at])
    for at, block in enumerate(blocks):
        products_ref[8 * at : 8 * at + 8, :] = block


def column_kernel(
    products_ref, hist_ref, vectors_ref, near_ref, beyond_ref, out_ref, state_ref, halo_ref
):
    width = hist_ref.shape[1]
    halo = halo_of(near_ref, beyond_ref)
    halo_ref[...] = halo
    current = extended(vectors_ref[0:1, :], halo[100:101])
    estimate = solver_map(
        current,
        extended(vectors_ref[3:4, :], halo[101:102]),
        extended(vectors_ref[4:5, :], halo[102:103]),
        inside_mask(width, halo[102:103]),
    )
    residual = estimate - current
    column = residual[:, :width] - vectors_ref[1:2, :]
    state_ref[0:1, :] = estimate
    state_ref[1:2, :] = residual
    state_ref[2:3, :width] = column
    residual = residual[:, :width]
    before = COUPLING * coefficient_of(halo[100:101], LANES - 1)
    after = COUPLING * coefficient_of(halo[100:101], 0)
    lane, sub = iota((8, LANES), 1), iota((8, LANES), 0)
    blocks = [products_ref[8 * at : 8 * at + 8, :] for at in range(HALF // 8)]
    for g in range(GROUPS):
        rows = rows_of(g)
        edge = before * hist_ref[rows, :LANES][:, :1] + after * hist_ref[rows, width - LANES :][:, LANES - 1 :]
        if edge.shape[0] < 8:
            edge = jnp.concatenate([edge, jnp.zeros((8 - edge.shape[0], 1), F32)], axis=0)
        at = g % (HALF // 8)
        mask = (lane == place(g, 0)[1]) | (lane == place(g, 1)[1])
        blocks[at] = blocks[at] + jnp.where(mask, edge, 0.0)
    square, mixed = dot_rows(column, column), dot_rows(column, residual)
    blocks[0] = jnp.where(lane == SCALARS, jnp.where(sub == 0, square, jnp.where(sub == 1, mixed, 0.0)), blocks[0])
    for at, block in enumerate(blocks):
        out_ref[8 * at : 8 * at + 8, :] = block


def pair_kernel(mine_ref, other_ref, products_ref, out_ref):
    filled = jnp.where(iota((HALF, LANES), 1) >= FREE, products_ref[...], mine_ref[...] + other_ref[...])
    out_ref[...] = jnp.broadcast_to(filled[None], out_ref.shape)


def total_kernel(got_ref, out_ref):
    out_ref[...] = jnp.sum(got_ref[...], axis=0)


def spread_kernel(got_ref, out_ref):
    total = jnp.sum(got_ref[...], axis=0)
    out_ref[...] = jnp.broadcast_to(total[None], out_ref.shape)


def unfold(packed):
    lane, sub = iota((FOLD, LANES), 1), iota((FOLD, LANES), 0)
    square = jnp.concatenate([packed, jnp.zeros((LANES - FOLD, LANES), F32)], axis=0)
    turned = square.T
    top = jnp.where(lane >= sub, packed, turned[:FOLD, :])
    lower = packed[8:FOLD, :]
    upper = pltpu.roll(turned[: FOLD - 8, :], LANES - 8, 1)
    lane2, sub2 = iota((FOLD - 8, LANES), 1), iota((FOLD - 8, LANES), 0)
    corner = pltpu.roll(jnp.where(lane2 <= sub2, lower, upper), FOLD, 1)
    bottom = jnp.where(lane2 < FOLD, turned[FOLD:104, :], corner)
    return [top[8 * g : 8 * g + 8] for g in range(FOLD // 8)] + [
        bottom[8 * g : 8 * g + 8] for g in range(GROUPS - FOLD // 8)
    ]


def with_products(groups, sums):
    lane, sub = iota((8, LANES), 1), iota((8, LANES), 0)
    lane1 = iota((1, LANES), 1)
    groups = list(groups)
    columns = [[], []]
    for g in range(GROUPS):
        for kind in range(2):
            rows, at = place(g, kind)
            columns[kind].append(sums[rows, at : at + 1])
            groups[g] = jnp.where(lane == NEW + kind, columns[kind][g], groups[g])
    square, mixed = sums[0:1, SCALARS : SCALARS + 1], sums[1:2, SCALARS : SCALARS + 1]
    by_column = jnp.where(lane1 == NEW, square, jnp.where(lane1 == RES, mixed, columns_to_row(columns[0])))
    by_residual = jnp.where(lane1 == NEW, mixed, columns_to_row(columns[1]))
    at = NEW - 8 * (GROUPS - 1)
    groups[-1] = jnp.where(sub == at, by_column, jnp.where(sub == at + 1, by_residual, groups[-1]))
    return groups


def eliminate(groups):
    lane, sub = iota((8, LANES), 1), iota((8, LANES), 0)
    whole = lambda v: jnp.broadcast_to(v, (8, LANES))
    groups = list(groups)
    pivots = [jnp.ones((8, LANES), F32) for _ in range(GROUPS)]
    for g in range(GROUPS):
        first, count = 8 * g, min(8, RES - 8 * g)
        inside = (lane >= first) & (lane < first + count)
        columns = [[whole(group[:, first + j : first + j + 1]) for j in range(count)] for group in groups[g:]]
        left = [[whole(columns[0][j][i : i + 1, :]) for j in range(i + 1)] for i in range(count)]
        low = [[None] * count for _ in range(count)]
        inverse, rows = [], []
        for j in range(count):
            for i in range(j, count):
                for m in range(j):
                    left[i][j] = left[i][j] - low[i][m] * left[j][m]
            inverse.append(1.0 / left[j][j])
            for i in range(j + 1, count):
                low[i][j] = left[i][j] * inverse[j]
        for j in range(count):
            row = jnp.where(inside, jnp.where(lane == first + j, 1.0, 0.0), whole(groups[g][j : j + 1, :]))
            for m in range(j):
                row = row - low[j][m] * rows[m]
            rows.append(row)
            pivots[g] = jnp.where(sub == j, left[j][j], pivots[g])
        for h in range(g, GROUPS):
            if h == g and count == 8:
                continue
            new = jnp.where(inside, 0.0, groups[h])
            factors = []
            for j in range(count):
                factor = columns[h - g][j]
                for m in range(j):
                    factor = factor - factors[m] * left[j][m]
                factors.append(factor * inverse[j])
                new = new - factors[j] * rows[j]
            groups[h] = new
        for j in range(count):
            groups[g] = jnp.where(sub == j, rows[j], groups[g])
    return groups, pivots


def update(current, coefficients, hist_ref, halo, width):
    wide = [jnp.broadcast_to(c, (8, LANES)) for c in coefficients]
    pieces = []
    for start in range(0, width + LANES, LANES):
        total = jnp.zeros((8, LANES), F32)
        for g in range(GROUPS - 1):
            if start < width:
                part = hist_ref[8 * g : 8 * g + 8, start : start + LANES]
            else:
                part = halo[8 * g : 8 * g + 8, :]
            total = total + wide[g] * part
        if start < width:
            last = hist_ref[96:100, start : start + LANES]
        else:
            last = halo[96:100, :]
        pieces.append(
            jnp.sum(total, axis=0, keepdims=True)
            + jnp.sum(wide[GROUPS - 1][:4] * last, axis=0, keepdims=True)
        )
    return current + jnp.concatenate(pieces, axis=1)


def history_products(hist_ref, column, width):
    totals = [jnp.zeros((8, LANES), F32) for _ in range(GROUPS - 1)]
    last = jnp.zeros((4, LANES), F32)
    for start in range(0, width, LANES):
        part = column[:, start : start + LANES]
        wide = jnp.broadcast_to(part, (8, LANES))
        for g in range(GROUPS - 1):
            totals[g] = totals[g] + hist_ref[8 * g : 8 * g + 8, start : start + LANES] * wide
        last = last + hist_ref[96:100, start : start + LANES] * wide[:4]
    totals.append(jnp.concatenate([last, jnp.zeros((4, LANES), F32)], axis=0))
    return [jnp.sum(t, axis=1, keepdims=True) for t in totals]


def dot_rows(a, b):
    return jnp.sum(a * b, axis=1, keepdims=True)


def coefficient_of(row, at):
    return jnp.sum(jnp.where(iota((1, LANES), 1) == at, row, 0.0), axis=1, keepdims=True)


def send_row(out_ref, hist_ref, columns, column, residual, width):
    row = columns_to_row(history_products(hist_ref, column, width))
    lane = iota((1, LANES), 1)
    for at, other in enumerate((*columns, column, residual)):
        row = jnp.where(lane == HIST + at, dot_rows(other, column), row)
    out_ref[...] = jnp.broadcast_to(row, out_ref.shape)


def first_kernel(
    mine_ref, other_ref, hist_ref, hist_w_ref, state_ref, vectors_ref, halo_ref,
    row_ref, next_ref, factor_ref,
):
    width = hist_ref.shape[1]
    mine, other = mine_ref[...], other_ref[...]
    is_low = first_core()
    low, high = jnp.where(is_low, mine, other), jnp.where(is_low, other, mine)
    packed = jnp.concatenate([low, high[: FOLD - HALF]], axis=0)
    whole = unfold(jnp.where(iota((FOLD, LANES), 1) < FREE, packed, 0.0))
    whole = with_products(whole, mine + other)
    products = whole[RES // 8][RES % 8 : RES % 8 + 1, :]
    groups, pivots = eliminate(whole)
    coeffs = groups[RES // 8][RES % 8 : RES % 8 + 1, :]
    lane1 = iota((1, LANES), 1)
    coeffs = jnp.where(lane1 < RES, coeffs, 0.0)
    lane, sub = iota((8, LANES), 1), iota((8, LANES), 0)
    for g, group in enumerate(groups):
        row = sub + 8 * g
        scale = lax.rsqrt(pivots[g])
        unit = jnp.where(lane < row, group, jnp.where(lane == row, 1.0, 0.0))
        factor_ref[8 * g : 8 * g + 8, :] = jnp.where(row < RES, unit * scale, 0.0)
    factor_ref[104:112, :] = jnp.broadcast_to(jnp.where(lane1 < RES, products, 0.0), (8, LANES))

    halo = halo_ref[...]
    forcing = extended(vectors_ref[3:4, :], halo[101:102])
    stiffness = extended(vectors_ref[4:5, :], halo[102:103])
    inside = inside_mask(width, halo[102:103])
    estimate = state_ref[0:1, :]
    residual = state_ref[1:2, :]
    moved = estimate - extended(vectors_ref[2:3, :], halo[103:104])
    column = state_ref[2:3, :width]
    current = update(estimate, row_to_columns(coeffs), hist_w_ref, halo, width)
    current = current + coefficient_of(coeffs, NEW) * moved
    estimate2 = solver_map(current, forcing, stiffness, inside)
    residual2 = estimate2 - current
    column2 = residual2[:, :width] - residual[:, :width]
    next_ref[0:1, :] = estimate2
    next_ref[1:2, :] = residual2
    next_ref[2:3, :width] = column
    next_ref[3:4, :width] = column2
    next_ref[4:5, :] = moved
    next_ref[5:6, :] = estimate2 - estimate
    send_row(row_ref, hist_ref, (column,), column2, residual2[:, :width], width)


def bordered(factor_ref, products, sent, count, extra):
    lane = iota((1, LANES), 1)
    cross = jnp.where(lane < count, sent, 0.0)
    square = coefficient_of(sent, count)
    with_residual = coefficient_of(sent, count + 1)
    products = jnp.where(lane == count, with_residual, jnp.where(lane < count, products + cross, 0.0))

    def solve(row):
        total = jnp.zeros((8, LANES), F32)
        norm = jnp.zeros((8, 1), F32)
        for g in range(GROUPS):
            block = factor_ref[8 * g : 8 * g + 8, :]
            y = jnp.sum(block * row, axis=1, keepdims=True)
            total = total + y * block
            norm = norm + y * y
        out, length = jnp.sum(total, axis=0, keepdims=True), jnp.sum(norm, axis=0, keepdims=True)
        for line in extra:
            y = dot_rows(line, row)
            out, length = out + y * line, length + y * y
        return out, length

    applied, length = solve(cross)
    scale = lax.rsqrt(square - length)
    line = jnp.where(lane == count, 1.0, -applied) * scale
    coeffs, _ = solve(products)
    coeffs = -(coeffs + dot_rows(line, products) * line)
    return coeffs, line, products


def second_kernel(
    got_ref, hist_ref, hist_w_ref, factor_ref, state_ref, vectors_ref, halo_ref,
    row_ref, next_ref, lines_ref,
):
    width = hist_ref.shape[1]
    sent = jnp.sum(got_ref[...], axis=0, keepdims=True)
    coeffs, line, products = bordered(factor_ref, factor_ref[104:105, :], sent, RES, ())
    lines_ref[0:1, :] = line
    lines_ref[1:2, :] = products
    halo = halo_ref[...]
    forcing = extended(vectors_ref[3:4, :], halo[101:102])
    stiffness = extended(vectors_ref[4:5, :], halo[102:103])
    inside = inside_mask(width, halo[102:103])
    estimate = state_ref[0:1, :]
    residual = state_ref[1:2, :]
    moved, moved2 = state_ref[4:5, :], state_ref[5:6, :]
    column, column2 = state_ref[2:3, :width], state_ref[3:4, :width]
    current = update(estimate, row_to_columns(coeffs), hist_w_ref, halo, width)
    current = current + coefficient_of(coeffs, NEW) * moved + coefficient_of(coeffs, NEW + 1) * moved2
    estimate3 = solver_map(current, forcing, stiffness, inside)
    residual3 = estimate3 - current
    column3 = residual3[:, :width] - residual[:, :width]
    next_ref[0:1, :] = estimate3
    next_ref[1:2, :] = residual3
    next_ref[4:5, :] = moved
    next_ref[5:6, :] = moved2
    next_ref[6:7, :] = estimate3 - estimate
    send_row(row_ref, hist_ref, (column, column2), column3, residual3[:, :width], width)


def third_kernel(
    got_ref, hist_w_ref, factor_ref, lines_ref, state_ref, current_ref, residual_ref,
):
    width = hist_w_ref.shape[1]
    sent = jnp.sum(got_ref[...], axis=0, keepdims=True)
    coeffs, _, _ = bordered(factor_ref, lines_ref[1:2, :], sent, RES + 1, (lines_ref[0:1, :],))
    estimate = state_ref[0:1, :]
    halo = jnp.zeros((104, LANES), F32)
    current = update(estimate, row_to_columns(coeffs), hist_w_ref, halo, width)
    for at in range(ITERS):
        current = current + coefficient_of(coeffs, NEW + at) * state_ref[4 + at : 5 + at, :]
    current_ref[...] = current[:, :width]
    residual_ref[...] = state_ref[1:2, :width]


def call(kernel, outs, scratch=(), held=0, inputs=0, copies=0, flops=0):
    extra = {}
    if inputs:
        extra["in_specs"] = [VMEM] * held + [pl.BlockSpec(memory_space=pltpu.HBM)] * inputs
    return pl.pallas_call(
        kernel,
        out_shape=[jax.ShapeDtypeStruct(s, F32) for s in outs],
        out_specs=[VMEM] * len(outs),
        scratch_shapes=[*scratch, *([pltpu.SemaphoreType.DMA((copies,))] if copies else [])],
        cost_estimate=pl.CostEstimate(flops=flops, bytes_accessed=2**22, transcendentals=0) if flops else None,
        compiler_params=pltpu.CompilerParams(vmem_limit_bytes=12 * 2**20),
        **extra,
    )


def in_hbm(value):
    return pltpu.with_memory_space_constraint(value, pltpu.HBM)


def everywhere(blocks, axes):
    return lax.all_to_all(blocks, axes, 0, 0)


def spread_rows(rows):
    count = rows.shape[0]
    return everywhere(rows.reshape(count, 1, LANES), AXES).reshape(count, LANES)


def shards(interface, previous_residual, previous_estimate, forcing, stiffness, hist_v, hist_w):
    width = interface.shape[0]
    count = lax.axis_size(AXES)
    plane, depth = lax.axis_size(("y", "x")), lax.axis_size("z")
    row = lambda v: in_hbm(v.reshape(1, width))
    hist = pltpu.with_memory_space_constraint(hist_v, pltpu.VMEM)
    held_w = pltpu.with_memory_space_constraint(hist_w, pltpu.VMEM)
    current, residual, estimate = row(interface), row(previous_residual), row(previous_estimate)
    forcing, stiffness = row(forcing), row(stiffness)
    edge, state_shape = (104, LANES), (8, width + LANES)

    turned, block = (8, LANES), pltpu.VMEM((LANES, LANES), F32)
    near, beyond = call(edge_kernel, [turned, turned], [block, block], inputs=5, copies=10)(
        in_hbm(hist_w), current, forcing, stiffness, estimate
    )
    near = lax.ppermute(near, AXES, [(i, i ^ 1) for i in range(count)])
    steps = [(i, i + 1) for i in range(1, count - 1, 2)]
    beyond = lax.ppermute(beyond, AXES, steps + [(j, i) for i, j in steps])
    half = (HALF, LANES)
    vectors, mine, other, products = call(
        gram_kernel,
        [(8, width), half, half, half],
        [pltpu.VMEM((2 * LANES, width), jnp.bfloat16), pltpu.VMEM((2 * HALF, LANES), F32)],
        held=1,
        inputs=5,
        copies=5,
        flops=2**30,
    )(hist, current, residual, estimate, forcing, stiffness)
    swap = lambda v: lax.ppermute(v, "core", [(i, i ^ 1) for i in range(lax.axis_size("core"))])
    products, state, halo = call(column_kernel, [half, state_shape, edge], flops=2**29)(
        products, hist, vectors, near, beyond
    )
    (copies,) = call(pair_kernel, [(plane, *half)])(mine, swap(other), products)
    (copies,) = call(spread_kernel, [(depth, *half)])(everywhere(copies, ("y", "x")))
    (mine,) = call(total_kernel, [half])(everywhere(copies, "z"))
    sent, state, factor = call(first_kernel, [(count, LANES), state_shape, (112, LANES)])(
        mine, swap(mine), hist, held_w, state, vectors, halo
    )
    sent, state, lines = call(second_kernel, [(count, LANES), state_shape, (8, LANES)])(
        spread_rows(sent), hist, held_w, factor, state, vectors, halo
    )
    current, residual = call(third_kernel, [(1, width), (1, width)])(
        spread_rows(sent), held_w, factor, lines, state
    )
    return current.reshape(width), residual.reshape(width)


def solution(mesh):
    devices = mesh.devices.reshape(4, 8, 2, 4) if mesh.devices.size == 256 else mesh.devices.reshape(2, 2, 2, -1)
    finer = Mesh(devices, AXES)
    whole, columns = P(AXES), P(None, AXES)
    return jax.shard_map(
        shards,
        mesh=finer,
        in_specs=(whole,) * 5 + (columns,) * 2,
        out_specs=(whole, whole),
        check_vma=False,
    )
```

```python
import functools

import jax
import jax.numpy as jnp
from jax import lax
from jax.experimental import pallas as pl
from jax.experimental.pallas import tpu as pltpu
from jax.sharding import Mesh
from jax.sharding import PartitionSpec as P

ITERS = 3
AXES = ("y", "z", "core", "x")
COUPLING = 0.25
LANES = 128
HIST = 100
NEW = HIST
RES = HIST + 1
FOLD = 56
HALF = 32
FREE = 104
SCALARS = FREE + 8
GROUPS = 13

F32 = jnp.float32
VMEM = pl.BlockSpec(memory_space=pltpu.VMEM)


def iota(shape, axis):
    return lax.broadcasted_iota(jnp.int32, shape, axis)


def rows_of(group):
    return slice(8 * group, min(8 * group + 8, HIST))


def row_to_columns(row):
    lane, sub = iota((8, LANES), 1), iota((8, LANES), 0)
    full = jnp.broadcast_to(row, (8, LANES))
    return [
        jnp.sum(jnp.where(lane == sub + 8 * g, full, 0.0), axis=1, keepdims=True)
        for g in range(GROUPS)
    ]


def columns_to_row(columns):
    lane, sub = iota((8, LANES), 1), iota((8, LANES), 0)
    total = jnp.zeros((8, LANES), F32)
    for g, column in enumerate(columns):
        total = total + jnp.where(lane == sub + 8 * g, jnp.broadcast_to(column, (8, LANES)), 0.0)
    return jnp.sum(total, axis=0, keepdims=True)


def solver_map(current, forcing, stiffness, inside):
    width = current.shape[1]
    neighbours = pltpu.roll(current, 1, 1) + pltpu.roll(current, width - 1, 1)
    estimate = forcing + stiffness * jnp.tanh(current) + COUPLING * neighbours
    return jnp.where(inside, estimate, 0.0)


def even_place():
    return lax.rem(lax.axis_index("x"), 2) == 0


def halo_of(near_ref, beyond_ref):
    even = jnp.full((8, LANES), jnp.where(even_place(), 1, 0), jnp.int32) == 1
    near, beyond = near_ref[...], beyond_ref[...]
    right, left = jnp.where(even, near, beyond), jnp.where(even, beyond, near)
    return jnp.concatenate([right, jnp.zeros((LANES - 16, LANES), F32), left], axis=0).T[:104]


def extended(row, halo):
    return jnp.concatenate([row, halo], axis=1)


def inside_mask(width, stiffness_halo):
    ones = jnp.ones((1, width), F32)
    return extended(ones, jnp.where(stiffness_halo != 0.0, 1.0, 0.0)) > 0.5


def copy_all(pairs, sems):
    copies = [pltpu.make_async_copy(src, dst, sems.at[i]) for i, (src, dst) in enumerate(pairs)]
    for copy in copies:
        copy.start()
    return copies


def edge_kernel(
    hist_ref, current_ref, forcing_ref, stiffness_ref, old_est_ref,
    near_ref, beyond_ref, first_ref, last_ref, sems,
):
    width = hist_ref.shape[1]
    pairs = []
    for block_ref, at in ((first_ref, 0), (last_ref, width - LANES)):
        columns = slice(at, at + LANES)
        pairs.append((hist_ref.at[:, columns], block_ref.at[:HIST, :]))
        for i, ref in enumerate((current_ref, forcing_ref, stiffness_ref, old_est_ref)):
            pairs.append((ref.at[:, columns], block_ref.at[HIST + i : HIST + i + 1, :]))
    copies = copy_all(pairs, sems)
    for block_ref in (first_ref, last_ref):
        block_ref[104:, :] = jnp.zeros((LANES - 104, LANES), F32)
    for copy in copies:
        copy.wait()
    even = jnp.full((8, LANES), jnp.where(even_place(), 1, 0), jnp.int32) == 1
    first, last = first_ref[...].T[:8], last_ref[...].T[LANES - 8 :]
    near_ref[...] = jnp.where(even, last, first)
    beyond_ref[...] = jnp.where(even, first, last)


def first_core():
    return jnp.full((HALF, LANES), lax.axis_index("core"), jnp.int32) == 0


def place(g, kind):
    at = 8 * (g % (HALF // 8))
    return slice(at, at + 8), FREE + 4 * kind + g // (HALF // 8)


def gram_kernel(
    hist_ref, current_ref, old_res_ref, old_est_ref, forcing_ref, stiffness_ref,
    vectors_ref, mine_ref, other_ref, products_ref, parts_ref, packed_ref, sems,
):
    width = hist_ref.shape[1]
    vectors = (current_ref, old_res_ref, old_est_ref, forcing_ref, stiffness_ref)
    copies = copy_all([(ref, vectors_ref.at[i : i + 1, :]) for i, ref in enumerate(vectors)], sems)

    def put(row, values):
        high = values.astype(jnp.bfloat16)
        parts_ref[row : row + values.shape[0], :] = high
        parts_ref[LANES + row : LANES + row + values.shape[0], :] = (
            values - high.astype(F32)
        ).astype(jnp.bfloat16)

    put(112, jnp.zeros((16, width), F32))
    for start in range(0, 96, 16):
        put(start, hist_ref[start : start + 16, :])
    put(96, jnp.concatenate([hist_ref[96:100, :], jnp.zeros((12, width), F32)], axis=0))
    products = lax.dot_general(
        parts_ref[...],
        parts_ref[...],
        (((1,), (1,)), ((), ())),
        preferred_element_type=F32,
    )
    cross = products[:104, LANES:] + products[LANES : LANES + 104, :LANES]
    gram = products[:104, :LANES] + (cross + products[LANES : LANES + 104, LANES:])
    lane, sub = iota((8, LANES), 1), iota((8, LANES), 0)
    packed_ref[:8, :] = gram[:8]
    for g in range(1, FOLD // 8):
        corner = pltpu.roll(gram[FOLD + 8 * g - 8 : FOLD + 8 * g], LANES - FOLD, 1)
        packed_ref[8 * g : 8 * g + 8, :] = jnp.where(
            lane <= sub + 8 * (g - 1), corner, gram[8 * g : 8 * g + 8]
        )
    packed_ref[FOLD:, :] = jnp.zeros((2 * HALF - FOLD, LANES), F32)
    low, high = packed_ref[:HALF, :], packed_ref[HALF:, :]
    is_low = first_core()
    mine_ref[...] = jnp.where(is_low, low, high)
    other_ref[...] = jnp.where(is_low, high, low)

    for copy in copies:
        copy.wait()
    nothing = jnp.zeros((1, LANES), F32)
    wide = [extended(vectors_ref[i : i + 1, :], nothing) for i in (0, 3, 4)]
    residual = (solver_map(*wide, iota((1, width + LANES), 1) < width) - wide[0])[:, :width]
    column = residual - vectors_ref[1:2, :]
    blocks = [jnp.zeros((8, LANES), F32) for _ in range(HALF // 8)]
    for kind, row in enumerate((column, residual)):
        for g, part in enumerate(history_products(hist_ref, row, width)):
            at = g % (HALF // 8)
            blocks[at] = jnp.where(lane == place(g, kind)[1], part, blocks[at])
    for at, block in enumerate(blocks):
        products_ref[8 * at : 8 * at + 8, :] = block


def column_kernel(
    products_ref, hist_ref, vectors_ref, beyond_ref, near_ref, out_ref, state_ref, halo_ref
):
    width = hist_ref.shape[1]
    halo = halo_of(near_ref, beyond_ref)
    halo_ref[...] = halo
    current = extended(vectors_ref[0:1, :], halo[100:101])
    estimate = solver_map(
        current,
        extended(vectors_ref[3:4, :], halo[101:102]),
        extended(vectors_ref[4:5, :], halo[102:103]),
        inside_mask(width, halo[102:103]),
    )
    residual = estimate - current
    column = residual[:, :width] - vectors_ref[1:2, :]
    state_ref[0:1, :] = estimate
    state_ref[1:2, :] = residual
    state_ref[2:3, :width] = column
    residual = residual[:, :width]
    before = COUPLING * coefficient_of(halo[100:101], LANES - 1)
    after = COUPLING * coefficient_of(halo[100:101], 0)
    lane, sub = iota((8, LANES), 1), iota((8, LANES), 0)
    blocks = [products_ref[8 * at : 8 * at + 8, :] for at in range(HALF // 8)]
    for g in range(GROUPS):
        rows = rows_of(g)
        edge = before * hist_ref[rows, :LANES][:, :1] + after * hist_ref[rows, width - LANES :][:, LANES - 1 :]
        if edge.shape[0] < 8:
            edge = jnp.concatenate([edge, jnp.zeros((8 - edge.shape[0], 1), F32)], axis=0)
        at = g % (HALF // 8)
        mask = (lane == place(g, 0)[1]) | (lane == place(g, 1)[1])
        blocks[at] = blocks[at] + jnp.where(mask, edge, 0.0)
    square, mixed = dot_rows(column, column), dot_rows(column, residual)
    blocks[0] = jnp.where(lane == SCALARS, jnp.where(sub == 0, square, jnp.where(sub == 1, mixed, 0.0)), blocks[0])
    for at, block in enumerate(blocks):
        out_ref[8 * at : 8 * at + 8, :] = block


def pair_kernel(mine_ref, other_ref, products_ref, out_ref):
    filled = jnp.where(iota((HALF, LANES), 1) >= FREE, products_ref[...], mine_ref[...] + other_ref[...])
    out_ref[...] = jnp.broadcast_to(filled[None], out_ref.shape)


def total_kernel(got_ref, out_ref):
    out_ref[...] = jnp.sum(got_ref[...], axis=0)


def spread_kernel(got_ref, out_ref):
    total = jnp.sum(got_ref[...], axis=0)
    out_ref[...] = jnp.broadcast_to(total[None], out_ref.shape)


def unfold(packed):
    lane, sub = iota((FOLD, LANES), 1), iota((FOLD, LANES), 0)
    square = jnp.concatenate([packed, jnp.zeros((LANES - FOLD, LANES), F32)], axis=0)
    turned = square.T
    top = jnp.where(lane >= sub, packed, turned[:FOLD, :])
    lower = packed[8:FOLD, :]
    upper = pltpu.roll(turned[: FOLD - 8, :], LANES - 8, 1)
    lane2, sub2 = iota((FOLD - 8, LANES), 1), iota((FOLD - 8, LANES), 0)
    corner = pltpu.roll(jnp.where(lane2 <= sub2, lower, upper), FOLD, 1)
    bottom = jnp.where(lane2 < FOLD, turned[FOLD:104, :], corner)
    return [top[8 * g : 8 * g + 8] for g in range(FOLD // 8)] + [
        bottom[8 * g : 8 * g + 8] for g in range(GROUPS - FOLD // 8)
    ]


def with_products(groups, sums):
    lane, sub = iota((8, LANES), 1), iota((8, LANES), 0)
    lane1 = iota((1, LANES), 1)
    groups = list(groups)
    columns = [[], []]
    for g in range(GROUPS):
        for kind in range(2):
            rows, at = place(g, kind)
            columns[kind].append(sums[rows, at : at + 1])
            groups[g] = jnp.where(lane == NEW + kind, columns[kind][g], groups[g])
    square, mixed = sums[0:1, SCALARS : SCALARS + 1], sums[1:2, SCALARS : SCALARS + 1]
    by_column = jnp.where(lane1 == NEW, square, jnp.where(lane1 == RES, mixed, columns_to_row(columns[0])))
    by_residual = jnp.where(lane1 == NEW, mixed, columns_to_row(columns[1]))
    at = NEW - 8 * (GROUPS - 1)
    groups[-1] = jnp.where(sub == at, by_column, jnp.where(sub == at + 1, by_residual, groups[-1]))
    return groups


def eliminate(groups):
    lane, sub = iota((8, LANES), 1), iota((8, LANES), 0)
    whole = lambda v: jnp.broadcast_to(v, (8, LANES))
    groups = list(groups)
    pivots = [jnp.ones((8, LANES), F32) for _ in range(GROUPS)]
    for g in range(GROUPS):
        first, count = 8 * g, min(8, RES - 8 * g)
        inside = (lane >= first) & (lane < first + count)
        columns = [[whole(group[:, first + j : first + j + 1]) for j in range(count)] for group in groups[g:]]
        left = [[whole(columns[0][j][i : i + 1, :]) for j in range(i + 1)] for i in range(count)]
        low = [[None] * count for _ in range(count)]
        inverse, rows = [], []
        for j in range(count):
            for i in range(j, count):
                for m in range(j):
                    left[i][j] = left[i][j] - low[i][m] * left[j][m]
            inverse.append(1.0 / left[j][j])
            for i in range(j + 1, count):
                low[i][j] = left[i][j] * inverse[j]
        for j in range(count):
            row = jnp.where(inside, jnp.where(lane == first + j, 1.0, 0.0), whole(groups[g][j : j + 1, :]))
            for m in range(j):
                row = row - low[j][m] * rows[m]
            rows.append(row)
            pivots[g] = jnp.where(sub == j, left[j][j], pivots[g])
        for h in range(g, GROUPS):
            if h == g and count == 8:
                continue
            new = jnp.where(inside, 0.0, groups[h])
            factors = []
            for j in range(count):
                factor = columns[h - g][j]
                for m in range(j):
                    factor = factor - factors[m] * left[j][m]
                factors.append(factor * inverse[j])
                new = new - factors[j] * rows[j]
            groups[h] = new
        for j in range(count):
            groups[g] = jnp.where(sub == j, rows[j], groups[g])
    return groups, pivots


def update(current, coefficients, hist_ref, halo, width):
    wide = [jnp.broadcast_to(c, (8, LANES)) for c in coefficients]
    pieces = []
    for start in range(0, width + LANES, LANES):
        total = jnp.zeros((8, LANES), F32)
        for g in range(GROUPS - 1):
            if start < width:
                part = hist_ref[8 * g : 8 * g + 8, start : start + LANES]
            else:
                part = halo[8 * g : 8 * g + 8, :]
            total = total + wide[g] * part
        if start < width:
            last = hist_ref[96:100, start : start + LANES]
        else:
            last = halo[96:100, :]
        pieces.append(
            jnp.sum(total, axis=0, keepdims=True)
            + jnp.sum(wide[GROUPS - 1][:4] * last, axis=0, keepdims=True)
        )
    return current + jnp.concatenate(pieces, axis=1)


def history_products(hist_ref, column, width):
    totals = [jnp.zeros((8, LANES), F32) for _ in range(GROUPS - 1)]
    last = jnp.zeros((4, LANES), F32)
    for start in range(0, width, LANES):
        part = column[:, start : start + LANES]
        wide = jnp.broadcast_to(part, (8, LANES))
        for g in range(GROUPS - 1):
            totals[g] = totals[g] + hist_ref[8 * g : 8 * g + 8, start : start + LANES] * wide
        last = last + hist_ref[96:100, start : start + LANES] * wide[:4]
    totals.append(jnp.concatenate([last, jnp.zeros((4, LANES), F32)], axis=0))
    return [jnp.sum(t, axis=1, keepdims=True) for t in totals]


def dot_rows(a, b):
    return jnp.sum(a * b, axis=1, keepdims=True)


def coefficient_of(row, at):
    return jnp.sum(jnp.where(iota((1, LANES), 1) == at, row, 0.0), axis=1, keepdims=True)


def send_row(out_ref, hist_ref, columns, column, residual, width):
    row = columns_to_row(history_products(hist_ref, column, width))
    lane = iota((1, LANES), 1)
    for at, other in enumerate((*columns, column, residual)):
        row = jnp.where(lane == HIST + at, dot_rows(other, column), row)
    out_ref[...] = jnp.broadcast_to(row, out_ref.shape)


def first_kernel(
    mine_ref, other_ref, hist_ref, hist_w_ref, state_ref, vectors_ref, halo_ref,
    row_ref, next_ref, factor_ref,
):
    width = hist_ref.shape[1]
    mine, other = mine_ref[...], other_ref[...]
    is_low = first_core()
    low, high = jnp.where(is_low, mine, other), jnp.where(is_low, other, mine)
    packed = jnp.concatenate([low, high[: FOLD - HALF]], axis=0)
    whole = unfold(jnp.where(iota((FOLD, LANES), 1) < FREE, packed, 0.0))
    whole = with_products(whole, mine + other)
    products = whole[RES // 8][RES % 8 : RES % 8 + 1, :]
    groups, pivots = eliminate(whole)
    coeffs = groups[RES // 8][RES % 8 : RES % 8 + 1, :]
    lane1 = iota((1, LANES), 1)
    coeffs = jnp.where(lane1 < RES, coeffs, 0.0)
    lane, sub = iota((8, LANES), 1), iota((8, LANES), 0)
    for g, group in enumerate(groups):
        row = sub + 8 * g
        scale = lax.rsqrt(pivots[g])
        unit = jnp.where(lane < row, group, jnp.where(lane == row, 1.0, 0.0))
        factor_ref[8 * g : 8 * g + 8, :] = jnp.where(row < RES, unit * scale, 0.0)
    factor_ref[104:112, :] = jnp.broadcast_to(jnp.where(lane1 < RES, products, 0.0), (8, LANES))

    halo = halo_ref[...]
    forcing = extended(vectors_ref[3:4, :], halo[101:102])
    stiffness = extended(vectors_ref[4:5, :], halo[102:103])
    inside = inside_mask(width, halo[102:103])
    estimate = state_ref[0:1, :]
    residual = state_ref[1:2, :]
    moved = estimate - extended(vectors_ref[2:3, :], halo[103:104])
    column = state_ref[2:3, :width]
    current = update(estimate, row_to_columns(coeffs), hist_w_ref, halo, width)
    current = current + coefficient_of(coeffs, NEW) * moved
    estimate2 = solver_map(current, forcing, stiffness, inside)
    residual2 = estimate2 - current
    column2 = residual2[:, :width] - residual[:, :width]
    next_ref[0:1, :] = estimate2
    next_ref[1:2, :] = residual2
    next_ref[2:3, :width] = column
    next_ref[3:4, :width] = column2
    next_ref[4:5, :] = moved
    next_ref[5:6, :] = estimate2 - estimate
    send_row(row_ref, hist_ref, (column,), column2, residual2[:, :width], width)


def bordered(factor_ref, products, sent, count, extra):
    lane = iota((1, LANES), 1)
    cross = jnp.where(lane < count, sent, 0.0)
    square = coefficient_of(sent, count)
    with_residual = coefficient_of(sent, count + 1)
    products = jnp.where(lane == count, with_residual, jnp.where(lane < count, products + cross, 0.0))

    def solve(row):
        total = jnp.zeros((8, LANES), F32)
        norm = jnp.zeros((8, 1), F32)
        for g in range(GROUPS):
            block = factor_ref[8 * g : 8 * g + 8, :]
            y = jnp.sum(block * row, axis=1, keepdims=True)
            total = total + y * block
            norm = norm + y * y
        out, length = jnp.sum(total, axis=0, keepdims=True), jnp.sum(norm, axis=0, keepdims=True)
        for line in extra:
            y = dot_rows(line, row)
            out, length = out + y * line, length + y * y
        return out, length

    applied, length = solve(cross)
    scale = lax.rsqrt(square - length)
    line = jnp.where(lane == count, 1.0, -applied) * scale
    coeffs, _ = solve(products)
    coeffs = -(coeffs + dot_rows(line, products) * line)
    return coeffs, line, products


def second_kernel(
    got_ref, hist_ref, hist_w_ref, factor_ref, state_ref, vectors_ref, halo_ref,
    row_ref, next_ref, lines_ref,
):
    width = hist_ref.shape[1]
    sent = jnp.sum(got_ref[...], axis=0, keepdims=True)
    coeffs, line, products = bordered(factor_ref, factor_ref[104:105, :], sent, RES, ())
    lines_ref[0:1, :] = line
    lines_ref[1:2, :] = products
    halo = halo_ref[...]
    forcing = extended(vectors_ref[3:4, :], halo[101:102])
    stiffness = extended(vectors_ref[4:5, :], halo[102:103])
    inside = inside_mask(width, halo[102:103])
    estimate = state_ref[0:1, :]
    residual = state_ref[1:2, :]
    moved, moved2 = state_ref[4:5, :], state_ref[5:6, :]
    column, column2 = state_ref[2:3, :width], state_ref[3:4, :width]
    current = update(estimate, row_to_columns(coeffs), hist_w_ref, halo, width)
    current = current + coefficient_of(coeffs, NEW) * moved + coefficient_of(coeffs, NEW + 1) * moved2
    estimate3 = solver_map(current, forcing, stiffness, inside)
    residual3 = estimate3 - current
    column3 = residual3[:, :width] - residual[:, :width]
    next_ref[0:1, :] = estimate3
    next_ref[1:2, :] = residual3
    next_ref[4:5, :] = moved
    next_ref[5:6, :] = moved2
    next_ref[6:7, :] = estimate3 - estimate
    send_row(row_ref, hist_ref, (column, column2), column3, residual3[:, :width], width)


def third_kernel(
    got_ref, hist_w_ref, factor_ref, lines_ref, state_ref, current_ref, residual_ref,
):
    width = hist_w_ref.shape[1]
    sent = jnp.sum(got_ref[...], axis=0, keepdims=True)
    coeffs, _, _ = bordered(factor_ref, lines_ref[1:2, :], sent, RES + 1, (lines_ref[0:1, :],))
    estimate = state_ref[0:1, :]
    halo = jnp.zeros((104, LANES), F32)
    current = update(estimate, row_to_columns(coeffs), hist_w_ref, halo, width)
    for at in range(ITERS):
        current = current + coefficient_of(coeffs, NEW + at) * state_ref[4 + at : 5 + at, :]
    current_ref[...] = current[:, :width]
    residual_ref[...] = state_ref[1:2, :width]


def call(kernel, outs, scratch=(), held=0, inputs=0, copies=0, flops=0):
    extra = {}
    if inputs:
        extra["in_specs"] = [VMEM] * held + [pl.BlockSpec(memory_space=pltpu.HBM)] * inputs
    return pl.pallas_call(
        kernel,
        out_shape=[jax.ShapeDtypeStruct(s, F32) for s in outs],
        out_specs=[VMEM] * len(outs),
        scratch_shapes=[*scratch, *([pltpu.SemaphoreType.DMA((copies,))] if copies else [])],
        cost_estimate=pl.CostEstimate(flops=flops, bytes_accessed=2**22, transcendentals=0) if flops else None,
        compiler_params=pltpu.CompilerParams(vmem_limit_bytes=12 * 2**20),
        **extra,
    )


def in_hbm(value):
    return pltpu.with_memory_space_constraint(value, pltpu.HBM)


def everywhere(blocks, axes):
    return lax.all_to_all(blocks, axes, 0, 0)


def spread_rows(rows):
    count = rows.shape[0]
    return everywhere(rows.reshape(count, 1, LANES), AXES).reshape(count, LANES)


def shards(interface, previous_residual, previous_estimate, forcing, stiffness, hist_v, hist_w):
    width = interface.shape[0]
    count = lax.axis_size(AXES)
    plane, depth = lax.axis_size(("y", "x")), lax.axis_size("z")
    row = lambda v: in_hbm(v.reshape(1, width))
    hist = pltpu.with_memory_space_constraint(hist_v, pltpu.VMEM)
    held_w = pltpu.with_memory_space_constraint(hist_w, pltpu.VMEM)
    current, residual, estimate = row(interface), row(previous_residual), row(previous_estimate)
    forcing, stiffness = row(forcing), row(stiffness)
    edge, state_shape = (104, LANES), (8, width + LANES)

    turned, block = (8, LANES), pltpu.VMEM((LANES, LANES), F32)
    near, beyond = call(edge_kernel, [turned, turned], [block, block], inputs=5, copies=10)(
        in_hbm(hist_w), current, forcing, stiffness, estimate
    )
    steps = [(i, i + 1) for i in range(1, count - 1, 2)]
    beyond = lax.ppermute(beyond, AXES, steps + [(j, i) for i, j in steps])
    near = lax.ppermute(near, AXES, [(i, i ^ 1) for i in range(count)])
    half = (HALF, LANES)
    vectors, mine, other, products = call(
        gram_kernel,
        [(8, width), half, half, half],
        [pltpu.VMEM((2 * LANES, width), jnp.bfloat16), pltpu.VMEM((2 * HALF, LANES), F32)],
        held=1,
        inputs=5,
        copies=5,
        flops=2**30,
    )(hist, current, residual, estimate, forcing, stiffness)
    swap = lambda v: lax.ppermute(v, "core", [(i, i ^ 1) for i in range(lax.axis_size("core"))])
    products, state, halo = call(column_kernel, [half, state_shape, edge], flops=2**29)(
        products, hist, vectors, beyond, near
    )
    (copies,) = call(pair_kernel, [(plane, *half)])(mine, swap(other), products)
    (copies,) = call(spread_kernel, [(depth, *half)])(everywhere(copies, ("y", "x")))
    (mine,) = call(total_kernel, [half])(everywhere(copies, "z"))
    sent, state, factor = call(first_kernel, [(count, LANES), state_shape, (112, LANES)])(
        mine, swap(mine), hist, held_w, state, vectors, halo
    )
    sent, state, lines = call(second_kernel, [(count, LANES), state_shape, (8, LANES)])(
        spread_rows(sent), hist, held_w, factor, state, vectors, halo
    )
    current, residual = call(third_kernel, [(1, width), (1, width)])(
        spread_rows(sent), held_w, factor, lines, state
    )
    return current.reshape(width), residual.reshape(width)


def solution(mesh):
    devices = mesh.devices.reshape(4, 8, 2, 4) if mesh.devices.size == 256 else mesh.devices.reshape(2, 2, 2, -1)
    finer = Mesh(devices, AXES)
    whole, columns = P(AXES), P(None, AXES)
    return jax.shard_map(
        shards,
        mesh=finer,
        in_specs=(whole,) * 5 + (columns,) * 2,
        out_specs=(whole, whole),
        check_vma=False,
    )
```

```python
import functools

import jax
import jax.numpy as jnp
from jax import lax
from jax.experimental import pallas as pl
from jax.experimental.pallas import tpu as pltpu
from jax.sharding import Mesh
from jax.sharding import PartitionSpec as P

ITERS = 3
AXES = ("y", "z", "core", "x")
COUPLING = 0.25
LANES = 128
HIST = 100
NEW = HIST
RES = HIST + 1
FOLD = 56
HALF = 32
FREE = 104
SCALARS = FREE + 8
GROUPS = 13

F32 = jnp.float32
VMEM = pl.BlockSpec(memory_space=pltpu.VMEM)


def iota(shape, axis):
    return lax.broadcasted_iota(jnp.int32, shape, axis)


def rows_of(group):
    return slice(8 * group, min(8 * group + 8, HIST))


def row_to_columns(row):
    lane, sub = iota((8, LANES), 1), iota((8, LANES), 0)
    full = jnp.broadcast_to(row, (8, LANES))
    return [
        jnp.sum(jnp.where(lane == sub + 8 * g, full, 0.0), axis=1, keepdims=True)
        for g in range(GROUPS)
    ]


def columns_to_row(columns):
    lane, sub = iota((8, LANES), 1), iota((8, LANES), 0)
    total = jnp.zeros((8, LANES), F32)
    for g, column in enumerate(columns):
        total = total + jnp.where(lane == sub + 8 * g, jnp.broadcast_to(column, (8, LANES)), 0.0)
    return jnp.sum(total, axis=0, keepdims=True)


def solver_map(current, forcing, stiffness, inside):
    width = current.shape[1]
    neighbours = pltpu.roll(current, 1, 1) + pltpu.roll(current, width - 1, 1)
    estimate = forcing + stiffness * jnp.tanh(current) + COUPLING * neighbours
    return jnp.where(inside, estimate, 0.0)


def even_place():
    return lax.rem(lax.axis_index("x"), 2) == 0


def halo_of(near_ref, beyond_ref):
    even = jnp.full((8, LANES), jnp.where(even_place(), 1, 0), jnp.int32) == 1
    near, beyond = near_ref[...], beyond_ref[...]
    right, left = jnp.where(even, near, beyond), jnp.where(even, beyond, near)
    return jnp.concatenate([right, jnp.zeros((LANES - 16, LANES), F32), left], axis=0).T[:104]


def extended(row, halo):
    return jnp.concatenate([row, halo], axis=1)


def inside_mask(width, stiffness_halo):
    ones = jnp.ones((1, width), F32)
    return extended(ones, jnp.where(stiffness_halo != 0.0, 1.0, 0.0)) > 0.5


def copy_all(pairs, sems):
    copies = [pltpu.make_async_copy(src, dst, sems.at[i]) for i, (src, dst) in enumerate(pairs)]
    for copy in copies:
        copy.start()
    return copies


def edge_kernel(
    hist_ref, current_ref, forcing_ref, stiffness_ref, old_est_ref,
    near_ref, beyond_ref, first_ref, last_ref, sems,
):
    width = hist_ref.shape[1]
    pairs = []
    for block_ref, at in ((first_ref, 0), (last_ref, width - LANES)):
        columns = slice(at, at + LANES)
        pairs.append((hist_ref.at[:, columns], block_ref.at[:HIST, :]))
        for i, ref in enumerate((current_ref, forcing_ref, stiffness_ref, old_est_ref)):
            pairs.append((ref.at[:, columns], block_ref.at[HIST + i : HIST + i + 1, :]))
    copies = copy_all(pairs, sems)
    for block_ref in (first_ref, last_ref):
        block_ref[104:, :] = jnp.zeros((LANES - 104, LANES), F32)
    for copy in copies:
        copy.wait()
    even = jnp.full((8, LANES), jnp.where(even_place(), 1, 0), jnp.int32) == 1
    first, last = first_ref[...].T[:8], last_ref[...].T[LANES - 8 :]
    near_ref[...] = jnp.where(even, last, first)
    beyond_ref[...] = jnp.where(even, first, last)


def first_core():
    return jnp.full((HALF, LANES), lax.axis_index("core"), jnp.int32) == 0


def place(g, kind):
    at = 8 * (g % (HALF // 8))
    return slice(at, at + 8), FREE + 4 * kind + g // (HALF // 8)


def gram_kernel(
    hist_ref, current_ref, old_res_ref, old_est_ref, forcing_ref, stiffness_ref,
    vectors_ref, mine_ref, other_ref, products_ref, parts_ref, packed_ref, sems,
):
    width = hist_ref.shape[1]
    vectors = (current_ref, old_res_ref, old_est_ref, forcing_ref, stiffness_ref)
    copies = copy_all([(ref, vectors_ref.at[i : i + 1, :]) for i, ref in enumerate(vectors)], sems)

    def put(row, values):
        high = values.astype(jnp.bfloat16)
        parts_ref[row : row + values.shape[0], :] = high
        parts_ref[LANES + row : LANES + row + values.shape[0], :] = (
            values - high.astype(F32)
        ).astype(jnp.bfloat16)

    put(112, jnp.zeros((16, width), F32))
    for start in range(0, 96, 16):
        put(start, hist_ref[start : start + 16, :])
    put(96, jnp.concatenate([hist_ref[96:100, :], jnp.zeros((12, width), F32)], axis=0))
    products = lax.dot_general(
        parts_ref[...],
        parts_ref[...],
        (((1,), (1,)), ((), ())),
        preferred_element_type=F32,
    )
    cross = products[:104, LANES:] + products[LANES : LANES + 104, :LANES]
    gram = products[:104, :LANES] + (cross + products[LANES : LANES + 104, LANES:])
    lane, sub = iota((8, LANES), 1), iota((8, LANES), 0)
    packed_ref[:8, :] = gram[:8]
    for g in range(1, FOLD // 8):
        corner = pltpu.roll(gram[FOLD + 8 * g - 8 : FOLD + 8 * g], LANES - FOLD, 1)
        packed_ref[8 * g : 8 * g + 8, :] = jnp.where(
            lane <= sub + 8 * (g - 1), corner, gram[8 * g : 8 * g + 8]
        )
    packed_ref[FOLD:, :] = jnp.zeros((2 * HALF - FOLD, LANES), F32)
    low, high = packed_ref[:HALF, :], packed_ref[HALF:, :]
    is_low = first_core()
    mine_ref[...] = jnp.where(is_low, low, high)
    other_ref[...] = jnp.where(is_low, high, low)

    for copy in copies:
        copy.wait()
    nothing = jnp.zeros((1, LANES), F32)
    wide = [extended(vectors_ref[i : i + 1, :], nothing) for i in (0, 3, 4)]
    residual = (solver_map(*wide, iota((1, width + LANES), 1) < width) - wide[0])[:, :width]
    column = residual - vectors_ref[1:2, :]
    blocks = [jnp.zeros((8, LANES), F32) for _ in range(HALF // 8)]
    for kind, parts in enumerate(history_products(hist_ref, (column, residual), width)):
        for g, part in enumerate(parts):
            at = g % (HALF // 8)
            blocks[at] = jnp.where(lane == place(g, kind)[1], part, blocks[at])
    for at, block in enumerate(blocks):
        products_ref[8 * at : 8 * at + 8, :] = block


def column_kernel(
    products_ref, hist_ref, vectors_ref, beyond_ref, near_ref, out_ref, state_ref, halo_ref
):
    width = hist_ref.shape[1]
    halo = halo_of(near_ref, beyond_ref)
    halo_ref[...] = halo
    current = extended(vectors_ref[0:1, :], halo[100:101])
    estimate = solver_map(
        current,
        extended(vectors_ref[3:4, :], halo[101:102]),
        extended(vectors_ref[4:5, :], halo[102:103]),
        inside_mask(width, halo[102:103]),
    )
    residual = estimate - current
    column = residual[:, :width] - vectors_ref[1:2, :]
    state_ref[0:1, :] = estimate
    state_ref[1:2, :] = residual
    state_ref[2:3, :width] = column
    residual = residual[:, :width]
    before = COUPLING * coefficient_of(halo[100:101], LANES - 1)
    after = COUPLING * coefficient_of(halo[100:101], 0)
    lane, sub = iota((8, LANES), 1), iota((8, LANES), 0)
    blocks = [products_ref[8 * at : 8 * at + 8, :] for at in range(HALF // 8)]
    for g in range(GROUPS):
        rows = rows_of(g)
        edge = before * hist_ref[rows, :LANES][:, :1] + after * hist_ref[rows, width - LANES :][:, LANES - 1 :]
        if edge.shape[0] < 8:
            edge = jnp.concatenate([edge, jnp.zeros((8 - edge.shape[0], 1), F32)], axis=0)
        at = g % (HALF // 8)
        mask = (lane == place(g, 0)[1]) | (lane == place(g, 1)[1])
        blocks[at] = blocks[at] + jnp.where(mask, edge, 0.0)
    square, mixed = dot_rows(column, column), dot_rows(column, residual)
    blocks[0] = jnp.where(lane == SCALARS, jnp.where(sub == 0, square, jnp.where(sub == 1, mixed, 0.0)), blocks[0])
    for at, block in enumerate(blocks):
        out_ref[8 * at : 8 * at + 8, :] = block


def pair_kernel(mine_ref, other_ref, products_ref, out_ref):
    filled = jnp.where(iota((HALF, LANES), 1) >= FREE, products_ref[...], mine_ref[...] + other_ref[...])
    out_ref[...] = jnp.broadcast_to(filled[None], out_ref.shape)


def total_kernel(got_ref, out_ref):
    out_ref[...] = jnp.sum(got_ref[...], axis=0)


def spread_kernel(got_ref, out_ref):
    total = jnp.sum(got_ref[...], axis=0)
    out_ref[...] = jnp.broadcast_to(total[None], out_ref.shape)


def unfold(packed):
    lane, sub = iota((FOLD, LANES), 1), iota((FOLD, LANES), 0)
    square = jnp.concatenate([packed, jnp.zeros((LANES - FOLD, LANES), F32)], axis=0)
    turned = square.T
    top = jnp.where(lane >= sub, packed, turned[:FOLD, :])
    lower = packed[8:FOLD, :]
    upper = pltpu.roll(turned[: FOLD - 8, :], LANES - 8, 1)
    lane2, sub2 = iota((FOLD - 8, LANES), 1), iota((FOLD - 8, LANES), 0)
    corner = pltpu.roll(jnp.where(lane2 <= sub2, lower, upper), FOLD, 1)
    bottom = jnp.where(lane2 < FOLD, turned[FOLD:104, :], corner)
    return [top[8 * g : 8 * g + 8] for g in range(FOLD // 8)] + [
        bottom[8 * g : 8 * g + 8] for g in range(GROUPS - FOLD // 8)
    ]


def with_products(groups, sums):
    lane, sub = iota((8, LANES), 1), iota((8, LANES), 0)
    lane1 = iota((1, LANES), 1)
    groups = list(groups)
    columns = [[], []]
    for g in range(GROUPS):
        for kind in range(2):
            rows, at = place(g, kind)
            columns[kind].append(sums[rows, at : at + 1])
            groups[g] = jnp.where(lane == NEW + kind, columns[kind][g], groups[g])
    square, mixed = sums[0:1, SCALARS : SCALARS + 1], sums[1:2, SCALARS : SCALARS + 1]
    by_column = jnp.where(lane1 == NEW, square, jnp.where(lane1 == RES, mixed, columns_to_row(columns[0])))
    by_residual = jnp.where(lane1 == NEW, mixed, columns_to_row(columns[1]))
    at = NEW - 8 * (GROUPS - 1)
    groups[-1] = jnp.where(sub == at, by_column, jnp.where(sub == at + 1, by_residual, groups[-1]))
    return groups


def eliminate(groups):
    lane, sub = iota((8, LANES), 1), iota((8, LANES), 0)
    whole = lambda v: jnp.broadcast_to(v, (8, LANES))
    groups = list(groups)
    pivots = [jnp.ones((8, LANES), F32) for _ in range(GROUPS)]
    for g in range(GROUPS):
        first, count = 8 * g, min(8, RES - 8 * g)
        inside = (lane >= first) & (lane < first + count)
        columns = [[whole(group[:, first + j : first + j + 1]) for j in range(count)] for group in groups[g:]]
        left = [[whole(columns[0][j][i : i + 1, :]) for j in range(i + 1)] for i in range(count)]
        low = [[None] * count for _ in range(count)]
        inverse, rows = [], []
        for j in range(count):
            for i in range(j, count):
                for m in range(j):
                    left[i][j] = left[i][j] - low[i][m] * left[j][m]
            inverse.append(1.0 / left[j][j])
            for i in range(j + 1, count):
                low[i][j] = left[i][j] * inverse[j]
        for j in range(count):
            row = jnp.where(inside, jnp.where(lane == first + j, 1.0, 0.0), whole(groups[g][j : j + 1, :]))
            for m in range(j):
                row = row - low[j][m] * rows[m]
            rows.append(row)
            pivots[g] = jnp.where(sub == j, left[j][j], pivots[g])
        for h in range(g, GROUPS):
            if h == g and count == 8:
                continue
            new = jnp.where(inside, 0.0, groups[h])
            factors = []
            for j in range(count):
                factor = columns[h - g][j]
                for m in range(j):
                    factor = factor - factors[m] * left[j][m]
                factors.append(factor * inverse[j])
                new = new - factors[j] * rows[j]
            groups[h] = new
        for j in range(count):
            groups[g] = jnp.where(sub == j, rows[j], groups[g])
    return groups, pivots


def update(current, coefficients, hist_ref, halo, width):
    wide = [jnp.broadcast_to(c, (8, LANES)) for c in coefficients]
    pieces = []
    for start in range(0, width + LANES, LANES):
        total = jnp.zeros((8, LANES), F32)
        for g in range(GROUPS - 1):
            if start < width:
                part = hist_ref[8 * g : 8 * g + 8, start : start + LANES]
            else:
                part = halo[8 * g : 8 * g + 8, :]
            total = total + wide[g] * part
        if start < width:
            last = hist_ref[96:100, start : start + LANES]
        else:
            last = halo[96:100, :]
        pieces.append(
            jnp.sum(total, axis=0, keepdims=True)
            + jnp.sum(wide[GROUPS - 1][:4] * last, axis=0, keepdims=True)
        )
    return current + jnp.concatenate(pieces, axis=1)


def history_products(hist_ref, columns, width):
    totals = [[jnp.zeros((8, LANES), F32) for _ in range(GROUPS - 1)] for _ in columns]
    last = [jnp.zeros((4, LANES), F32) for _ in columns]
    for start in range(0, width, LANES):
        wide = [jnp.broadcast_to(c[:, start : start + LANES], (8, LANES)) for c in columns]
        for g in range(GROUPS - 1):
            part = hist_ref[8 * g : 8 * g + 8, start : start + LANES]
            for total, row in zip(totals, wide):
                total[g] = total[g] + part * row
        part = hist_ref[96:100, start : start + LANES]
        last = [total + part * row[:4] for total, row in zip(last, wide)]
    for total, end in zip(totals, last):
        total.append(jnp.concatenate([end, jnp.zeros((4, LANES), F32)], axis=0))
    return [[jnp.sum(t, axis=1, keepdims=True) for t in total] for total in totals]


def dot_rows(a, b):
    return jnp.sum(a * b, axis=1, keepdims=True)


def coefficient_of(row, at):
    return jnp.sum(jnp.where(iota((1, LANES), 1) == at, row, 0.0), axis=1, keepdims=True)


def send_row(out_ref, hist_ref, columns, column, residual, width):
    row = columns_to_row(history_products(hist_ref, (column,), width)[0])
    lane = iota((1, LANES), 1)
    for at, other in enumerate((*columns, column, residual)):
        row = jnp.where(lane == HIST + at, dot_rows(other, column), row)
    out_ref[...] = jnp.broadcast_to(row, out_ref.shape)


def first_kernel(
    mine_ref, other_ref, hist_ref, hist_w_ref, state_ref, vectors_ref, halo_ref,
    row_ref, next_ref, factor_ref,
):
    width = hist_ref.shape[1]
    mine, other = mine_ref[...], other_ref[...]
    is_low = first_core()
    low, high = jnp.where(is_low, mine, other), jnp.where(is_low, other, mine)
    packed = jnp.concatenate([low, high[: FOLD - HALF]], axis=0)
    whole = unfold(jnp.where(iota((FOLD, LANES), 1) < FREE, packed, 0.0))
    whole = with_products(whole, mine + other)
    products = whole[RES // 8][RES % 8 : RES % 8 + 1, :]
    groups, pivots = eliminate(whole)
    coeffs = groups[RES // 8][RES % 8 : RES % 8 + 1, :]
    lane1 = iota((1, LANES), 1)
    coeffs = jnp.where(lane1 < RES, coeffs, 0.0)
    lane, sub = iota((8, LANES), 1), iota((8, LANES), 0)
    for g, group in enumerate(groups):
        row = sub + 8 * g
        scale = lax.rsqrt(pivots[g])
        unit = jnp.where(lane < row, group, jnp.where(lane == row, 1.0, 0.0))
        factor_ref[8 * g : 8 * g + 8, :] = jnp.where(row < RES, unit * scale, 0.0)
    factor_ref[104:112, :] = jnp.broadcast_to(jnp.where(lane1 < RES, products, 0.0), (8, LANES))

    halo = halo_ref[...]
    forcing = extended(vectors_ref[3:4, :], halo[101:102])
    stiffness = extended(vectors_ref[4:5, :], halo[102:103])
    inside = inside_mask(width, halo[102:103])
    estimate = state_ref[0:1, :]
    residual = state_ref[1:2, :]
    moved = estimate - extended(vectors_ref[2:3, :], halo[103:104])
    column = state_ref[2:3, :width]
    current = update(estimate, row_to_columns(coeffs), hist_w_ref, halo, width)
    current = current + coefficient_of(coeffs, NEW) * moved
    estimate2 = solver_map(current, forcing, stiffness, inside)
    residual2 = estimate2 - current
    column2 = residual2[:, :width] - residual[:, :width]
    next_ref[0:1, :] = estimate2
    next_ref[1:2, :] = residual2
    next_ref[2:3, :width] = column
    next_ref[3:4, :width] = column2
    next_ref[4:5, :] = moved
    next_ref[5:6, :] = estimate2 - estimate
    send_row(row_ref, hist_ref, (column,), column2, residual2[:, :width], width)


def bordered(factor_ref, products, sent, count, extra):
    lane = iota((1, LANES), 1)
    cross = jnp.where(lane < count, sent, 0.0)
    square = coefficient_of(sent, count)
    with_residual = coefficient_of(sent, count + 1)
    products = jnp.where(lane == count, with_residual, jnp.where(lane < count, products + cross, 0.0))

    def solve(row):
        total = jnp.zeros((8, LANES), F32)
        norm = jnp.zeros((8, 1), F32)
        for g in range(GROUPS):
            block = factor_ref[8 * g : 8 * g + 8, :]
            y = jnp.sum(block * row, axis=1, keepdims=True)
            total = total + y * block
            norm = norm + y * y
        out, length = jnp.sum(total, axis=0, keepdims=True), jnp.sum(norm, axis=0, keepdims=True)
        for line in extra:
            y = dot_rows(line, row)
            out, length = out + y * line, length + y * y
        return out, length

    applied, length = solve(cross)
    scale = lax.rsqrt(square - length)
    line = jnp.where(lane == count, 1.0, -applied) * scale
    coeffs, _ = solve(products)
    coeffs = -(coeffs + dot_rows(line, products) * line)
    return coeffs, line, products


def second_kernel(
    got_ref, hist_ref, hist_w_ref, factor_ref, state_ref, vectors_ref, halo_ref,
    row_ref, next_ref, lines_ref,
):
    width = hist_ref.shape[1]
    sent = jnp.sum(got_ref[...], axis=0, keepdims=True)
    coeffs, line, products = bordered(factor_ref, factor_ref[104:105, :], sent, RES, ())
    lines_ref[0:1, :] = line
    lines_ref[1:2, :] = products
    halo = halo_ref[...]
    forcing = extended(vectors_ref[3:4, :], halo[101:102])
    stiffness = extended(vectors_ref[4:5, :], halo[102:103])
    inside = inside_mask(width, halo[102:103])
    estimate = state_ref[0:1, :]
    residual = state_ref[1:2, :]
    moved, moved2 = state_ref[4:5, :], state_ref[5:6, :]
    column, column2 = state_ref[2:3, :width], state_ref[3:4, :width]
    current = update(estimate, row_to_columns(coeffs), hist_w_ref, halo, width)
    current = current + coefficient_of(coeffs, NEW) * moved + coefficient_of(coeffs, NEW + 1) * moved2
    estimate3 = solver_map(current, forcing, stiffness, inside)
    residual3 = estimate3 - current
    column3 = residual3[:, :width] - residual[:, :width]
    next_ref[0:1, :] = estimate3
    next_ref[1:2, :] = residual3
    next_ref[4:5, :] = moved
    next_ref[5:6, :] = moved2
    next_ref[6:7, :] = estimate3 - estimate
    send_row(row_ref, hist_ref, (column, column2), column3, residual3[:, :width], width)


def third_kernel(
    got_ref, hist_w_ref, factor_ref, lines_ref, state_ref, current_ref, residual_ref,
):
    width = hist_w_ref.shape[1]
    sent = jnp.sum(got_ref[...], axis=0, keepdims=True)
    coeffs, _, _ = bordered(factor_ref, lines_ref[1:2, :], sent, RES + 1, (lines_ref[0:1, :],))
    estimate = state_ref[0:1, :]
    halo = jnp.zeros((104, LANES), F32)
    current = update(estimate, row_to_columns(coeffs), hist_w_ref, halo, width)
    for at in range(ITERS):
        current = current + coefficient_of(coeffs, NEW + at) * state_ref[4 + at : 5 + at, :]
    current_ref[...] = current[:, :width]
    residual_ref[...] = state_ref[1:2, :width]


def call(kernel, outs, scratch=(), held=0, inputs=0, copies=0, flops=0):
    extra = {}
    if inputs:
        extra["in_specs"] = [VMEM] * held + [pl.BlockSpec(memory_space=pltpu.HBM)] * inputs
    return pl.pallas_call(
        kernel,
        out_shape=[jax.ShapeDtypeStruct(s, F32) for s in outs],
        out_specs=[VMEM] * len(outs),
        scratch_shapes=[*scratch, *([pltpu.SemaphoreType.DMA((copies,))] if copies else [])],
        cost_estimate=pl.CostEstimate(flops=flops, bytes_accessed=2**22, transcendentals=0) if flops else None,
        compiler_params=pltpu.CompilerParams(vmem_limit_bytes=12 * 2**20),
        **extra,
    )


def in_hbm(value):
    return pltpu.with_memory_space_constraint(value, pltpu.HBM)


def everywhere(blocks, axes):
    return lax.all_to_all(blocks, axes, 0, 0)


def spread_rows(rows):
    count = rows.shape[0]
    return everywhere(rows.reshape(count, 1, LANES), AXES).reshape(count, LANES)


def shards(interface, previous_residual, previous_estimate, forcing, stiffness, hist_v, hist_w):
    width = interface.shape[0]
    count = lax.axis_size(AXES)
    plane, depth = lax.axis_size(("y", "x")), lax.axis_size("z")
    row = lambda v: in_hbm(v.reshape(1, width))
    hist = pltpu.with_memory_space_constraint(hist_v, pltpu.VMEM)
    held_w = pltpu.with_memory_space_constraint(hist_w, pltpu.VMEM)
    current, residual, estimate = row(interface), row(previous_residual), row(previous_estimate)
    forcing, stiffness = row(forcing), row(stiffness)
    edge, state_shape = (104, LANES), (8, width + LANES)

    turned, block = (8, LANES), pltpu.VMEM((LANES, LANES), F32)
    near, beyond = call(edge_kernel, [turned, turned], [block, block], inputs=5, copies=10)(
        in_hbm(hist_w), current, forcing, stiffness, estimate
    )
    steps = [(i, i + 1) for i in range(1, count - 1, 2)]
    beyond = lax.ppermute(beyond, AXES, steps + [(j, i) for i, j in steps])
    near = lax.ppermute(near, AXES, [(i, i ^ 1) for i in range(count)])
    half = (HALF, LANES)
    vectors, mine, other, products = call(
        gram_kernel,
        [(8, width), half, half, half],
        [pltpu.VMEM((2 * LANES, width), jnp.bfloat16), pltpu.VMEM((2 * HALF, LANES), F32)],
        held=1,
        inputs=5,
        copies=5,
        flops=2**30,
    )(hist, current, residual, estimate, forcing, stiffness)
    swap = lambda v: lax.ppermute(v, "core", [(i, i ^ 1) for i in range(lax.axis_size("core"))])
    products, state, halo = call(column_kernel, [half, state_shape, edge], flops=2**29)(
        products, hist, vectors, beyond, near
    )
    (copies,) = call(pair_kernel, [(plane, *half)])(mine, swap(other), products)
    (copies,) = call(spread_kernel, [(depth, *half)])(everywhere(copies, ("y", "x")))
    (mine,) = call(total_kernel, [half])(everywhere(copies, "z"))
    sent, state, factor = call(first_kernel, [(count, LANES), state_shape, (112, LANES)])(
        mine, swap(mine), hist, held_w, state, vectors, halo
    )
    sent, state, lines = call(second_kernel, [(count, LANES), state_shape, (8, LANES)])(
        spread_rows(sent), hist, held_w, factor, state, vectors, halo
    )
    current, residual = call(third_kernel, [(1, width), (1, width)])(
        spread_rows(sent), held_w, factor, lines, state
    )
    return current.reshape(width), residual.reshape(width)


def solution(mesh):
    devices = mesh.devices.reshape(4, 8, 2, 4) if mesh.devices.size == 256 else mesh.devices.reshape(2, 2, 2, -1)
    finer = Mesh(devices, AXES)
    whole, columns = P(AXES), P(None, AXES)
    return jax.shard_map(
        shards,
        mesh=finer,
        in_specs=(whole,) * 5 + (columns,) * 2,
        out_specs=(whole, whole),
        check_vma=False,
    )
```
